32 devices in a mesh: expert: 8 (over z, y), tensor: 4 (over x, core).
Axes of the slice: x: 2, y: 2, z: 4, core: 2. Of those that a mesh axis runs over, the one named last changes fastest.
Arguments:
- block_in: float32 [12608, 512], P(('expert', 'tensor')), may hold values from -6 to 6
- out_grad: float32 [12608, 512], P(('expert', 'tensor')), may hold values from -6 to 6
- routes: int32 [12608, 2], P('expert'), may hold values from 0 to 7, all different within a row; in each aligned block of 1576 rows (0 to 1575, 1576 to 3151, ...) at most 493 rows name the same one
- kept_pairs: int32 [12608, 2], P('expert'), may hold values 0 or 1
- ln1_gain: float32 [512], replicated, may hold values from 0.5 to 1.5
- ln1_bias: float32 [512], replicated, may hold values from -1.5 to 1.5
- w_query: float32 [512, 512], P(None, 'tensor'), may hold values from -0.375 to 0.375
- w_key: float32 [512, 512], P(None, 'tensor'), may hold values from -0.375 to 0.375
- w_value: float32 [512, 512], P(None, 'tensor'), may hold values from -0.25 to 0.25
- w_attn_out: float32 [512, 512], P('tensor'), may hold values from -1 to 1
- ln2_gain: float32 [512], replicated, may hold values from 0.5 to 1.5
- ln2_bias: float32 [512], replicated, may hold values from -1.5 to 1.5
- w_router: float32 [512, 8], replicated, may hold values from -0.1875 to 0.1875
- w_expert_in: float32 [8, 512, 2048], P('expert', None, 'tensor'), may hold values from -0.25 to 0.25
- w_expert_out: float32 [8, 2048, 512], P('expert', 'tensor'), may hold values from -0.5 to 0.5
Outputs:
- block_out: float32 [12608, 512], P(('expert', 'tensor'))
- input_grad: float32 [12608, 512], P(('expert', 'tensor'))
- grad_ln1_gain: float32 [512], replicated
- grad_ln1_bias: float32 [512], replicated
- grad_query: float32 [512, 512], P(None, 'tensor')
- grad_key: float32 [512, 512], P(None, 'tensor')
- grad_value: float32 [512, 512], P(None, 'tensor')
- grad_attn_out: float32 [512, 512], P('tensor')
- grad_ln2_gain: float32 [512], replicated
- grad_ln2_bias: float32 [512], replicated
- grad_router: float32 [512, 8], replicated
- grad_expert_in: float32 [8, 512, 2048], P('expert', None, 'tensor')
- grad_expert_out: float32 [8, 2048, 512], P('expert', 'tensor')
- head_maxima: float32 [8], P('tensor')
- clipped_query: float32 [512, 512], P(None, 'tensor')
- clipped_key: float32 [512, 512], P(None, 'tensor')
The draws below stay inside these ranges and needn't reach their ends.
Inputs may be any that keep to these rules, and one draw needn't show every extreme that they name: `routes`: A token's two experts differ. In every aligned block of 1576 tokens (one index of the expert axis) each expert is named by at most 493 pairs, and in some block some expert is named by exactly 493 pairs.
All inputs are finite; a program needn't handle non-finite values. No bound on the sum of `kept_pairs` on one device may be relied on, other than what follows from the above.
Results may differ from the reference program's by a relative error of at most 0.02.
The reference program's roundings to bfloat16 on the way count: a program that leaves them out, or rounds other values in their place, can miss the bound.
Values may be sent and summed in bfloat16 or wider, within the bound.
No kernel may reach another device: no remote copies, remote signals or barrier semaphores. Data moves between devices by JAX's collectives and lax.ppermute only.
A program may use at most 256 MiB of HBM per device.

```python
import math
import jax
import jax.numpy as jnp
import numpy as np
from jax import lax

D = 512
HEADS = 8
HEAD_DIM = 64
FF = 2048
IMAGE_TOKENS = 197
IMG_DEV = 2
TOK_GROUP = 1576
TOKENS = 12608
EXPERTS = 8
CAP = 493
N_EXPERT = 8


def touch_ends(values, rng, low, largest):
    place = [jax.random.randint(jax.random.fold_in(rng, axis), (), 0, length) for axis, length in enumerate(values.shape)]
    longest = values.shape.index(max(values.shape))
    neighbour = place[:longest] + [(place[longest] + 1) % values.shape[longest]] + place[longest + 1:]
    return values.at[tuple(place)].set(low).at[tuple(neighbour)].set(largest)


def block_scale(stream_key, shape, shards, low, high):
    loudness = 1.0
    for axis_at, parts in shards:
        draws = jax.random.uniform(jax.random.fold_in(jax.random.fold_in(stream_key, 6), axis_at), (parts,), jnp.float32, low / len(shards), high / len(shards))
        loudness = loudness * jnp.repeat(jnp.exp(draws), shape[axis_at] // parts).reshape((-1,) + (1,) * (len(shape) - 1 - axis_at))
    return loudness


def routed_block(stream_key, own, number, rows, amount, top, bound, slope):
    order = jax.random.permutation(stream_key, amount)
    heavy_load, common = shares(amount, rows * top, bound, slope, True), shares(amount, rows * top, bound, slope, False)
    places = jnp.arange(amount)

    def named(lengths, rotation):
        used = int((lengths > 0).sum())
        fixed = max(1, used // 4)
        moved = fixed + (places - fixed + rotation * (used - fixed)) % max(1, amount - fixed)
        return jnp.zeros((amount,), jnp.int32).at[order[jnp.where(places < fixed, places, moved)]].set(jnp.asarray(lengths, jnp.int32))

    lengths = jnp.where(number % 4 == 0, named(heavy_load, number // 4), named(common, number - number // 4 - 1))
    mixed = jax.random.permutation(jax.random.fold_in(own, 3), amount)
    donor, sink = mixed[0:amount // 2 * 2:2], mixed[1:amount // 2 * 2:2]
    margin = jnp.minimum(lengths[donor] - 1, bound - lengths[sink]) // 2
    margin = jnp.where((donor == order[0]) | (sink == order[0]) | (lengths[sink] == 0), 0, jnp.maximum(margin, 0))
    moved = jax.random.randint(jax.random.fold_in(own, 4), (amount // 2,), 0, 1 << 20) % (margin + 1)
    lengths = lengths.at[donor].add(-moved).at[sink].add(moved)
    members = jnp.searchsorted(jnp.cumsum(lengths), jnp.arange(rows * top), side="right").astype(jnp.int32)
    table = members.reshape(top, rows).T
    table = table[jax.random.permutation(jax.random.fold_in(own, 1), rows)]
    rotation = jax.random.randint(jax.random.fold_in(own, 2), (rows, 1), 0, top)
    return jnp.take_along_axis(table, (jnp.arange(top)[None, :] + rotation) % top, axis=1)


def shares(count, total, reach, skew, full):
    loads = [(1 << 20) // math.isqrt(rank ** skew) + 1 for rank in range(1, count + 1)]
    largest = reach if full else min(reach, max(-(-total // count), total * loads[0] // sum(loads)))
    least = 1 if total - largest >= count - 1 else 0
    counts, spare = [largest] + [least] * (count - 1), total - largest - least * (count - 1)
    while spare > 0:
        movable = [i for i in range(1, count) if counts[i] < largest] or [i for i in range(1, count) if counts[i] < reach]
        mass, budget = sum([loads[i] for i in movable]), spare
        for i in movable:
            extra = min(reach - counts[i], max(1, budget * loads[i] // mass), spare)
            counts[i] = counts[i] + extra
            spare = spare - extra
    return np.array(counts)


def noise(stream_key, shape, scale, most, split=(), kind=jnp.bfloat16):
    array = scale * jax.random.normal(stream_key, shape, jnp.float32)
    if split:
        array = array * block_scale(stream_key, shape, split, -0.22, 0.18)
    return jnp.clip(array, -most, most).astype(kind)


def setup_inputs(seed: int = 0) -> dict:
    seeds = jax.random.split(jax.random.key(seed), 16)
    block_in = noise(seeds[0], (TOKENS, D), 1.0, 6.0, ((0, 32),), jnp.float32)
    out_grad = noise(seeds[1], (TOKENS, D), 1.0, 6.0, ((0, 32),), jnp.float32)
    routes_keys = jax.random.split(jax.random.fold_in(seeds[2], 1), TOKENS // TOK_GROUP)
    routes_turns = jax.random.permutation(jax.random.fold_in(seeds[2], 3), TOKENS // TOK_GROUP)
    routes = jax.vmap(lambda own, number: routed_block(jax.random.fold_in(seeds[2], 2), own, number, TOK_GROUP, EXPERTS, 2, CAP, 1))(routes_keys, routes_turns).reshape((TOKENS, 2))
    kept_pairs = touch_ends((jax.random.randint(seeds[3], (TOKENS, 2), 0, 8) < 7).astype(jnp.int32), jax.random.fold_in(seeds[3], 1), 0, 1)
    ln1_gain = jnp.clip(1.0 + 0.1 * jax.random.normal(seeds[4], (D,), jnp.float32), 0.5, 1.5)
    ln1_bias = noise(seeds[5], (D,), 0.3, 1.5, (), jnp.float32)
    w_query = noise(seeds[6], (D, D), (D // 2) ** -0.5, 0.375, ((1, 4),), jnp.float32)
    w_key = noise(seeds[7], (D, D), (D // 2) ** -0.5, 0.375, ((1, 4),), jnp.float32)
    w_value = noise(seeds[8], (D, D), D ** -0.5, 0.25, ((1, 4),), jnp.float32)
    w_attn_out = noise(seeds[9], (D, D), (D // 16) ** -0.5, 1.0, ((0, 4),), jnp.float32)
    ln2_gain = jnp.clip(1.0 + 0.1 * jax.random.normal(seeds[10], (D,), jnp.float32), 0.5, 1.5)
    ln2_bias = noise(seeds[11], (D,), 0.3, 1.5, (), jnp.float32)
    w_router = noise(seeds[12], (D, EXPERTS), (2 * D) ** -0.5, 0.1875, (), jnp.float32)
    w_expert_in = noise(seeds[13], (EXPERTS, D, FF), D ** -0.5, 0.25, ((0, 8), (2, 4)), jnp.float32)
    w_expert_out = noise(seeds[14], (EXPERTS, FF, D), (max(1, FF * 4 // (EXPERTS * EXPERTS))) ** -0.5, 0.5, ((0, 8), (1, 4)), jnp.float32)
    return dict(block_in=block_in, out_grad=out_grad, routes=routes, kept_pairs=kept_pairs, ln1_gain=ln1_gain, ln1_bias=ln1_bias, w_query=w_query, w_key=w_key, w_value=w_value, w_attn_out=w_attn_out, ln2_gain=ln2_gain, ln2_bias=ln2_bias, w_router=w_router, w_expert_in=w_expert_in, w_expert_out=w_expert_out)


clip_limit = 4.0
norm_eps = 1e-06

@jax.custom_vjp
def low(v):
    return lax.optimization_barrier(v.astype(jnp.bfloat16)).astype(jnp.float32)

@jax.custom_vjp
def low_back(v):
    return v

def low_keep(v):
    return (low(v), None)

def low_pass(kept, grad):
    return (grad,)

def back_keep(v):
    return (v, None)

def back_low(kept, grad):
    return (low(grad),)
low.defvjp(low_keep, low_pass)
low_back.defvjp(back_keep, back_low)

def matmul(left, right):
    return jnp.dot(left, right, precision=lax.Precision.HIGHEST, preferred_element_type=jnp.float32)

def layer_norm(rows, gain, shift):
    center = lax.optimization_barrier(jnp.mean(rows, axis=-1, keepdims=True))
    offset = rows - center
    spread = lax.optimization_barrier(jnp.mean(offset * offset, axis=-1, keepdims=True))
    return offset * lax.rsqrt(spread + norm_eps) * gain + shift

def slot_table(routes):
    grouped = routes.reshape(N_EXPERT, 2 * TOK_GROUP).astype(jnp.int32)
    onehot = (grouped[:, :, None] == jnp.arange(EXPERTS, dtype=jnp.int32)[None, None, :]).astype(jnp.int32)
    before = (jnp.cumsum(onehot, axis=1) - onehot).astype(jnp.int32)
    position = lax.optimization_barrier(jnp.sum(before * onehot, axis=2)).astype(jnp.int32)
    return (grouped * CAP + position).astype(jnp.int32)

def attend(block):
    query, keys, values = block
    scores = jnp.einsum('bqhd,bkhd->bhqk', query, keys, precision=lax.Precision.HIGHEST) * HEAD_DIM ** (-0.5)
    scores = low_back(scores)
    tops = lax.optimization_barrier(jnp.max(scores, axis=(0, 2, 3)))
    probs = jax.nn.softmax(scores, axis=-1)
    context = jnp.einsum('bhqk,bkhd->bqhd', low(probs), values, precision=lax.Precision.HIGHEST)
    return (context, tops)

def expert_apply(block):
    rows, w_first, w_second = block
    hidden = low_back(matmul(rows, low(w_first)))
    active = low(jax.nn.gelu(hidden))
    return low_back(matmul(active, low(w_second)))

def forward(block_in, ln1_gain, ln1_bias, w_query, w_key, w_value, w_attn_out, ln2_gain, ln2_bias, w_router, w_expert_in, w_expert_out, routes, kept_pairs):
    normed = low(layer_norm(block_in, ln1_gain, ln1_bias))
    query = low(low_back(matmul(normed, low(w_query))))
    keys = low(low_back(matmul(normed, low(w_key))))
    values = low(low_back(matmul(normed, low(w_value))))
    blocks = TOKENS // (IMG_DEV * IMAGE_TOKENS)
    shape = (blocks, IMG_DEV, IMAGE_TOKENS, HEADS, HEAD_DIM)
    context, tops = lax.map(jax.checkpoint(attend), (query.reshape(shape), keys.reshape(shape), values.reshape(shape)))
    context = low(low_back(context.reshape(TOKENS, D)))
    attn = low_back(matmul(context, low(w_attn_out)))
    resid = block_in + attn
    second = layer_norm(resid, ln2_gain, ln2_bias)
    probs = jax.nn.softmax(matmul(second, w_router), axis=-1)
    gates = jnp.take_along_axis(probs, routes, axis=1) * kept_pairs.astype(jnp.float32)
    slots = slot_table(routes)
    group_ids = jnp.arange(N_EXPERT, dtype=jnp.int32)[:, None]
    token_ids = (group_ids * TOK_GROUP + jnp.arange(2 * TOK_GROUP, dtype=jnp.int32)[None, :] // 2).astype(jnp.int32)
    table = jnp.full((N_EXPERT, EXPERTS * CAP), TOKENS, jnp.int32).at[group_ids, slots].set(token_ids)
    table = table.reshape(N_EXPERT, EXPERTS, CAP).transpose(1, 0, 2).reshape(EXPERTS, N_EXPERT * CAP)
    padded = jnp.concatenate([low(second), jnp.zeros((1, D), jnp.float32)], axis=0)
    rows = padded[table]
    outputs = lax.map(jax.checkpoint(expert_apply), (rows, w_expert_in, w_expert_out))
    outputs = outputs.reshape(EXPERTS, N_EXPERT, CAP, D).transpose(1, 0, 2, 3).reshape(N_EXPERT, EXPERTS * CAP, D)
    pair_out = outputs[group_ids, slots].reshape(TOKENS, 2, D)
    mixed = lax.optimization_barrier(jnp.sum(gates[:, :, None] * pair_out, axis=1))
    return (resid + mixed, lax.optimization_barrier(jnp.max(tops, axis=0)))

def reference(block_in, out_grad, routes, kept_pairs, ln1_gain, ln1_bias, w_query, w_key, w_value, w_attn_out, ln2_gain, ln2_bias, w_router, w_expert_in, w_expert_out):

    def wrapped(*params):
        return forward(*params, routes, kept_pairs)
    block_out, pull, head_maxima = jax.vjp(wrapped, block_in, ln1_gain, ln1_bias, w_query, w_key, w_value, w_attn_out, ln2_gain, ln2_bias, w_router, w_expert_in, w_expert_out, has_aux=True)
    grads = pull(out_grad)
    factor = jnp.repeat(jnp.sqrt(jnp.minimum(1.0, clip_limit / head_maxima)), HEAD_DIM)
    clipped_query = w_query * factor[None, :]
    clipped_key = w_key * factor[None, :]
    return (block_out, grads[0], grads[1], grads[2], grads[3], grads[4], grads[5], grads[6], grads[7], grads[8], grads[9], grads[10], grads[11], head_maxima, clipped_query, clipped_key)
```

```python
import functools

import jax
import jax.numpy as jnp
from jax import lax
from jax.experimental import pallas as pl
from jax.experimental.pallas import tpu as pltpu
from jax.sharding import PartitionSpec as P

HEAD_DIM = 64
IMAGE_TOKENS = 197
SPARE = 200
TOP_ROW = 197

F32 = jnp.float32
BF16 = jnp.bfloat16
I32 = jnp.int32

clip_limit = 4.0
norm_eps = 1e-06
low_value = -1e30


def round_up(value, unit):
    return -(-value // unit) * unit


def dot_nn(a, b):
    return lax.dot_general(a, b, (((1,), (0,)), ((), ())), preferred_element_type=F32)


def dot_nt(a, b):
    return lax.dot_general(a, b, (((1,), (1,)), ((), ())), preferred_element_type=F32)


def dot_tn(a, b):
    return lax.dot_general(a, b, (((0,), (0,)), ((), ())), preferred_element_type=F32)


def iota(shape, dim):
    return lax.broadcasted_iota(I32, shape, dim)


def split2(v):
    high = v.astype(BF16).astype(F32)
    return high, (v - high).astype(BF16).astype(F32)


def normalize(rows):
    center = jnp.mean(rows, axis=-1, keepdims=True)
    offset = rows - center
    rstd = lax.rsqrt(jnp.mean(offset * offset, axis=-1, keepdims=True) + norm_eps)
    return offset * rstd, rstd


def norm_back(grad, unit, rstd):
    return rstd * (
        grad
        - jnp.mean(grad, axis=-1, keepdims=True)
        - unit * jnp.mean(grad * unit, axis=-1, keepdims=True)
    )


class Sizes:
    def __init__(self, nt, ne, width, tok_dev, tok_group, head_cols, hidden):
        self.nt, self.ne, self.width = nt, ne, width
        self.tok_dev = tok_dev
        self.images = tok_dev // IMAGE_TOKENS
        self.lp = round_up(SPARE + ne, 16)
        self.rows = self.images * self.lp
        self.chunks = nt * self.images
        self.cap = 5 * tok_group // (2 * ne) + 1
        self.spr = -(-self.cap // nt)
        need = self.spr + 2
        self.blk = next((b for b in (16, 32, 64, 128) if b >= need), round_up(need, 128))
        self.epl = 128 // self.blk
        self.hw = head_cols
        self.hpb = head_cols // HEAD_DIM
        self.hid = hidden
        self.slots = ne * self.blk
        self.pieces = width // (4 * self.hw)
        self.small = (4 + ne) * self.pieces
        self.pay = round_up(width + self.small, 8 * ne)


VM = pl.BlockSpec(memory_space=pltpu.VMEM)
SM = pl.BlockSpec(memory_space=pltpu.SMEM)


def call(body, outs, scratch=(), n_in=0, flops=0, nbytes=0, vmem=60):
    return pl.pallas_call(
        body,
        out_shape=outs,
        in_specs=[SM] + [VM] * n_in,
        out_specs=jax.tree.map(lambda _: VM, outs),
        scratch_shapes=list(scratch),
        compiler_params=pltpu.CompilerParams(vmem_limit_bytes=vmem * 1024 * 1024),
        cost_estimate=pl.CostEstimate(flops=flops, bytes_accessed=nbytes, transcendentals=0),
    )


def shape(dims, kind):
    return jax.ShapeDtypeStruct(dims, kind)


def index_body(z, who, route_ref, kept_ref, pos_ref, keep_ref):
    me_t, me_e = who[0], who[1]
    named = jnp.bitwise_xor(iota((z.ne, z.lp), 0), me_e)
    before = jnp.where(iota((z.lp, z.lp), 0) < iota((z.lp, z.lp), 1), 1.0, 0.0).astype(BF16)
    count = jnp.zeros((z.ne, 1), F32)
    for c in range(z.chunks):
        block, img = c // z.images, c % z.images
        first = route_ref[0, c : c + 1, :] == named
        other = route_ref[1, c : c + 1, :] == named
        hit = jnp.where(first | other, 1.0, 0.0)
        place = dot_nn(hit.astype(BF16), before) + count
        count = count + jnp.sum(hit, axis=1, keepdims=True)
        at = jnp.bitwise_xor(block, me_t) * z.images + img
        pos_ref[at] = jnp.where(hit > 0, place, -1.0).astype(I32)
        keep_ref[at] = jnp.where(first, kept_ref[0, c : c + 1, :], 0.0) + jnp.where(
            other, kept_ref[1, c : c + 1, :], 0.0
        )


def attend_body(z, who, x_ref, ln_ref, wr_ref, *refs):
    nt, lp, hw = z.nt, z.lp, z.hw
    qkv_w, out_w = refs[:nt], refs[nt : 2 * nt]
    z_ref, resid_ref, qkv_ref, ctx_ref, p_ref, xp, zb, pt = refs[2 * nt :]
    me_t = who[0]
    xp[...] = jnp.zeros(xp.shape, F32)
    for i in range(z.images):
        xp[i * lp : i * lp + IMAGE_TOKENS, :] = x_ref[
            i * IMAGE_TOKENS : (i + 1) * IMAGE_TOKENS, :
        ]
    unit, _ = normalize(xp[...])
    h1 = (unit * ln_ref[0:1, :] + ln_ref[1:2, :]).astype(BF16)
    head_of = iota((lp, hw), 1) // HEAD_DIM
    real = iota((lp, lp), 1) < IMAGE_TOKENS
    real_row = iota((lp, 1), 0) < IMAGE_TOKENS
    lane = iota((1, 128), 1)
    tops = jnp.full((1, 128), low_value, F32)
    attn = jnp.zeros((z.rows, z.width), F32)
    for r in range(nt):
        qkv = dot_nn(h1, qkv_w[r][...]).astype(BF16)
        qkv_ref[r] = qkv
        ctxs = []
        for i in range(z.images):
            at = slice(i * lp, (i + 1) * lp)
            q, k, v = (qkv[at, n * hw : (n + 1) * hw] for n in range(3))
            ctx = jnp.zeros((lp, hw), F32)
            for j in range(z.hpb):
                mine = head_of == j
                s = dot_nt(jnp.where(mine, q, jnp.zeros_like(q)), k) * (HEAD_DIM**-0.5)
                s = jnp.where(real, s, low_value)
                peak = jnp.max(s, axis=1, keepdims=True)
                top = jnp.max(jnp.where(real_row, peak, low_value), axis=0, keepdims=True)
                head = jnp.bitwise_xor(me_t, r) * z.hpb + j
                tops = jnp.where(lane == head, jnp.maximum(tops, top), tops)
                e = jnp.exp(s - peak)
                p = (e * (1.0 / jnp.sum(e, axis=1, keepdims=True))).astype(BF16)
                p_ref[(r * z.images + i) * z.hpb + j] = p
                ctx = jnp.where(mine, dot_nn(p, v), ctx)
            ctxs.append(ctx.astype(BF16))
        ctx = jnp.concatenate(ctxs, axis=0)
        ctx_ref[r] = ctx
        attn = attn + dot_nn(ctx, out_w[r][...])
    resid = xp[...] + attn
    resid_ref[...] = resid
    unit, _ = normalize(resid)
    second = unit * ln_ref[2:3, :] + ln_ref[3:4, :]
    w_hi, w_lo = (v.astype(BF16) for v in split2(wr_ref[...]))
    row = iota((lp, 1), 0)
    t_hi = tops.astype(BF16).astype(F32)
    t_mid = (tops - t_hi).astype(BF16).astype(F32)
    t_lo = tops - t_hi - t_mid
    for i in range(z.images):
        part = second[i * lp : (i + 1) * lp]
        s_hi, s_lo = (v.astype(BF16) for v in split2(part))
        logits = dot_nt(w_hi, s_hi) + (dot_nt(w_hi, s_lo) + dot_nt(w_lo, s_hi))
        e = jnp.exp(logits - jnp.max(logits, axis=0, keepdims=True))
        p_hi, p_lo = split2(e / jnp.sum(e, axis=0, keepdims=True))
        pt[...] = jnp.zeros(pt.shape, F32)
        pt[:, 0:lp] = p_hi
        pt[:, 256 : 256 + lp] = p_lo
        zb[...] = jnp.where(row < IMAGE_TOKENS, part, 0.0)
        for n, t in enumerate((t_hi, t_mid, t_lo)):
            zb[TOP_ROW + n : TOP_ROW + n + 1, 0:128] = t
        zb[SPARE : SPARE + z.ne, :] = pt[...]
        z_ref[i * lp : (i + 1) * lp, :] = zb[...].astype(BF16)


def tail_rows(z, ref, i):
    start = (TOP_ROW // 16) * 16
    return ref[i * z.lp + start : (i + 1) * z.lp, :].astype(F32), start


def probs_of(z, ref, i):
    tail, start = tail_rows(z, ref, i)
    both = tail[SPARE - start : SPARE - start + z.ne]
    return both[:, 0 : z.lp] + both[:, 256 : 256 + z.lp]


def dispatch_body(z, with_gates, who, pos_ref, *refs):
    nt, ne, lp, blk = z.nt, z.ne, z.lp, z.blk
    me_t = who[0]
    if with_gates:
        keep_ref, refs = refs[0], refs[1:]
    rows, outs, acc = refs[:nt], refs[nt : nt + ne], refs[nt + ne]
    gacc = refs[nt + ne + 1] if with_gates else None
    slot = iota((blk, lp), 0)
    slot = jnp.where(slot < z.spr, slot + me_t * z.spr, -2)
    tops = None
    for c in range(z.chunks):
        r, i = c // z.images, c % z.images
        hot = jnp.concatenate(
            [
                jnp.where(pos_ref[c, e : e + 1, :] == slot, 1.0, 0.0).astype(BF16)
                for e in range(ne)
            ],
            axis=0,
        )
        part = dot_nn(hot, rows[r][i * lp : (i + 1) * lp, :])
        acc[...] = part if c == 0 else acc[...] + part
        if with_gates:
            g_hi, g_lo = split2(probs_of(z, rows[r], i) * keep_ref[c])
            both = jnp.concatenate([g_hi, g_lo], axis=0).astype(BF16)
            part = dot_nt(both, hot)
            gacc[...] = part if c == 0 else gacc[...] + part
            if i == 0:
                tail, start = tail_rows(z, rows[r], i)
                three = tail[TOP_ROW - start : TOP_ROW - start + 3, 0:128]
                top = three[0:1] + three[1:2] + three[2:3]
                tops = top if tops is None else jnp.maximum(tops, top)
    if with_gates:
        t_hi = tops.astype(BF16).astype(F32)
        t_mid = (tops - t_hi).astype(BF16).astype(F32)
        t_lo = tops - t_hi - t_mid
        none = jnp.zeros((1, 128), F32)
        top_row = jnp.concatenate([t_hi, t_mid, t_lo, none], axis=1)
        row = iota((blk, 1), 0)
        half = iota((1, 128), 1) // blk
    for e in range(ne):
        block = acc[e * blk : (e + 1) * blk, :]
        if with_gates:
            tile = slice((e // z.epl) * 128, (e // z.epl) * 128 + 128)
            g_hi = jnp.where(half == e % z.epl, gacc[e : e + 1, tile], 0.0)
            g_lo = jnp.where(half == e % z.epl, gacc[ne + e : ne + e + 1, tile], 0.0)
            gates = jnp.concatenate([g_hi, g_lo, none, none], axis=1)
            block = jnp.where(row == z.spr, gates, block)
            block = jnp.where(row == z.spr + 1, top_row, block)
        outs[e][...] = block.astype(BF16)


def spare_pair(z, ref):
    start = (z.spr // 16) * 16
    tail = ref[start : z.blk, :].astype(F32)
    return tail[z.spr - start : z.spr - start + 1], tail[z.spr - start + 1 : z.spr - start + 2]


def expert_body(z, who, *refs):
    nt, ne, blk, hid, width = z.nt, z.ne, z.blk, z.hid, z.width
    rows_in, dy_in = refs[:ne], refs[ne : 2 * ne]
    weights = refs[2 * ne : 2 * ne + nt]
    refs = refs[2 * ne + nt :]
    back, mixed, grads = refs[:ne], refs[ne : 2 * ne], refs[2 * ne : 2 * ne + nt]
    top_ref, rows, g, rows_t, g_t, gate, o_acc, d_acc, act, du = refs[2 * ne + nt :]
    diag = iota((blk, 128), 0) == iota((blk, 128), 1) % blk
    real = iota((blk, 1), 0) < z.spr
    tops = None
    for e in range(ne):
        at = slice(e * blk, (e + 1) * blk)
        rows[at, :] = jnp.where(real, rows_in[e][...], jnp.zeros((), BF16))
        gates, top = spare_pair(z, rows_in[e])
        top = top[:, 0:128] + top[:, 128:256] + top[:, 256:384]
        tops = top if tops is None else jnp.maximum(tops, top)
        line = gates[:, 0:128] + gates[:, 128:256]
        column = jnp.sum(jnp.where(diag, line, 0.0), axis=1, keepdims=True)
        gate[at, :] = jnp.broadcast_to(column, (blk, 128))
        g[at, :] = (column * dy_in[e][...].astype(F32)).astype(BF16)
    top_ref[...] = tops
    rows_t[...] = rows[...].T
    g_t[...] = g[...].T
    tile = min(512, z.slots)
    for r in range(nt):

        def step(n, carry, r=r):
            at = pl.ds(pl.multiple_of(n * tile, tile), tile)
            u = dot_nn(rows[at, :], weights[r][0:width, :])
            cube = 0.7978845608028654 * 0.044715 * u * u
            t = jnp.tanh(u * (0.7978845608028654 + cube))
            h = 0.5 + 0.5 * t
            a = (u * h).astype(BF16)
            slope = h + 2.0 * h * (1.0 - h) * u * (0.7978845608028654 + 3.0 * cube)
            second_w = weights[r][width : 2 * width, :]
            da = dot_nn(g[at, :], second_w)
            d = (da * slope).astype(BF16)
            act[at, :] = a
            du[at, :] = d
            o = dot_nt(a, second_w)
            b = dot_nt(d, weights[r][0:width, :])
            o_acc[at, :] = o if r == 0 else o_acc[at, :] + o
            d_acc[at, :] = b if r == 0 else d_acc[at, :] + b
            return carry

        lax.fori_loop(0, z.slots // tile, step, 0)
        grads[r][:, 0:hid] = dot_nn(rows_t[...], du[...]).astype(BF16)
        grads[r][:, hid : 2 * hid] = dot_nn(g_t[...], act[...]).astype(BF16)
    row = iota((blk, 1), 0)
    none = jnp.zeros((1, 128), F32)
    for e in range(ne):
        at = slice(e * blk, (e + 1) * blk)
        o = o_acc[at, :]
        dgate = jnp.sum(o * dy_in[e][...].astype(F32), axis=1, keepdims=True)
        line = jnp.sum(jnp.where(diag, dgate, 0.0), axis=0, keepdims=True)
        hi, lo = split2(line)
        line = jnp.concatenate([hi, lo, none, none], axis=1)
        back[e][...] = jnp.where(row == z.spr, line, d_acc[at, :]).astype(BF16)
        mixed[e][...] = (gate[at, 0:1] * o).astype(BF16)


def hot_columns(z, post_ref, c, base):
    lane = iota((z.lp, 128), 1)
    slot = lane % z.blk
    slot = jnp.where(slot < z.spr, slot + base, -2)
    tiles = []
    for p in range(z.ne // z.epl):
        column = post_ref[c, :, p * z.epl : p * z.epl + 1]
        pick = jnp.broadcast_to(column, (z.lp, 128))
        for n in range(1, z.epl):
            e = p * z.epl + n
            pick = jnp.where(lane // z.blk == n, post_ref[c, :, e : e + 1], pick)
        tiles.append(jnp.where(pick == slot, 1.0, 0.0).astype(BF16))
    return jnp.concatenate(tiles, axis=1)


def combine_body(z, with_router, who, post_ref, *refs):
    nt, ne, lp, blk = z.nt, z.ne, z.lp, z.blk
    base = who[0] * z.spr
    if with_router:
        keep_ref, wr_ref = refs[:2]
        rows, refs = refs[2 : 2 + nt], refs[2 + nt :]
    blocks, outs, refs = refs[:ne], refs[ne : ne + nt], refs[ne + nt :]
    if with_router:
        gr_ref, refs = refs[0], refs[1:]
    stack = refs[0]
    for e in range(ne):
        stack[e * blk : (e + 1) * blk, :] = blocks[e][...]
    if with_router:
        row = iota((ne, 128), 0)
        half = iota((ne, 128), 1) // blk
        tiles = []
        for p in range(ne // z.epl):
            hi = jnp.zeros((ne, 128), F32)
            lo = jnp.zeros((ne, 128), F32)
            for n in range(z.epl):
                e = p * z.epl + n
                line, _ = spare_pair(z, blocks[e])
                own = (row == e) & (half == n)
                hi = jnp.where(own, line[:, 0:128], hi)
                lo = jnp.where(own, line[:, 128:256], lo)
            tiles.append(jnp.concatenate([hi, lo], axis=0))
        dgate = jnp.concatenate(tiles, axis=1).astype(BF16)
        unit = jnp.where(iota((lp, lp), 0) == iota((lp, lp), 1), 1.0, 0.0).astype(BF16)
        wr = wr_ref[...].astype(BF16)
        wr = jnp.concatenate([wr, wr], axis=0)
        total = jnp.zeros((2 * ne, z.width), F32)
    for c in range(z.chunks):
        r, i = c // z.images, c % z.images
        at = slice(i * lp, (i + 1) * lp)
        hot = hot_columns(z, post_ref, c, base)
        part = dot_nn(hot, stack[...])
        if with_router:
            both = dot_nt(dgate, hot)
            dp = (both[0:ne] + both[ne : 2 * ne]) * keep_ref[c]
            pr = probs_of(z, rows[r], i)
            dl = pr * (dp - jnp.sum(pr * dp, axis=0, keepdims=True))
            dl = jnp.concatenate(split2(dl), axis=0).astype(BF16)
            part = part + dot_nn(dot_nt(unit, dl).astype(BF16), wr)
            total = total + dot_nn(dl, rows[r][at, :])
        outs[r][at, :] = part.astype(BF16)
    if with_router:
        gr_ref[...] = total[0:ne] + total[ne : 2 * ne]


def attend_back_body(z, parts, who, x_ref, dy_ref, ln_ref, resid_ref, gr_ref, qkv_ref, ctx_ref, p_ref, *refs):
    nt, lp, hw = z.nt, z.lp, z.hw
    dz_parts, refs = refs[:parts], refs[parts:]
    qkv_w, out_w, refs = refs[:nt], refs[nt : 2 * nt], refs[2 * nt :]
    in_ref, pays, xp, dyp, tail = refs[0], refs[1 : 1 + nt], *refs[1 + nt :]
    me_e = who[1]
    xp[...] = jnp.zeros(xp.shape, F32)
    dyp[...] = jnp.zeros(dyp.shape, F32)
    for i in range(z.images):
        to = slice(i * lp, i * lp + IMAGE_TOKENS)
        of = slice(i * IMAGE_TOKENS, (i + 1) * IMAGE_TOKENS)
        xp[to, :] = x_ref[of, :]
        dyp[to, :] = dy_ref[of, :]
    unit1, rstd1 = normalize(xp[...])
    h1 = (unit1 * ln_ref[0:1, :] + ln_ref[1:2, :]).astype(BF16)
    dz = dz_parts[0][...].astype(F32)
    for p in dz_parts[1:]:
        dz = dz + p[...].astype(F32)
    unit2, rstd2 = normalize(resid_ref[...])
    dresid = norm_back(dz * ln_ref[2:3, :], unit2, rstd2) + dyp[...]
    tail[...] = jnp.zeros(tail.shape, F32)
    tail[2:3, :] = jnp.sum(dz * unit2, axis=0, keepdims=True)
    tail[3:4, :] = jnp.sum(dz, axis=0, keepdims=True)
    for e in range(z.ne):
        tail[pl.ds(4 + jnp.bitwise_xor(e, me_e), 1), :] = gr_ref[e : e + 1, :]
    da = dresid.astype(BF16)
    head_of = iota((lp, hw), 1) // HEAD_DIM
    dh = jnp.zeros((z.rows, z.width), F32)
    scale = HEAD_DIM**-0.5
    for r in range(nt):
        dctx = dot_nt(da, out_w[r][...]).astype(BF16)
        pieces = []
        for i in range(z.images):
            at = slice(i * lp, (i + 1) * lp)
            q, k, v = (qkv_ref[r, at, n * hw : (n + 1) * hw] for n in range(3))
            dc = dctx[at]
            dq = jnp.zeros((lp, hw), F32)
            dk = jnp.zeros((lp, hw), F32)
            dv = jnp.zeros((lp, hw), F32)
            for j in range(z.hpb):
                mine = head_of == j
                p = p_ref[(r * z.images + i) * z.hpb + j]
                dp = dot_nt(jnp.where(mine, dc, jnp.zeros_like(dc)), v)
                pf = p.astype(F32)
                w = pf * dp
                ds = (w - pf * jnp.sum(w, axis=1, keepdims=True)).astype(BF16)
                dq = jnp.where(mine, dot_nn(ds, k) * scale, dq)
                dk = jnp.where(mine, dot_tn(ds, q) * scale, dk)
                dv = jnp.where(mine, dot_tn(p, dc), dv)
            pieces.append(jnp.concatenate([dq, dk, dv], axis=1).astype(BF16))
        dqkv = jnp.concatenate(pieces, axis=0)
        pays[r][0 : z.width, 0 : 3 * hw] = dot_tn(h1, dqkv).astype(BF16)
        pays[r][0 : z.width, 3 * hw : 4 * hw] = dot_tn(da, ctx_ref[r]).astype(BF16)
        dh = dh + dot_nt(dqkv, qkv_w[r][...])
    tail[0:1, :] = jnp.sum(dh * unit1, axis=0, keepdims=True)
    tail[1:2, :] = jnp.sum(dh, axis=0, keepdims=True)
    din = dresid + norm_back(dh * ln_ref[0:1, :], unit1, rstd1)
    xp[...] = din
    for i in range(z.images):
        in_ref[i * IMAGE_TOKENS : (i + 1) * IMAGE_TOKENS, :] = xp[
            i * lp : i * lp + IMAGE_TOKENS, :
        ]
    n = 4 + z.ne
    lines = tail[0:n, :]
    wide = 4 * hw
    extra = jnp.concatenate(
        [lines[:, s * wide : (s + 1) * wide] for s in range(z.pieces)]
        + [jnp.zeros((z.pay - z.width - z.small, wide), F32)],
        axis=0,
    ).astype(BF16)
    for r in range(nt):
        pays[r][z.width : z.pay, :] = extra


def finish_body(z, parts, who, resid_ref, *refs):
    out_ref, xp = refs[parts], refs[parts + 1]
    total = refs[0][...].astype(F32)
    for p in refs[1:parts]:
        total = total + p[...].astype(F32)
    xp[...] = resid_ref[...] + total
    for i in range(z.images):
        out_ref[i * IMAGE_TOKENS : (i + 1) * IMAGE_TOKENS, :] = xp[
            i * z.lp : i * z.lp + IMAGE_TOKENS, :
        ]


def swap(value, axis, bit):
    n = lax.axis_size(axis)
    return lax.ppermute(value, axis, [(k, k ^ bit) for k in range(n)])


def gather_blocks(own, axis):
    n = lax.axis_size(axis)
    bits = [1 << k for k in range(n.bit_length() - 1)]
    blocks = {0: own}
    for bit in bits[1:] + bits[:1]:
        for r in list(blocks):
            blocks[r ^ bit] = swap(blocks[r], axis, bit)
    return [blocks[r] for r in range(n)]


def scatter_sum(blocks, axis):
    n = lax.axis_size(axis)
    bits = [1 << k for k in range(n.bit_length() - 1)]
    left = {r: [b] for r, b in enumerate(blocks)}
    for bit in bits:
        for r in sorted(left, reverse=True):
            if r & bit:
                left[r ^ bit].append(swap(total_low(left.pop(r)), axis, bit))
    return left[0]


def total_low(parts):
    if len(parts) == 1:
        return parts[0]
    return total(parts).astype(BF16)


def total(parts):
    out = parts[0].astype(F32)
    for p in parts[1:]:
        out = out + p.astype(F32)
    return out


def trade(blocks, axis):
    return [b if r == 0 else swap(b, axis, r) for r, b in enumerate(blocks)]


def sum_all(value, axis):
    n = lax.axis_size(axis)
    bits = [1 << k for k in range(n.bit_length() - 1)]
    me = lax.axis_index(axis)
    for bit in bits:
        half = value.shape[0] // 2
        upper = (me // bit) % 2
        keep = lax.dynamic_slice_in_dim(value, upper * half, half, 0)
        send = lax.dynamic_slice_in_dim(value, (1 - upper) * half, half, 0)
        value = total_low([keep, swap(send, axis, bit)])
    for bit in reversed(bits):
        upper = (me // bit) % 2
        other = swap(value, axis, bit)
        value = jnp.where(
            upper == 0,
            jnp.concatenate([value, other], 0),
            jnp.concatenate([other, value], 0),
        )
    return value


def shards(
    block_in,
    out_grad,
    routes,
    kept_pairs,
    ln1_gain,
    ln1_bias,
    w_query,
    w_key,
    w_value,
    w_attn_out,
    ln2_gain,
    ln2_bias,
    w_router,
    w_expert_in,
    w_expert_out,
):
    nt, ne = lax.axis_size("tensor"), lax.axis_size("expert")
    width = block_in.shape[1]
    z = Sizes(
        nt, ne, width, block_in.shape[0], routes.shape[0], w_query.shape[1], w_expert_in.shape[2]
    )
    lp, hw, hid, blk = z.lp, z.hw, z.hid, z.blk
    me_t, me_e = lax.axis_index("tensor"), lax.axis_index("expert")
    who = jnp.stack([me_t, me_e]).astype(I32)
    body = functools.partial

    qkv_own = jnp.concatenate([w_query, w_key, w_value], axis=1).astype(BF16)
    out_own = w_attn_out.astype(BF16)
    qkv_w = gather_blocks(qkv_own, "tensor")
    out_w = gather_blocks(out_own, "tensor")
    pad = ((0, 0), (0, lp - IMAGE_TOKENS), (0, 0))
    dy_low = jnp.pad(
        out_grad.astype(BF16).reshape(z.images, IMAGE_TOKENS, width), pad
    ).reshape(z.rows, width)
    dy_rows = gather_blocks(dy_low, "tensor")
    expert_w = gather_blocks(
        jnp.concatenate([w_expert_in[0], w_expert_out[0].T], 0).astype(BF16), "tensor"
    )

    lines = jnp.pad(
        jnp.stack([routes.T, kept_pairs.T]).reshape(2, 2, z.chunks, IMAGE_TOKENS),
        ((0, 0), (0, 0), (0, 0), (0, lp - IMAGE_TOKENS)),
        constant_values=-1,
    )
    pos, keep = call(
        body(index_body, z),
        [shape((z.chunks, ne, lp), I32), shape((z.chunks, ne, lp), F32)],
        n_in=2,
        flops=10**7,
        nbytes=10**5,
    )(who, lines[0], lines[1].astype(F32))
    post = pos.transpose(0, 2, 1)
    block = shape((blk, width), BF16)
    rows_low = shape((z.rows, width), BF16)

    dy_sent = call(
        body(dispatch_body, z, False),
        [block] * ne,
        [pltpu.VMEM((z.slots, width), F32)],
        n_in=1 + nt,
        flops=2 * z.slots * z.rows * nt * width,
        nbytes=3 * 10**6,
    )(who, pos, *dy_rows)
    dy_in = trade(dy_sent, "expert")

    norms = jnp.stack([ln1_gain, ln1_bias, ln2_gain, ln2_bias])
    wr = w_router.T[jnp.bitwise_xor(jnp.arange(ne, dtype=I32), me_e)]
    heads = nt * z.images * z.hpb
    second, resid, qkv, ctx, probs = call(
        body(attend_body, z),
        [
            rows_low,
            shape((z.rows, width), F32),
            shape((nt, z.rows, 3 * hw), BF16),
            shape((nt, z.rows, hw), BF16),
            shape((heads, lp, lp), BF16),
        ],
        [
            pltpu.VMEM((z.rows, width), F32),
            pltpu.VMEM((lp, width), F32),
            pltpu.VMEM((ne, width), F32),
        ],
        n_in=3 + 2 * nt,
        flops=2 * z.rows * width * width * 4,
        nbytes=6 * 10**6,
    )(who, block_in, norms, wr, *qkv_w, *out_w)
    rows = gather_blocks(second, "tensor")
    sent = call(
        body(dispatch_body, z, True),
        [block] * ne,
        [pltpu.VMEM((z.slots, width), F32), pltpu.VMEM((2 * ne, z.slots), F32)],
        n_in=2 + nt,
        flops=2 * z.slots * z.rows * nt * width,
        nbytes=3 * 10**6,
    )(who, pos, keep, *rows)
    arrived = trade(sent, "expert")

    outs = call(
        body(expert_body, z),
        [block] * (2 * ne) + [shape((width, 2 * hid), BF16)] * nt + [shape((1, 128), F32)],
        [
            pltpu.VMEM((z.slots, width), BF16),
            pltpu.VMEM((z.slots, width), BF16),
            pltpu.VMEM((width, z.slots), BF16),
            pltpu.VMEM((width, z.slots), BF16),
            pltpu.VMEM((z.slots, 128), F32),
            pltpu.VMEM((z.slots, width), F32),
            pltpu.VMEM((z.slots, width), F32),
            pltpu.VMEM((z.slots, hid), BF16),
            pltpu.VMEM((z.slots, hid), BF16),
        ],
        n_in=2 * ne + nt,
        flops=12 * z.slots * width * hid * nt,
        nbytes=16 * 10**6,
    )(who, *arrived, *dy_in, *expert_w)
    back = trade(outs[:ne], "expert")
    mixed = trade(outs[ne : 2 * ne], "expert")
    expert_parts = scatter_sum(outs[2 * ne : 2 * ne + nt], "tensor")
    tops = outs[2 * ne + nt]

    partial = call(
        body(combine_body, z, True),
        [rows_low] * nt + [shape((ne, width), F32)],
        [pltpu.VMEM((z.slots, width), BF16)],
        n_in=3 + nt + ne,
        flops=2 * z.slots * z.rows * nt * width,
        nbytes=5 * 10**6,
    )(who, post, keep, wr, *rows, *back)
    router_part = partial[nt]
    dz_parts = scatter_sum(partial[:nt], "tensor")
    mixed_part = call(
        body(combine_body, z, False),
        [rows_low] * nt,
        [pltpu.VMEM((z.slots, width), BF16)],
        n_in=1 + ne,
        flops=2 * z.slots * z.rows * nt * width,
        nbytes=4 * 10**6,
    )(who, post, *mixed)
    mixed_parts = scatter_sum(mixed_part, "tensor")
    block_out = call(
        body(finish_body, z, len(mixed_parts)),
        shape((z.tok_dev, width), F32),
        [pltpu.VMEM((z.rows, width), F32)],
        n_in=1 + len(mixed_parts),
        flops=10**6,
        nbytes=3 * 10**6,
    )(who, resid, *mixed_parts)

    outs = call(
        body(attend_back_body, z, len(dz_parts)),
        [shape((z.tok_dev, width), F32)] + [shape((z.pay, 4 * hw), BF16)] * nt,
        [
            pltpu.VMEM((z.rows, width), F32),
            pltpu.VMEM((z.rows, width), F32),
            pltpu.VMEM((round_up(4 + ne, 8), width), F32),
        ],
        n_in=8 + len(dz_parts) + 2 * nt,
        flops=2 * z.rows * width * width * 8,
        nbytes=10**7,
    )(who, block_in, out_grad, norms, resid, router_part, qkv, ctx, probs, *dz_parts, *qkv_w, *out_w)
    input_grad = outs[0]
    summed = sum_all(total_low(scatter_sum(outs[1:], "tensor")), "expert").astype(F32)
    small = (
        summed[width : width + z.small]
        .reshape(z.pieces, 4 + ne, 4 * hw)
        .transpose(1, 0, 2)
        .reshape(4 + ne, width)
    )
    grads = total(expert_parts)
    head_maxima = lax.dynamic_slice_in_dim(tops[0], me_t * z.hpb, z.hpb, 0)
    factor = jnp.repeat(jnp.sqrt(jnp.minimum(1.0, clip_limit / head_maxima)), HEAD_DIM)
    return (
        block_out,
        input_grad,
        small[0],
        small[1],
        summed[:width, :hw],
        summed[:width, hw : 2 * hw],
        summed[:width, 2 * hw : 3 * hw],
        summed[:width, 3 * hw :].T,
        small[2],
        small[3],
        small[4:].T,
        grads[:, :hid][None],
        grads[:, hid:].T[None],
        head_maxima,
        w_query * factor[None, :],
        w_key * factor[None, :],
    )


def solution(mesh):
    placed = (
        P(("expert", "tensor"), None),
        P(("expert", "tensor"), None),
        P("expert", None),
        P("expert", None),
        P(),
        P(),
        P(None, "tensor"),
        P(None, "tensor"),
        P(None, "tensor"),
        P("tensor", None),
        P(),
        P(),
        P(),
        P("expert", None, "tensor"),
        P("expert", "tensor", None),
    )
    return jax.shard_map(
        shards,
        mesh=mesh,
        in_specs=placed,
        out_specs=(
            P(("expert", "tensor"), None),
            P(("expert", "tensor"), None),
            P(),
            P(),
            P(None, "tensor"),
            P(None, "tensor"),
            P(None, "tensor"),
            P("tensor", None),
            P(),
            P(),
            P(),
            P("expert", None, "tensor"),
            P("expert", "tensor", None),
            P("tensor"),
            P(None, "tensor"),
            P(None, "tensor"),
        ),
        check_vma=False,
    )
```

```python
import functools

import jax
import jax.numpy as jnp
from jax import lax
from jax.experimental import pallas as pl
from jax.experimental.pallas import tpu as pltpu
from jax.sharding import PartitionSpec as P

HEAD_DIM = 64
IMAGE_TOKENS = 197
SPARE = 200
TOP_ROW = 197

F32 = jnp.float32
BF16 = jnp.bfloat16
I32 = jnp.int32

clip_limit = 4.0
norm_eps = 1e-06
low_value = -1e30


def round_up(value, unit):
    return -(-value // unit) * unit


def dot_nn(a, b):
    return lax.dot_general(a, b, (((1,), (0,)), ((), ())), preferred_element_type=F32)


def dot_nt(a, b):
    return lax.dot_general(a, b, (((1,), (1,)), ((), ())), preferred_element_type=F32)


def dot_tn(a, b):
    return lax.dot_general(a, b, (((0,), (0,)), ((), ())), preferred_element_type=F32)


def iota(shape, dim):
    return lax.broadcasted_iota(I32, shape, dim)


def split2(v):
    high = v.astype(BF16).astype(F32)
    return high, (v - high).astype(BF16).astype(F32)


def normalize(rows):
    center = jnp.mean(rows, axis=-1, keepdims=True)
    offset = rows - center
    rstd = lax.rsqrt(jnp.mean(offset * offset, axis=-1, keepdims=True) + norm_eps)
    return offset * rstd, rstd


def norm_back(grad, unit, rstd):
    return rstd * (
        grad
        - jnp.mean(grad, axis=-1, keepdims=True)
        - unit * jnp.mean(grad * unit, axis=-1, keepdims=True)
    )


def halving_bits(n):
    return [1 << k for k in range(n.bit_length() - 1)]


class Sizes:
    def __init__(self, nt, ne, width, tok_dev, tok_group, head_cols, hidden):
        self.nt, self.ne, self.width = nt, ne, width
        self.tok_dev = tok_dev
        self.images = tok_dev // IMAGE_TOKENS
        self.lp = round_up(SPARE + ne, 16)
        self.rows = self.images * self.lp
        self.chunks = nt * self.images
        self.cap = 5 * tok_group // (2 * ne) + 1
        self.spr = -(-self.cap // nt)
        need = self.spr + 2
        self.blk = next((b for b in (16, 32, 64, 128) if b >= need), round_up(need, 128))
        self.epl = 128 // self.blk
        self.hw = head_cols
        self.hpb = head_cols // HEAD_DIM
        self.hid = hidden
        self.slots = ne * self.blk
        self.wide = 2 * self.hw
        self.pieces = width // self.wide
        self.crow = width // ne
        self.prow = self.crow + 8
        bits = halving_bits(ne)
        self.offset = places(bits)


SM = pl.BlockSpec(memory_space=pltpu.SMEM)
VM = pl.BlockSpec(memory_space=pltpu.VMEM)
ANY = pl.BlockSpec(memory_space=pl.ANY)


class Far:
    def __init__(self, value):
        self.value = value


class Given:
    def __init__(self, ref, copy):
        self.ref, self.copy = ref, copy
        copy.start()

    def wait(self):
        if self.copy is not None:
            self.copy.wait()
            self.copy = None

    def __getitem__(self, at):
        self.wait()
        return self.ref[at]


def place(value, space):
    return pltpu.with_memory_space_constraint(value, space)


def call(body, outs, args, scratch=(), after=()):
    skip = len(after)
    keep = lax.axis_size("tensor") <= 4
    vmem = 12 if keep else 60
    single = not isinstance(outs, list)
    flat = [outs] if single else outs
    far = [k for k, a in enumerate(args) if isinstance(a, Far)]

    def run(*refs):
        ins, refs = [refs[0], *refs[1 + skip : skip + len(args)]], refs[skip + len(args) :]
        results, refs = refs[: len(flat)], refs[len(flat) :]
        own, refs = refs[: len(scratch)], refs[len(scratch) :]
        for n, k in enumerate(far):
            ins[k] = Given(refs[n], pltpu.make_async_copy(ins[k], refs[n], refs[-1].at[n]))
        body(*ins, *results, *own)
        for k in far:
            ins[k].wait()

    extra = [pltpu.VMEM(args[k].value.shape, args[k].value.dtype) for k in far]
    if far:
        extra.append(pltpu.SemaphoreType.DMA((len(far),)))
    got = pl.pallas_call(
        run,
        out_shape=[
            o.value if isinstance(o, Far) else pltpu.VMEM(o.shape, o.dtype) if keep else o
            for o in flat
        ],
        in_specs=[SM] + [ANY] * skip + [ANY if k in far else VM for k in range(1, len(args))],
        out_specs=[VM] * len(flat),
        scratch_shapes=[*scratch, *extra],
        compiler_params=pltpu.CompilerParams(vmem_limit_bytes=vmem * 1024 * 1024),
    )(
        args[0],
        *after,
        *[
            place(a.value, pltpu.HBM) if isinstance(a, Far) else place(a, pltpu.VMEM) if keep else a
            for a in args[1:]
        ],
    )
    return got[0] if single else list(got)


def hold(values, after):
    n, m = len(values), len(after)

    def run(*refs):
        pass

    out = pl.pallas_call(
        run,
        out_shape=[shape(v.shape, v.dtype) for v in values],
        in_specs=[ANY] * (n + m),
        out_specs=[ANY] * n,
        input_output_aliases={k: k for k in range(n)},
        compiler_params=pltpu.CompilerParams(vmem_limit_bytes=1024 * 1024),
    )(*values, *after)
    return list(out)


def shape(dims, kind):
    return jax.ShapeDtypeStruct(dims, kind)


def first_body(z, who, q_ref, k_ref, v_ref, o_ref, out_ref):
    hw = z.hw
    for n, ref in enumerate((q_ref, k_ref, v_ref)):
        out_ref[:, n * hw : (n + 1) * hw] = ref[...].astype(BF16)
    out_ref[:, 3 * hw : 4 * hw] = o_ref[...].T.astype(BF16)


def early_body(z, who, dy_ref, in_ref, out_ref, route_ref, kept_ref, *refs):
    low_ref, w_ref, pos_ref, keep_ref, post_ref, pad = refs
    pad[...] = jnp.zeros(pad.shape, F32)
    for i in range(z.images):
        pad[i * z.lp : i * z.lp + IMAGE_TOKENS, :] = dy_ref[
            i * IMAGE_TOKENS : (i + 1) * IMAGE_TOKENS, :
        ]
    low_ref[...] = pad[...].astype(BF16)
    w_ref[0 : z.width, :] = in_ref[...].astype(BF16)
    w_ref[z.width : 2 * z.width, :] = out_ref[...].T.astype(BF16)
    me_t, me_e = who[0], who[1]
    named = jnp.bitwise_xor(iota((z.ne, z.lp), 0), me_e)
    before = jnp.where(iota((z.lp, z.lp), 0) < iota((z.lp, z.lp), 1), 1.0, 0.0).astype(BF16)
    count = jnp.zeros((z.ne, 1), F32)
    for c in range(z.chunks):
        block, img = c // z.images, c % z.images
        first = route_ref[0, c : c + 1, :] == named
        other = route_ref[1, c : c + 1, :] == named
        hit = jnp.where(first | other, 1.0, 0.0)
        place = dot_nn(hit.astype(BF16), before) + count
        count = count + jnp.sum(hit, axis=1, keepdims=True)
        at = jnp.bitwise_xor(block, me_t) * z.images + img
        place = jnp.where(hit > 0, place, -1.0)
        pos_ref[at] = place.astype(I32)
        post_ref[at] = place.T.astype(I32)
        keep_ref[at] = jnp.where(first, kept_ref[0, c : c + 1, :], 0.0) + jnp.where(
            other, kept_ref[1, c : c + 1, :], 0.0
        )


def attend_body(z, who, x_ref, ln_ref, wr_ref, *refs):
    nt, lp, hw = z.nt, z.lp, z.hw
    weights = refs[:nt]
    z_ref, resid_ref, h1_ref, refs = refs[nt], refs[nt + 1], refs[nt + 2], refs[nt + 3 :]
    qkv_ref, ctx_ref, p_ref = refs[:nt], refs[nt : 2 * nt], refs[2 * nt : 3 * nt]
    xp, zb, pt = refs[3 * nt :]
    me_t = who[0]
    xp[...] = jnp.zeros(xp.shape, F32)
    for i in range(z.images):
        xp[i * lp : i * lp + IMAGE_TOKENS, :] = x_ref[
            i * IMAGE_TOKENS : (i + 1) * IMAGE_TOKENS, :
        ]
    unit, _ = normalize(xp[...])
    h1 = (unit * ln_ref[0:1, :] + ln_ref[1:2, :]).astype(BF16)
    h1_ref[...] = h1
    head_of = iota((lp, hw), 1) // HEAD_DIM
    real = iota((lp, lp), 1) < IMAGE_TOKENS
    real_row = iota((lp, 1), 0) < IMAGE_TOKENS
    lane = iota((1, 128), 1)
    tops = jnp.full((1, 128), low_value, F32)
    attn = jnp.zeros((z.rows, z.width), F32)
    for r in range(nt):
        qkv = dot_nn(h1, weights[r][:, 0 : 3 * hw]).astype(BF16)
        qkv_ref[r][...] = qkv
        ctxs = []
        for i in range(z.images):
            at = slice(i * lp, (i + 1) * lp)
            q, k, v = (qkv[at, n * hw : (n + 1) * hw] for n in range(3))
            ctx = jnp.zeros((lp, hw), F32)
            for j in range(z.hpb):
                mine = head_of == j
                s = dot_nt(jnp.where(mine, q, jnp.zeros_like(q)), k) * (HEAD_DIM**-0.5)
                s = jnp.where(real, s, low_value)
                peak = jnp.max(s, axis=1, keepdims=True)
                top = jnp.max(jnp.where(real_row, peak, low_value), axis=0, keepdims=True)
                head = jnp.bitwise_xor(me_t, r) * z.hpb + j
                tops = jnp.where(lane == head, jnp.maximum(tops, top), tops)
                e = jnp.exp(s - peak)
                p = (e * (1.0 / jnp.sum(e, axis=1, keepdims=True))).astype(BF16)
                p_ref[r][i * z.hpb + j] = p
                ctx = jnp.where(mine, dot_nn(p, v), ctx)
            ctxs.append(ctx.astype(BF16))
        ctx = jnp.concatenate(ctxs, axis=0)
        ctx_ref[r][...] = ctx
        attn = attn + dot_nt(ctx, weights[r][:, 3 * hw : 4 * hw])
    resid = xp[...] + attn
    resid_ref[...] = resid
    unit, _ = normalize(resid)
    second = unit * ln_ref[2:3, :] + ln_ref[3:4, :]
    w_hi, w_lo = (v.astype(BF16) for v in split2(router_rows(z, who, wr_ref)))
    row = iota((lp, 1), 0)
    t_hi = tops.astype(BF16).astype(F32)
    t_mid = (tops - t_hi).astype(BF16).astype(F32)
    t_lo = tops - t_hi - t_mid
    for i in range(z.images):
        part = second[i * lp : (i + 1) * lp]
        s_hi, s_lo = (v.astype(BF16) for v in split2(part))
        logits = dot_nt(w_hi, s_hi) + (dot_nt(w_hi, s_lo) + dot_nt(w_lo, s_hi))
        e = jnp.exp(logits - jnp.max(logits, axis=0, keepdims=True))
        p_hi, p_lo = split2(e / jnp.sum(e, axis=0, keepdims=True))
        pt[...] = jnp.zeros(pt.shape, F32)
        pt[:, 0:lp] = p_hi
        pt[:, 256 : 256 + lp] = p_lo
        zb[...] = jnp.where(row < IMAGE_TOKENS, part, 0.0)
        for n, t in enumerate((t_hi, t_mid, t_lo)):
            zb[TOP_ROW + n : TOP_ROW + n + 1, 0:128] = t
        zb[SPARE : SPARE + z.ne, :] = pt[...]
        z_ref[i * lp : (i + 1) * lp, :] = zb[...].astype(BF16)


def router_rows(z, who, ref):
    return jnp.concatenate(
        [ref[pl.ds(jnp.bitwise_xor(e, who[1]), 1), :] for e in range(z.ne)], axis=0
    )


def tail_rows(z, ref, i):
    start = (TOP_ROW // 16) * 16
    return ref[i * z.lp + start : (i + 1) * z.lp, :].astype(F32), start


def probs_of(z, ref, i):
    tail, start = tail_rows(z, ref, i)
    both = tail[SPARE - start : SPARE - start + z.ne]
    return both[:, 0 : z.lp] + both[:, 256 : 256 + z.lp]


def dispatch_body(z, who, pos_ref, keep_ref, *refs):
    nt, ne, lp, blk = z.nt, z.ne, z.lp, z.blk
    me_t = who[0]
    rows, dy_rows, refs = refs[:nt], refs[nt : 2 * nt], refs[2 * nt :]
    count = ne // 4 + ne // 2
    outs, (acc, dy_acc, gacc) = refs[:count], refs[count:]
    slot = iota((blk, lp), 0)
    slot = jnp.where(slot < z.spr, slot + me_t * z.spr, -2)
    tops = None
    for c in range(z.chunks):
        r, i = c // z.images, c % z.images
        hot = jnp.concatenate(
            [
                jnp.where(pos_ref[c, e : e + 1, :] == slot, 1.0, 0.0).astype(BF16)
                for e in range(ne)
            ],
            axis=0,
        )
        part = dot_nn(hot, dy_rows[r][i * lp : (i + 1) * lp, :])
        dy_acc[...] = part if c == 0 else dy_acc[...] + part
        part = dot_nn(hot, rows[r][i * lp : (i + 1) * lp, :])
        acc[...] = part if c == 0 else acc[...] + part
        g_hi, g_lo = split2(probs_of(z, rows[r], i) * keep_ref[c])
        both = jnp.concatenate([g_hi, g_lo], axis=0).astype(BF16)
        part = dot_nt(both, hot)
        gacc[...] = part if c == 0 else gacc[...] + part
        if i == 0:
            tail, start = tail_rows(z, rows[r], i)
            three = tail[TOP_ROW - start : TOP_ROW - start + 3, 0:128]
            top = three[0:1] + three[1:2] + three[2:3]
            tops = top if tops is None else jnp.maximum(tops, top)
    t_hi = tops.astype(BF16).astype(F32)
    t_mid = (tops - t_hi).astype(BF16).astype(F32)
    t_lo = tops - t_hi - t_mid
    none = jnp.zeros((1, 128), F32)
    top_row = jnp.concatenate([t_hi, t_mid, t_lo, none], axis=1)
    row = iota((blk, 1), 0)
    half = iota((1, 128), 1) // blk
    for e in range(ne):
        tile = slice((e // z.epl) * 128, (e // z.epl) * 128 + 128)
        g_hi = jnp.where(half == e % z.epl, gacc[e : e + 1, tile], 0.0)
        g_lo = jnp.where(half == e % z.epl, gacc[ne + e : ne + e + 1, tile], 0.0)
        gates = jnp.concatenate([g_hi, g_lo, none, none], axis=1)
        block = acc[e * blk : (e + 1) * blk, :]
        block = jnp.where(row == z.spr, gates, block)
        block = jnp.where(row == z.spr + 1, top_row, block)
        if e < ne // 2:
            to, first = outs[e // 2], (e % 2) * 2 * blk
        else:
            to, first = outs[e - ne // 4], 0
        to[first : first + blk, :] = block.astype(BF16)
        to[first + blk : first + 2 * blk, :] = dy_acc[e * blk : (e + 1) * blk, :].astype(BF16)


class Part:
    def __init__(self, ref, first):
        self.ref, self.first = ref, first

    def rows(self, start, stop):
        return self.ref[self.first + start : self.first + stop, :]

    def put(self, value):
        self.ref[self.first : self.first + value.shape[0], :] = value


def blocks_of(z, direct, passed, size=1, at=0):
    out = []
    for k, ref in enumerate(direct):
        out += [Part(ref, at * z.blk), Part(passed, (k * size + at) * z.blk)]
    return out


def spare_pair(z, part):
    start = (z.spr // 16) * 16
    tail = part.rows(start, z.blk).astype(F32)
    return tail[z.spr - start : z.spr - start + 1], tail[z.spr - start + 1 : z.spr - start + 2]


def expert_body(z, near, count, who, *refs):
    nt, ne, blk, hid, width = z.nt, z.ne, z.blk, z.hid, z.width
    half = count // 2
    if near:
        rows_in, dy_in = (blocks_of(z, refs[:half], refs[half], 2, at) for at in range(2))
        refs = refs[half + 1 :]
    else:
        rows_in, dy_in = ([Part(ref, at * blk) for ref in refs[:count]] for at in range(2))
        refs = refs[count:]
    weights, refs = refs[:nt], refs[nt:]
    w = z.width
    if near:
        far_top, refs = refs[0], refs[1:]
    back, refs = [Part(ref, at * blk) for ref in refs[:half] for at in range(2)], refs[half:]
    mixed, refs = [Part(ref, at * blk) for ref in refs[:half] for at in range(2)], refs[half:]
    act, du, refs = refs[:nt], refs[nt : 2 * nt], refs[2 * nt :]
    g, top_ref, rows, gate, o_acc, d_acc = refs
    real = iota((blk, 1), 0) < z.spr
    diag = iota((blk, 128), 0) == iota((blk, 128), 1) % blk
    tops = far_top[...] if near else None
    for n in range(count):
        at = slice(n * blk, (n + 1) * blk)
        rows[at, :] = jnp.where(real, rows_in[n].rows(0, blk), jnp.zeros((), BF16))
        gates, top = spare_pair(z, rows_in[n])
        top = top[:, 0:128] + top[:, 128:256] + top[:, 256:384]
        tops = top if tops is None else jnp.maximum(tops, top)
        line = gates[:, 0:128] + gates[:, 128:256]
        column = jnp.sum(jnp.where(diag, line, 0.0), axis=1, keepdims=True)
        gate[at, :] = jnp.broadcast_to(column, (blk, 128))
    top_ref[...] = tops
    u_first = dot_nn(rows[...], weights[0][0:w, :])
    for n in range(count):
        at = slice(n * blk, (n + 1) * blk)
        g[at, :] = (gate[at, 0:1] * dy_in[n].rows(0, blk).astype(F32)).astype(BF16)
    for r in range(nt):
        u = dot_nn(rows[...], weights[r][0:w, :]) if r else u_first
        second_w = weights[r][w : 2 * w, :]
        cube = 0.7978845608028654 * 0.044715 * u * u
        t = jnp.tanh(u * (0.7978845608028654 + cube))
        h = 0.5 + 0.5 * t
        a = (u * h).astype(BF16)
        slope = h + 2.0 * h * (1.0 - h) * u * (0.7978845608028654 + 3.0 * cube)
        d = (dot_nn(g[...], second_w) * slope).astype(BF16)
        act[r][...] = a
        du[r][...] = d
        o = dot_nt(a, second_w)
        b = dot_nt(d, weights[r][0:w, :])
        o_acc[...] = o if r == 0 else o_acc[...] + o
        d_acc[...] = b if r == 0 else d_acc[...] + b
    row = iota((blk, 1), 0)
    none = jnp.zeros((1, 128), F32)
    for n in range(count):
        at = slice(n * blk, (n + 1) * blk)
        o = o_acc[at, :]
        dgate = jnp.sum(o * dy_in[n].rows(0, blk).astype(F32), axis=1, keepdims=True)
        line = jnp.sum(jnp.where(diag, dgate, 0.0), axis=0, keepdims=True)
        hi, lo = split2(line)
        line = jnp.concatenate([hi, lo, none, none], axis=1)
        back[n].put(jnp.where(row == z.spr, line, d_acc[at, :]).astype(BF16))
        mixed[n].put((gate[at, 0:1] * o).astype(BF16))


def expert_weights_body(z, who, *refs):
    nt, ne, blk, hid = z.nt, z.ne, z.blk, z.hid
    quarter = ne // 4
    rows_in, refs = blocks_of(z, refs[:quarter], refs[quarter], 2), refs[quarter + 1 :]
    rows_in, refs = rows_in + [Part(ref, 0) for ref in refs[: 2 * quarter]], refs[2 * quarter :]
    g, refs = refs[:2], refs[2:]
    act, du = (refs[:nt], refs[2 * nt : 3 * nt]), (refs[nt : 2 * nt], refs[3 * nt : 4 * nt])
    one, two, (rows_t, g_t) = refs[4 * nt : 5 * nt], refs[5 * nt : 6 * nt], refs[6 * nt :]
    real = iota((blk, 1), 0) < z.spr
    rows = [jnp.where(real, part.rows(0, blk), jnp.zeros((), BF16)) for part in rows_in]
    half = ne // 2
    for k in range(2):
        rows_t[k] = jnp.concatenate(rows[k * half : (k + 1) * half], axis=0).T
        g_t[k] = g[k][...].T
    for r in range(nt):
        first = dot_nn(rows_t[0], du[0][r][...]) + dot_nn(rows_t[1], du[1][r][...])
        one[r][...] = first.astype(BF16)
        second = dot_nn(g_t[0], act[0][r][...]) + dot_nn(g_t[1], act[1][r][...])
        two[r][...] = second.astype(BF16)


def hot_columns(z, post_ref, c, base):
    lane = iota((z.lp, 128), 1)
    slot = lane % z.blk
    slot = jnp.where(slot < z.spr, slot + base, -2)
    tiles = []
    for p in range(z.ne // z.epl):
        column = post_ref[c, :, p * z.epl : p * z.epl + 1]
        pick = jnp.broadcast_to(column, (z.lp, 128))
        for n in range(1, z.epl):
            e = p * z.epl + n
            pick = jnp.where(lane // z.blk == n, post_ref[c, :, e : e + 1], pick)
        tiles.append(jnp.where(pick == slot, 1.0, 0.0).astype(BF16))
    return jnp.concatenate(tiles, axis=1)


def combine_body(z, with_router, who, post_ref, *refs):
    nt, ne, lp, blk = z.nt, z.ne, z.lp, z.blk
    base = who[0] * z.spr
    if with_router:
        keep_ref, wr_ref = refs[:2]
        rows, refs = refs[2 : 2 + nt], refs[2 + nt :]
    quarter = ne // 4
    if with_router:
        blocks, refs = blocks_of(z, refs[:quarter], refs[quarter]), refs[quarter + 1 :]
        blocks, refs = blocks + blocks_of(z, refs[:quarter], refs[quarter]), refs[quarter + 1 :]
    else:
        blocks, refs = blocks_of(z, refs[: ne // 2], refs[ne // 2]), refs[ne // 2 + 1 :]
    outs, refs = refs[:nt], refs[nt:]
    if with_router:
        gr_ref, refs = refs[0], refs[1:]
    stack = refs[0]
    for e in range(ne):
        stack[e * blk : (e + 1) * blk, :] = blocks[e].rows(0, blk)
    if with_router:
        row = iota((ne, 128), 0)
        half = iota((ne, 128), 1) // blk
        tiles = []
        for p in range(ne // z.epl):
            hi = jnp.zeros((ne, 128), F32)
            lo = jnp.zeros((ne, 128), F32)
            for n in range(z.epl):
                e = p * z.epl + n
                line, _ = spare_pair(z, blocks[e])
                own = (row == e) & (half == n)
                hi = jnp.where(own, line[:, 0:128], hi)
                lo = jnp.where(own, line[:, 128:256], lo)
            tiles.append(jnp.concatenate([hi, lo], axis=0))
        dgate = jnp.concatenate(tiles, axis=1).astype(BF16)
        unit = jnp.where(iota((lp, lp), 0) == iota((lp, lp), 1), 1.0, 0.0).astype(BF16)
        wr = router_rows(z, who, wr_ref).astype(BF16)
        wr = jnp.concatenate([wr, wr], axis=0)
        total = jnp.zeros((2 * ne, z.width), F32)
    for c in range(z.chunks):
        r, i = c // z.images, c % z.images
        at = slice(i * lp, (i + 1) * lp)
        hot = hot_columns(z, post_ref, c, base)
        part = dot_nn(hot, stack[...])
        if with_router:
            both = dot_nt(dgate, hot)
            dp = (both[0:ne] + both[ne : 2 * ne]) * keep_ref[c]
            pr = probs_of(z, rows[r], i)
            dl = pr * (dp - jnp.sum(pr * dp, axis=0, keepdims=True))
            dl = jnp.concatenate(split2(dl), axis=0).astype(BF16)
            part = part + dot_nn(dot_nt(unit, dl).astype(BF16), wr)
            total = total + dot_nn(dl, rows[r][at, :])
        outs[r][at, :] = part.astype(BF16)
    if with_router:
        gr_ref[...] = total[0:ne] + total[ne : 2 * ne]


def spread_rows(z, lines):
    n = lines.shape[0] * z.pieces
    rows = [lines[:, s * z.wide : (s + 1) * z.wide] for s in range(z.pieces)]
    return jnp.concatenate(rows + [jnp.zeros((8 * z.ne - n, z.wide), F32)], axis=0)


def write_parts(z, who, ref, wide, lines):
    for p in range(z.ne):
        c = jnp.bitwise_xor(z.offset[p], who[1])
        ref[p] = jnp.concatenate([wide[c], lines[c]], axis=0).astype(BF16)


def back_one_body(z, parts, who, dy_ref, ln_ref, resid_ref, gr_ref, h1_ref, *refs):
    nt, lp, hw = z.nt, z.lp, z.hw
    dz_parts, refs = refs[:parts], refs[parts:]
    weights, p_ref, ctx_ref, refs = refs[:nt], refs[nt : 2 * nt], refs[2 * nt : 3 * nt], refs[3 * nt :]
    dresid_ref, dctx_ref, dv_ref, pays = refs[0], refs[1:][:nt], refs[1 + nt :][:nt], refs[1 + 2 * nt :][:nt]
    dyp, tail, buf, lines = refs[1 + 3 * nt :]
    dyp[...] = jnp.zeros(dyp.shape, F32)
    for i in range(z.images):
        dyp[i * lp : i * lp + IMAGE_TOKENS, :] = dy_ref[
            i * IMAGE_TOKENS : (i + 1) * IMAGE_TOKENS, :
        ]
    dz = dz_parts[0][...].astype(F32)
    for p in dz_parts[1:]:
        dz = dz + p[...].astype(F32)
    unit, rstd = normalize(resid_ref[...])
    dresid = norm_back(dz * ln_ref[2:3, :], unit, rstd) + dyp[...]
    dresid_ref[...] = dresid
    tail[...] = jnp.zeros(tail.shape, F32)
    tail[0:1, :] = jnp.sum(dz * unit, axis=0, keepdims=True)
    tail[1:2, :] = jnp.sum(dz, axis=0, keepdims=True)
    for e in range(z.ne):
        tail[pl.ds(8 + jnp.bitwise_xor(e, who[1]), 1), :] = gr_ref[e : e + 1, :]
    rows = spread_rows(z, tail[...])
    for p in range(z.ne):
        lines[p] = rows[8 * p : 8 * p + 8]
    da = dresid.astype(BF16)
    h1_t = h1_ref[...].T
    da_t = da.T
    head_of = iota((lp, hw), 1) // HEAD_DIM
    for r in range(nt):
        dctx = dot_nn(da, weights[r][:, 3 * hw : 4 * hw]).astype(BF16)
        dctx_ref[r][...] = dctx
        pieces = []
        for i in range(z.images):
            dc = dctx[i * lp : (i + 1) * lp]
            dv = jnp.zeros((lp, hw), F32)
            for j in range(z.hpb):
                p = p_ref[r][i * z.hpb + j]
                dv = jnp.where(head_of == j, dot_tn(p, dc), dv)
            pieces.append(dv.astype(BF16))
        dv = jnp.concatenate(pieces, axis=0)
        dv_ref[r][...] = dv
        dw = jnp.concatenate([dot_nn(h1_t, dv), dot_nn(da_t, ctx_ref[r][...])], axis=1)
        for p in range(z.ne):
            buf[p] = dw[p * z.crow : (p + 1) * z.crow]
        write_parts(z, who, pays[r], buf, lines)


def back_two_body(z, who, x_ref, ln_ref, h1_ref, *refs):
    nt, lp, hw = z.nt, z.lp, z.hw
    qkv_ref, dctx_ref, p_ref, dv_ref, refs = (*(refs[k * nt : (k + 1) * nt] for k in range(4)), refs[4 * nt :])
    dresid_ref, refs = refs[0], refs[1:]
    weights, in_ref, pays, xp, tail, buf, lines = (
        refs[:nt],
        refs[nt],
        refs[nt + 1 : 2 * nt + 1],
        *refs[2 * nt + 1 :],
    )
    xp[...] = jnp.zeros(xp.shape, F32)
    for i in range(z.images):
        xp[i * lp : i * lp + IMAGE_TOKENS, :] = x_ref[
            i * IMAGE_TOKENS : (i + 1) * IMAGE_TOKENS, :
        ]
    unit, rstd = normalize(xp[...])
    h1_t = h1_ref[...].T
    head_of = iota((lp, hw), 1) // HEAD_DIM
    dh = jnp.zeros((z.rows, z.width), F32)
    scale = HEAD_DIM**-0.5
    grads = []
    for r in range(nt):
        pieces = []
        for i in range(z.images):
            at = slice(i * lp, (i + 1) * lp)
            q, k, v = (qkv_ref[r][at, n * hw : (n + 1) * hw] for n in range(3))
            dc = dctx_ref[r][at, :]
            dq = jnp.zeros((lp, hw), F32)
            dk = jnp.zeros((lp, hw), F32)
            for j in range(z.hpb):
                mine = head_of == j
                pf = p_ref[r][i * z.hpb + j].astype(F32)
                dp = dot_nt(jnp.where(mine, dc, jnp.zeros_like(dc)), v)
                w = pf * dp
                ds = (w - pf * jnp.sum(w, axis=1, keepdims=True)).astype(BF16)
                dq = jnp.where(mine, dot_nn(ds, k) * scale, dq)
                dk = jnp.where(mine, dot_tn(ds, q) * scale, dk)
            pieces.append(jnp.concatenate([dq, dk], axis=1).astype(BF16))
        dqk = jnp.concatenate(pieces, axis=0)
        grads.append(dot_nn(h1_t, dqk))
        dh = dh + dot_nt(dqk, weights[r][:, 0 : 2 * hw]) + dot_nt(
            dv_ref[r][...], weights[r][:, 2 * hw : 3 * hw]
        )
    tail[...] = jnp.zeros(tail.shape, F32)
    tail[0:1, :] = jnp.sum(dh * unit, axis=0, keepdims=True)
    tail[1:2, :] = jnp.sum(dh, axis=0, keepdims=True)
    rows = spread_rows(z, tail[...])
    for p in range(z.ne):
        lines[p] = rows[8 * p : 8 * p + 8]
    for r in range(nt):
        for p in range(z.ne):
            buf[p] = grads[r][p * z.crow : (p + 1) * z.crow]
        write_parts(z, who, pays[r], buf, lines)
    xp[...] = dresid_ref[...] + norm_back(dh * ln_ref[0:1, :], unit, rstd)
    for i in range(z.images):
        in_ref[i * IMAGE_TOKENS : (i + 1) * IMAGE_TOKENS, :] = xp[
            i * lp : i * lp + IMAGE_TOKENS, :
        ]


def last_body(z, who, low, high, q_ref, k_ref, v_ref, o_ref, n1, n2, n3, n4, router_ref, wide, lines):
    hw, half = z.hw, z.ne // 2
    for p in range(z.ne):
        c = jnp.bitwise_xor(z.offset[p], who[1])
        both = (low, high)[p // half][p % half].astype(F32)
        wide[c] = both[0 : z.crow]
        lines[c] = both[z.crow : z.prow]
    both = jnp.concatenate([wide[p] for p in range(z.ne)], axis=0)
    v_ref[...] = both[:, 0:hw]
    o_ref[...] = both[:, hw : 2 * hw].T
    q_ref[...] = both[:, 2 * hw : 3 * hw]
    k_ref[...] = both[:, 3 * hw : 4 * hw]
    both = jnp.concatenate([lines[p] for p in range(z.ne)], axis=0)
    one, two = both[:, 0 : z.wide], both[:, z.wide : 2 * z.wide]
    n = 8 + z.ne
    one = jnp.concatenate([one[s * n : (s + 1) * n] for s in range(z.pieces)], axis=1)
    two = jnp.concatenate([two[s * 8 : (s + 1) * 8] for s in range(z.pieces)], axis=1)
    n1[...], n2[...], n3[...], n4[...] = two[0:1], two[1:2], one[0:1], one[1:2]
    router_ref[...] = one[8:n]


def expert_grads_body(z, parts, who, *refs):
    one, two, (first_ref, second_ref) = refs[:parts], refs[parts : 2 * parts], refs[2 * parts :]
    first_ref[...] = sum(p[...].astype(F32) for p in one)
    second_ref[...] = sum(p[...].astype(F32) for p in two).T


def finish_body(z, parts, who, resid_ref, *refs):
    out_ref, xp = refs[parts], refs[parts + 1]
    total = refs[0][...].astype(F32)
    for p in refs[1:parts]:
        total = total + p[...].astype(F32)
    xp[...] = resid_ref[...] + total
    for i in range(z.images):
        out_ref[i * IMAGE_TOKENS : (i + 1) * IMAGE_TOKENS, :] = xp[
            i * z.lp : i * z.lp + IMAGE_TOKENS, :
        ]


def swap(value, axis, bit):
    n = lax.axis_size(axis)
    return lax.ppermute(value, axis, [(k, k ^ bit) for k in range(n)])


def gather_far(own, axis):
    blocks = [own]
    for bit in halving_bits(lax.axis_size(axis))[1:]:
        blocks += [swap(v, axis, bit) for v in blocks]
    return blocks


def gather_near(blocks, axis):
    return [v for b in blocks for v in (b, swap(b, axis, 1))]


def gather_blocks(own, axis, late=None):
    blocks = gather_far(own, axis)
    if late is not None:
        blocks = blocks[:1] + hold(blocks[1:], late)
    return gather_near(blocks, axis)


def scatter_step(left, axis, bit):
    left = {r: list(parts) for r, parts in left.items()}
    for r in sorted(left, reverse=True):
        if r & bit:
            left[r ^ bit].append(swap(total_low(left.pop(r)), axis, bit))
    return left


def scatter_near(blocks, axis):
    left = {r: [b] for r, b in enumerate(blocks)}
    left = scatter_step(left, axis, 1)
    far = {r: [total_low(parts)] for r, parts in left.items() if r}
    return {**left, **far}


def hold_far(left, after):
    far = [r for r in left if r]
    held = hold([left[r][0] for r in far], after)
    return {0: left[0], **{r: [v] for r, v in zip(far, held)}}


def scatter_far(left, axis):
    for bit in halving_bits(lax.axis_size(axis))[1:]:
        left = scatter_step(left, axis, bit)
    return left[0]


def scatter_sum(blocks, axis):
    return scatter_far(scatter_near(blocks, axis), axis)


def total_low(parts):
    if len(parts) == 1:
        return parts[0]
    return total(parts).astype(BF16)


def total(parts):
    out = parts[0].astype(F32)
    for p in parts[1:]:
        out = out + p.astype(F32)
    return out


def split_last(values):
    return values[:-1], values[-1]


def send_pairs(pairs, first, axis):
    return [v if first + k == 0 else swap(v, axis, 2 * (first + k)) for k, v in enumerate(pairs)]


def pass_on(direct, axis):
    blk = direct[0].shape[0] // 2
    return swap(jnp.concatenate([v[blk:] for v in direct], axis=0), axis, 1)


def scatter_xy(left):
    bits = halving_bits(lax.axis_size("tensor"))
    for bit in bits[2:]:
        left = scatter_step(left, "tensor", bit)
    own, other = total_low(left[0]), total_low(left[2])
    half = own.shape[0] // 2
    nt, ne = lax.axis_size("tensor"), lax.axis_size("expert")
    both = [(e * nt + t, (e ^ 1) * nt + (t ^ 2)) for e in range(ne) for t in range(nt)]
    return [
        own[:half],
        lax.ppermute(other[half:], ("expert", "tensor"), both),
        swap(own[half:], "expert", 1),
        swap(other[:half], "tensor", 2),
    ]


def places(bits):
    n = 1 << len(bits)
    return [sum(b for k, b in enumerate(bits) if p & (n >> (k + 1))) for p in range(n)]


def exchange_sum(value, axis, bits):
    offsets = places(bits)
    step = value.shape[0] // len(offsets)
    parts = [value[p * step : (p + 1) * step] for p in range(len(offsets))]
    return total_low([parts[0]] + [swap(v, axis, o) for v, o in zip(parts[1:], offsets[1:])])


def exchange_all(value, axis, bits):
    return jnp.concatenate([value] + [swap(value, axis, o) for o in places(bits)[1:]], 0)


def sum_rest(value, axis):
    bits = halving_bits(lax.axis_size(axis))
    groups = [bits[k : k + 2] for k in range(1, len(bits), 2)]
    for group in groups:
        value = exchange_sum(value, axis, group)
    for group in groups[::-1]:
        value = exchange_all(value, axis, group)
    return value, swap(value, axis, bits[0])


def shards(
    block_in,
    out_grad,
    routes,
    kept_pairs,
    ln1_gain,
    ln1_bias,
    w_query,
    w_key,
    w_value,
    w_attn_out,
    ln2_gain,
    ln2_bias,
    w_router,
    w_expert_in,
    w_expert_out,
):
    nt, ne = lax.axis_size("tensor"), lax.axis_size("expert")
    width = block_in.shape[1]
    z = Sizes(
        nt, ne, width, block_in.shape[0], routes.shape[0], w_query.shape[1], w_expert_in.shape[2]
    )
    lp, hw, hid, blk = z.lp, z.hw, z.hid, z.blk
    me_t, me_e = lax.axis_index("tensor"), lax.axis_index("expert")
    who = jnp.stack([me_t, me_e]).astype(I32)
    body = functools.partial

    rows_low = shape((z.rows, width), BF16)
    pair = shape((2 * blk, width), BF16)
    quarter, half = ne // 4, ne // 2

    attn_own = call(
        body(first_body, z),
        shape((width, 4 * hw), BF16),
        [who, *map(Far, (w_query, w_key, w_value, w_attn_out))],
    )
    attn_w = gather_blocks(attn_own, "tensor")
    lines = jnp.pad(
        jnp.stack([routes.T, kept_pairs.T]).reshape(2, 2, z.chunks, IMAGE_TOKENS),
        ((0, 0), (0, 0), (0, 0), (0, lp - IMAGE_TOKENS)),
        constant_values=-1,
    )
    dy_low, expert_own, pos, keep, post = call(
        body(early_body, z),
        [
            rows_low,
            shape((2 * width, hid), BF16),
            shape((z.chunks, ne, lp), I32),
            shape((z.chunks, ne, lp), F32),
            shape((z.chunks, lp, ne), I32),
        ],
        [
            who,
            *map(Far, (out_grad, w_expert_in[0], w_expert_out[0])),
            lines[0],
            lines[1].astype(F32),
        ],
        [pltpu.VMEM((z.rows, width), F32)],
        after=[attn_own],
    )
    dy_low = hold([dy_low], [attn_w[nt // 2]])[0]
    dy_part = gather_far(dy_low, "tensor")

    norms = jnp.stack([ln1_gain, ln1_bias, ln2_gain, ln2_bias])
    wr = w_router.T
    second, resid, h1, *rest = call(
        body(attend_body, z),
        [
            rows_low,
            shape((z.rows, width), F32),
            rows_low,
            *[shape((z.rows, 3 * hw), BF16)] * nt,
            *[shape((z.rows, hw), BF16)] * nt,
            *[shape((z.images * z.hpb, lp, lp), BF16)] * nt,
        ],
        [who, Far(block_in), norms, Far(wr), *attn_w],
        [
            pltpu.VMEM((z.rows, width), F32),
            pltpu.VMEM((lp, width), F32),
            pltpu.VMEM((ne, width), F32),
        ],
    )
    qkv, ctx, probs = rest[:nt], rest[nt : 2 * nt], rest[2 * nt :]
    second, *rest = hold([second, *dy_part[1:]], [])
    dy_rows = gather_near([dy_part[0], *rest], "tensor")
    rows_part = gather_far(second, "tensor")
    rows = gather_near(rows_part, "tensor")
    sent = call(
        body(dispatch_body, z),
        [shape((4 * blk, width), BF16)] * quarter + [pair] * half,
        [who, pos, keep, *rows, *dy_rows],
        [
            pltpu.VMEM((z.slots, width), F32),
            pltpu.VMEM((z.slots, width), F32),
            pltpu.VMEM((2 * ne, z.slots), F32),
        ],
    )
    near_in = send_pairs(sent[:quarter], 0, "expert")
    far_in = [swap(v, "expert", half + k) for k, v in enumerate(sent[quarter:])]
    expert_own = hold([expert_own], rows_part[1:])[0]
    w_part = gather_far(expert_own, "tensor")
    near_in = near_in[:1] + hold(near_in[1:], far_in)
    near_in.append(pass_on(near_in, "expert"))
    own_core, *rest = hold([swap(w_part[0], "tensor", 1), *w_part[1:]], sent[:1])
    expert_w = [w_part[0], own_core, *gather_near(rest, "tensor")]

    size = half * blk
    passed = [
        *[shape((size, hid), BF16)] * (2 * nt),
        shape((size, width), BF16),
        shape((1, 128), F32),
    ]
    held = [
        pltpu.VMEM((size, width), BF16),
        pltpu.VMEM((size, 128), F32),
        pltpu.VMEM((size, width), F32),
        pltpu.VMEM((size, width), F32),
    ]
    far = call(
        body(expert_body, z, False, half),
        [pair] * half + passed,
        [who, *far_in, *expert_w],
        held,
    )
    far_out, far_mixed, (*far_hidden, far_g, far_top) = far[:quarter], far[quarter:half], far[half:]
    near = call(
        body(expert_body, z, True, half),
        [pair] * half + passed,
        [who, *near_in, *expert_w, far_top],
        held,
    )
    near_out, near_mixed, (*near_hidden, near_g, tops) = near[:quarter], near[quarter:half], near[half:]
    far_out = send_pairs(far_out, quarter, "expert")
    near_out = send_pairs(near_out, 0, "expert")
    expert_grads = call(
        body(expert_weights_body, z),
        [shape((width, hid), BF16)] * (2 * nt),
        [who, *near_in, *far_in, near_g, far_g, *near_hidden, *far_hidden],
        [pltpu.VMEM((2, width, size), BF16), pltpu.VMEM((2, width, size), BF16)],
    )
    far_out = hold(far_out, expert_grads[:1])
    far_out.append(pass_on(far_out, "expert"))
    near_out = near_out[:1] + hold(near_out[1:], expert_grads[:1])
    near_out.append(pass_on(near_out, "expert"))
    first_parts = scatter_sum(expert_grads[:nt], "tensor")
    second_near = scatter_near(expert_grads[nt:], "tensor")

    partial = call(
        body(combine_body, z, True),
        [rows_low] * nt + [shape((ne, width), F32)],
        [who, post, keep, Far(wr), *rows, *near_out, *far_out],
        [pltpu.VMEM((z.slots, width), BF16)],
    )
    router_part = partial[nt]
    dz_near = scatter_near(partial[:nt], "tensor")
    first_parts[1:] = hold(first_parts[1:], partial[nt:])
    second_near[0][1:] = hold(second_near[0][1:], partial[nt:])
    dz_parts = scatter_far(dz_near, "tensor")
    mixed = send_pairs([*near_mixed, *far_mixed], 0, "expert")
    second_parts = scatter_far(hold_far(second_near, dz_parts[-1:]), "tensor")

    pay = shape((ne, z.prow, z.wide), BF16)
    buffers = [pltpu.VMEM((ne, z.crow, z.wide), F32), pltpu.VMEM((ne, 8, z.wide), F32)]
    per_head = shape((z.rows, hw), BF16)
    outs = call(
        body(back_one_body, z, len(dz_parts)),
        [shape((z.rows, width), F32)] + [per_head] * (2 * nt) + [pay] * nt,
        [who, Far(out_grad), norms, resid, router_part, h1, *dz_parts, *attn_w, *probs, *ctx],
        [pltpu.VMEM((z.rows, width), F32), pltpu.VMEM((8 + ne, width), F32), *buffers],
    )
    dresid, dctx, dv = outs[0], outs[1:][:nt], outs[1 + nt :][:nt]
    one_near = scatter_near(outs[1 + 2 * nt :], "tensor")
    mixed = mixed[:1] + hold(mixed[1:], dctx[:1])
    passed = pass_on(mixed, "expert")
    outs = call(
        body(back_two_body, z),
        [Far(shape((z.tok_dev, width), F32))] + [pay] * nt,
        [who, Far(block_in), norms, h1, *qkv, *dctx, *probs, *dv, dresid, *attn_w],
        [pltpu.VMEM((z.rows, width), F32), pltpu.VMEM((8, width), F32), *buffers],
        after=[one_near[nt // 2][0]],
    )
    input_grad = outs[0]
    passed = hold([passed], outs[1:2])[0]
    one_parts = scatter_far(one_near, "tensor")
    one = total_low(one_parts)
    one = total_low([one[:half], swap(one[half:], "expert", 1)])
    two = hold(outs[1:], [one_parts[-1], second_parts[-1]])
    two_near = scatter_near(two, "tensor")
    two_parts = scatter_xy(two_near)

    mixed_part = call(
        body(combine_body, z, False),
        [rows_low] * nt,
        [who, post, *mixed, passed],
        [pltpu.VMEM((z.slots, width), BF16)],
        after=[two_near[nt // 2][0]],
    )
    mixed_part = hold(mixed_part, [two_parts[-1]])
    mixed_parts = scatter_sum(mixed_part, "tensor")
    grad_first, grad_second = call(
        body(expert_grads_body, z, len(first_parts)),
        [Far(shape((width, hid), F32)), Far(shape((hid, width), F32))],
        [who, *first_parts, *second_parts],
    )
    block_out = call(
        body(finish_body, z, len(mixed_parts)),
        Far(shape((z.tok_dev, width), F32)),
        [who, resid, *mixed_parts],
        [pltpu.VMEM((z.rows, width), F32)],
    )
    merged = jnp.concatenate([one, total_low(two_parts)], axis=2)
    sums = sum_rest(hold([merged], mixed_part[:1])[0], "expert")

    head = Far(shape((width, hw), F32))
    grad_q, grad_k, grad_v, grad_o, n1, n2, n3, n4, router_grad = call(
        body(last_body, z),
        [head] * 3
        + [Far(shape(v, F32)) for v in ((hw, width), *[(1, width)] * 4, (ne, width))],
        [who, *sums],
        [pltpu.VMEM((ne, z.crow, 2 * z.wide), F32), pltpu.VMEM((ne, 8, 2 * z.wide), F32)],
    )
    head_maxima = lax.dynamic_slice_in_dim(tops[0], me_t * z.hpb, z.hpb, 0)
    factor = jnp.repeat(jnp.sqrt(jnp.minimum(1.0, clip_limit / head_maxima)), HEAD_DIM)
    return (
        block_out,
        input_grad,
        n1[0],
        n2[0],
        grad_q,
        grad_k,
        grad_v,
        grad_o,
        n3[0],
        n4[0],
        router_grad.T,
        grad_first[None],
        grad_second[None],
        head_maxima,
        w_query * factor[None, :],
        w_key * factor[None, :],
    )


def solution(mesh):
    placed = (
        P(("expert", "tensor"), None),
        P(("expert", "tensor"), None),
        P("expert", None),
        P("expert", None),
        P(),
        P(),
        P(None, "tensor"),
        P(None, "tensor"),
        P(None, "tensor"),
        P("tensor", None),
        P(),
        P(),
        P(),
        P("expert", None, "tensor"),
        P("expert", "tensor", None),
    )
    return jax.shard_map(
        shards,
        mesh=mesh,
        in_specs=placed,
        out_specs=(
            P(("expert", "tensor"), None),
            P(("expert", "tensor"), None),
            P(),
            P(),
            P(None, "tensor"),
            P(None, "tensor"),
            P(None, "tensor"),
            P("tensor", None),
            P(),
            P(),
            P(),
            P("expert", None, "tensor"),
            P("expert", "tensor", None),
            P("tensor"),
            P(None, "tensor"),
            P(None, "tensor"),
        ),
        check_vma=False,
    )
```

```python
import functools

import jax
import jax.numpy as jnp
from jax import lax
from jax.experimental import pallas as pl
from jax.experimental.pallas import tpu as pltpu
from jax.sharding import PartitionSpec as P

HEAD_DIM = 64
IMAGE_TOKENS = 197
SPARE = 200
TOP_ROW = 197

F32 = jnp.float32
BF16 = jnp.bfloat16
I32 = jnp.int32

clip_limit = 4.0
norm_eps = 1e-06
low_value = -1e30


def round_up(value, unit):
    return -(-value // unit) * unit


def dot_nn(a, b):
    return lax.dot_general(a, b, (((1,), (0,)), ((), ())), preferred_element_type=F32)


def dot_nt(a, b):
    return lax.dot_general(a, b, (((1,), (1,)), ((), ())), preferred_element_type=F32)


def dot_tn(a, b):
    return lax.dot_general(a, b, (((0,), (0,)), ((), ())), preferred_element_type=F32)


def iota(shape, dim):
    return lax.broadcasted_iota(I32, shape, dim)


def split2(v):
    high = v.astype(BF16).astype(F32)
    return high, (v - high).astype(BF16).astype(F32)


def normalize(rows):
    center = jnp.mean(rows, axis=-1, keepdims=True)
    offset = rows - center
    rstd = lax.rsqrt(jnp.mean(offset * offset, axis=-1, keepdims=True) + norm_eps)
    return offset * rstd, rstd


def norm_back(grad, unit, rstd):
    return rstd * (
        grad
        - jnp.mean(grad, axis=-1, keepdims=True)
        - unit * jnp.mean(grad * unit, axis=-1, keepdims=True)
    )


def halving_bits(n):
    return [1 << k for k in range(n.bit_length() - 1)]


class Sizes:
    def __init__(self, nt, ne, width, tok_dev, tok_group, head_cols, hidden):
        self.nt, self.ne, self.width = nt, ne, width
        self.tok_dev = tok_dev
        self.images = tok_dev // IMAGE_TOKENS
        self.lp = round_up(SPARE + ne, 16)
        self.rows = self.images * self.lp
        self.chunks = nt * self.images
        self.cap = 5 * tok_group // (2 * ne) + 1
        self.spr = -(-self.cap // nt)
        need = self.spr + 2
        self.blk = next((b for b in (16, 32, 64, 128) if b >= need), round_up(need, 128))
        self.epl = 128 // self.blk
        self.hw = head_cols
        self.hpb = head_cols // HEAD_DIM
        self.hid = hidden
        self.slots = ne * self.blk
        self.wide = 2 * self.hw
        self.pieces = width // self.wide
        self.crow = width // ne
        self.prow = self.crow + 8
        bits = halving_bits(ne)
        self.offset = places(bits)


SM = pl.BlockSpec(memory_space=pltpu.SMEM)
VM = pl.BlockSpec(memory_space=pltpu.VMEM)
ANY = pl.BlockSpec(memory_space=pl.ANY)


class Far:
    def __init__(self, value):
        self.value = value


class Given:
    def __init__(self, ref, copy):
        self.ref, self.copy = ref, copy
        copy.start()

    def wait(self):
        if self.copy is not None:
            self.copy.wait()
            self.copy = None

    def __getitem__(self, at):
        self.wait()
        return self.ref[at]


def place(value, space):
    return pltpu.with_memory_space_constraint(value, space)


def call(body, outs, args, scratch=(), after=()):
    skip = len(after)
    keep = lax.axis_size("tensor") <= 4
    vmem = 12 if keep else 60
    single = not isinstance(outs, list)
    flat = [outs] if single else outs
    far = [k for k, a in enumerate(args) if isinstance(a, Far)]

    def run(*refs):
        ins, refs = [refs[0], *refs[1 + skip : skip + len(args)]], refs[skip + len(args) :]
        results, refs = refs[: len(flat)], refs[len(flat) :]
        own, refs = refs[: len(scratch)], refs[len(scratch) :]
        for n, k in enumerate(far):
            ins[k] = Given(refs[n], pltpu.make_async_copy(ins[k], refs[n], refs[-1].at[n]))
        body(*ins, *results, *own)
        for k in far:
            ins[k].wait()

    extra = [pltpu.VMEM(args[k].value.shape, args[k].value.dtype) for k in far]
    if far:
        extra.append(pltpu.SemaphoreType.DMA((len(far),)))
    got = pl.pallas_call(
        run,
        out_shape=[
            o.value if isinstance(o, Far) else pltpu.VMEM(o.shape, o.dtype) if keep else o
            for o in flat
        ],
        in_specs=[SM] + [ANY] * skip + [ANY if k in far else VM for k in range(1, len(args))],
        out_specs=[VM] * len(flat),
        scratch_shapes=[*scratch, *extra],
        compiler_params=pltpu.CompilerParams(vmem_limit_bytes=vmem * 1024 * 1024),
    )(
        args[0],
        *after,
        *[
            place(a.value, pltpu.HBM) if isinstance(a, Far) else place(a, pltpu.VMEM) if keep else a
            for a in args[1:]
        ],
    )
    return got[0] if single else list(got)


def hold(values, after):
    n, m = len(values), len(after)

    def run(*refs):
        pass

    out = pl.pallas_call(
        run,
        out_shape=[shape(v.shape, v.dtype) for v in values],
        in_specs=[ANY] * (n + m),
        out_specs=[ANY] * n,
        input_output_aliases={k: k for k in range(n)},
        compiler_params=pltpu.CompilerParams(vmem_limit_bytes=1024 * 1024),
    )(*values, *after)
    return list(out)


def shape(dims, kind):
    return jax.ShapeDtypeStruct(dims, kind)


def first_body(z, who, dy_ref, q_ref, k_ref, v_ref, o_ref, low_ref, out_ref, pad):
    hw = z.hw
    pad[...] = jnp.zeros(pad.shape, F32)
    for i in range(z.images):
        pad[i * z.lp : i * z.lp + IMAGE_TOKENS, :] = dy_ref[
            i * IMAGE_TOKENS : (i + 1) * IMAGE_TOKENS, :
        ]
    low_ref[...] = pad[...].astype(BF16)
    for n, ref in enumerate((q_ref, k_ref, v_ref)):
        out_ref[:, n * hw : (n + 1) * hw] = ref[...].astype(BF16)
    out_ref[:, 3 * hw : 4 * hw] = o_ref[...].T.astype(BF16)


def early_body(z, who, in_ref, out_ref, route_ref, kept_ref, *refs):
    w_ref, pos_ref, keep_ref, post_ref = refs
    w_ref[0 : z.width, :] = in_ref[...].astype(BF16)
    w_ref[z.width : 2 * z.width, :] = out_ref[...].T.astype(BF16)
    me_t, me_e = who[0], who[1]
    named = jnp.bitwise_xor(iota((z.ne, z.lp), 0), me_e)
    before = jnp.where(iota((z.lp, z.lp), 0) < iota((z.lp, z.lp), 1), 1.0, 0.0).astype(BF16)
    count = jnp.zeros((z.ne, 1), F32)
    for c in range(z.chunks):
        block, img = c // z.images, c % z.images
        first = route_ref[0, c : c + 1, :] == named
        other = route_ref[1, c : c + 1, :] == named
        hit = jnp.where(first | other, 1.0, 0.0)
        place = dot_nn(hit.astype(BF16), before) + count
        count = count + jnp.sum(hit, axis=1, keepdims=True)
        at = jnp.bitwise_xor(block, me_t) * z.images + img
        place = jnp.where(hit > 0, place, -1.0)
        pos_ref[at] = place.astype(I32)
        post_ref[at] = place.T.astype(I32)
        keep_ref[at] = jnp.where(first, kept_ref[0, c : c + 1, :], 0.0) + jnp.where(
            other, kept_ref[1, c : c + 1, :], 0.0
        )


def attend_body(z, who, x_ref, ln_ref, wr_ref, *refs):
    nt, lp, hw = z.nt, z.lp, z.hw
    weights = refs[:nt]
    z_refs, refs = refs[nt : nt + z.images], refs[nt + z.images :]
    resid_ref, h1_ref, refs = refs[0], refs[1], refs[2:]
    qkv_ref, ctx_ref, p_ref = refs[:nt], refs[nt : 2 * nt], refs[2 * nt : 3 * nt]
    xp, zb, pt = refs[3 * nt :]
    me_t = who[0]
    xp[...] = jnp.zeros(xp.shape, F32)
    for i in range(z.images):
        xp[i * lp : i * lp + IMAGE_TOKENS, :] = x_ref[
            i * IMAGE_TOKENS : (i + 1) * IMAGE_TOKENS, :
        ]
    unit, _ = normalize(xp[...])
    h1 = (unit * ln_ref[0:1, :] + ln_ref[1:2, :]).astype(BF16)
    h1_ref[...] = h1
    head_of = iota((lp, hw), 1) // HEAD_DIM
    real = iota((lp, lp), 1) < IMAGE_TOKENS
    real_row = iota((lp, 1), 0) < IMAGE_TOKENS
    lane = iota((1, 128), 1)
    tops = jnp.full((1, 128), low_value, F32)
    attn = jnp.zeros((z.rows, z.width), F32)
    for r in range(nt):
        qkv = dot_nn(h1, weights[r][:, 0 : 3 * hw]).astype(BF16)
        qkv_ref[r][...] = qkv
        ctxs = []
        for i in range(z.images):
            at = slice(i * lp, (i + 1) * lp)
            q, k, v = (qkv[at, n * hw : (n + 1) * hw] for n in range(3))
            ctx = jnp.zeros((lp, hw), F32)
            for j in range(z.hpb):
                mine = head_of == j
                s = dot_nt(jnp.where(mine, q, jnp.zeros_like(q)), k) * (HEAD_DIM**-0.5)
                s = jnp.where(real, s, low_value)
                peak = jnp.max(s, axis=1, keepdims=True)
                top = jnp.max(jnp.where(real_row, peak, low_value), axis=0, keepdims=True)
                head = jnp.bitwise_xor(me_t, r) * z.hpb + j
                tops = jnp.where(lane == head, jnp.maximum(tops, top), tops)
                e = jnp.exp(s - peak)
                p = (e * (1.0 / jnp.sum(e, axis=1, keepdims=True))).astype(BF16)
                p_ref[r][i * z.hpb + j] = p
                ctx = jnp.where(mine, dot_nn(p, v), ctx)
            ctxs.append(ctx.astype(BF16))
        ctx = jnp.concatenate(ctxs, axis=0)
        ctx_ref[r][...] = ctx
        attn = attn + dot_nt(ctx, weights[r][:, 3 * hw : 4 * hw])
    resid = xp[...] + attn
    resid_ref[...] = resid
    unit, _ = normalize(resid)
    second = unit * ln_ref[2:3, :] + ln_ref[3:4, :]
    w_hi, w_lo = (v.astype(BF16) for v in split2(router_rows(z, who, wr_ref)))
    row = iota((lp, 1), 0)
    t_hi = tops.astype(BF16).astype(F32)
    t_mid = (tops - t_hi).astype(BF16).astype(F32)
    t_lo = tops - t_hi - t_mid
    for i in range(z.images):
        part = second[i * lp : (i + 1) * lp]
        s_hi, s_lo = (v.astype(BF16) for v in split2(part))
        logits = dot_nt(w_hi, s_hi) + (dot_nt(w_hi, s_lo) + dot_nt(w_lo, s_hi))
        e = jnp.exp(logits - jnp.max(logits, axis=0, keepdims=True))
        p_hi, p_lo = split2(e / jnp.sum(e, axis=0, keepdims=True))
        pt[...] = jnp.zeros(pt.shape, F32)
        pt[:, 0:lp] = p_hi
        pt[:, 256 : 256 + lp] = p_lo
        zb[...] = jnp.where(row < IMAGE_TOKENS, part, 0.0)
        for n, t in enumerate((t_hi, t_mid, t_lo)):
            zb[TOP_ROW + n : TOP_ROW + n + 1, 0:128] = t
        zb[SPARE : SPARE + z.ne, :] = pt[...]
        z_refs[i][...] = zb[...].astype(BF16)


def router_rows(z, who, ref):
    return jnp.concatenate(
        [ref[pl.ds(jnp.bitwise_xor(e, who[1]), 1), :] for e in range(z.ne)], axis=0
    )


def split_at(n, values):
    return values[:n], values[n:]


def tail_rows(z, ref):
    start = (TOP_ROW // 16) * 16
    return ref[start : z.lp, :].astype(F32), start


def probs_of(z, ref):
    tail, start = tail_rows(z, ref)
    both = tail[SPARE - start : SPARE - start + z.ne]
    return both[:, 0 : z.lp] + both[:, 256 : 256 + z.lp]


def hot_rows(z, who, pos_ref, c, first, last):
    slot = iota((z.blk, z.lp), 0)
    slot = jnp.where(slot < z.spr, slot + who[0] * z.spr, -2)
    return jnp.concatenate(
        [
            jnp.where(pos_ref[c, e : e + 1, :] == slot, 1.0, 0.0).astype(BF16)
            for e in range(first, last)
        ],
        axis=0,
    )


def dispatch_dy_body(z, who, pos_ref, *refs):
    nt, ne, lp, blk = z.nt, z.ne, z.lp, z.blk
    rows, outs, acc = refs[:nt], refs[nt : nt + ne // 4], refs[nt + ne // 4]
    for c in range(z.chunks):
        r, i = c // z.images, c % z.images
        hot = hot_rows(z, who, pos_ref, c, ne // 2, ne)
        part = dot_nn(hot, rows[r][i * lp : (i + 1) * lp, :])
        acc[...] = part if c == 0 else acc[...] + part
    for k in range(ne // 4):
        outs[k][...] = acc[2 * k * blk : 2 * (k + 1) * blk, :].astype(BF16)


def dispatch_body(z, who, pos_ref, keep_ref, *refs):
    nt, ne, lp, blk = z.nt, z.ne, z.lp, z.blk
    rows, dy_rows, refs = refs[: z.chunks], refs[z.chunks :][:nt], refs[z.chunks + nt :]
    outs, (acc, dy_acc, gacc) = refs[:ne], refs[ne:]
    half = ne // 2
    tops = None
    for c in range(z.chunks):
        r, i = c // z.images, c % z.images
        hot = hot_rows(z, who, pos_ref, c, 0, ne)
        part = dot_nn(hot[: half * blk], dy_rows[r][i * lp : (i + 1) * lp, :])
        dy_acc[...] = part if c == 0 else dy_acc[...] + part
        part = dot_nn(hot, rows[c][...])
        acc[...] = part if c == 0 else acc[...] + part
        g_hi, g_lo = split2(probs_of(z, rows[c]) * keep_ref[c])
        both = jnp.concatenate([g_hi, g_lo], axis=0).astype(BF16)
        part = dot_nt(both, hot)
        gacc[...] = part if c == 0 else gacc[...] + part
        if i == 0:
            tail, start = tail_rows(z, rows[c])
            three = tail[TOP_ROW - start : TOP_ROW - start + 3, 0:128]
            top = three[0:1] + three[1:2] + three[2:3]
            tops = top if tops is None else jnp.maximum(tops, top)
    t_hi = tops.astype(BF16).astype(F32)
    t_mid = (tops - t_hi).astype(BF16).astype(F32)
    t_lo = tops - t_hi - t_mid
    none = jnp.zeros((1, 128), F32)
    top_row = jnp.concatenate([t_hi, t_mid, t_lo, none], axis=1)
    row = iota((blk, 1), 0)
    part_of = iota((1, 128), 1) // blk
    for e in range(ne):
        tile = slice((e // z.epl) * 128, (e // z.epl) * 128 + 128)
        g_hi = jnp.where(part_of == e % z.epl, gacc[e : e + 1, tile], 0.0)
        g_lo = jnp.where(part_of == e % z.epl, gacc[ne + e : ne + e + 1, tile], 0.0)
        gates = jnp.concatenate([g_hi, g_lo, none, none], axis=1)
        block = acc[e * blk : (e + 1) * blk, :]
        block = jnp.where(row == z.spr, gates, block)
        block = jnp.where(row == z.spr + 1, top_row, block)
        outs[e][0:blk, :] = block.astype(BF16)
        if e < half:
            outs[e][blk : 2 * blk, :] = dy_acc[e * blk : (e + 1) * blk, :].astype(BF16)


class Part:
    def __init__(self, ref, first):
        self.ref, self.first = ref, first

    def rows(self, start, stop):
        return self.ref[self.first + start : self.first + stop, :]

    def put(self, value):
        self.ref[self.first : self.first + value.shape[0], :] = value


def blocks_of(z, direct, passed, size=1, at=0):
    out = []
    for k, ref in enumerate(direct):
        out += [Part(ref, at * z.blk), Part(passed, (k * size + at) * z.blk)]
    return out


def spare_pair(z, part):
    start = (z.spr // 16) * 16
    tail = part.rows(start, z.blk).astype(F32)
    return tail[z.spr - start : z.spr - start + 1], tail[z.spr - start + 1 : z.spr - start + 2]


def expert_body(z, near, count, who, *refs):
    nt, ne, blk, hid, width = z.nt, z.ne, z.blk, z.hid, z.width
    half = count // 2
    rows_in = [Part(ref, 0) for ref in refs[:count]]
    if near:
        dy_in, refs = [Part(ref, blk) for ref in refs[:count]], refs[count:]
    else:
        refs = refs[count:]
        dy_in, refs = blocks_of(z, refs[:half], refs[half]), refs[half + 1 :]
    weights, refs = refs[:nt], refs[nt:]
    w = z.width
    if near:
        far_top, refs = refs[0], refs[1:]
        back, mixed = ([Part(ref, at * blk) for ref in refs[:count]] for at in range(2))
        refs = refs[count:]
    else:
        back, mixed = (
            [Part(ref, at * blk) for ref in some for at in range(2)]
            for some in (refs[:half], refs[half:count])
        )
        refs = refs[count:]
    act, du, refs = refs[:nt], refs[nt : 2 * nt], refs[2 * nt :]
    g, top_ref, rows, gate, o_acc, d_acc = refs
    real = iota((blk, 1), 0) < z.spr
    diag = iota((blk, 128), 0) == iota((blk, 128), 1) % blk
    tops = far_top[...] if near else None
    for n in range(count):
        at = slice(n * blk, (n + 1) * blk)
        rows[at, :] = jnp.where(real, rows_in[n].rows(0, blk), jnp.zeros((), BF16))
        gates, top = spare_pair(z, rows_in[n])
        top = top[:, 0:128] + top[:, 128:256] + top[:, 256:384]
        tops = top if tops is None else jnp.maximum(tops, top)
        line = gates[:, 0:128] + gates[:, 128:256]
        column = jnp.sum(jnp.where(diag, line, 0.0), axis=1, keepdims=True)
        gate[at, :] = jnp.broadcast_to(column, (blk, 128))
    top_ref[...] = tops
    u_first = dot_nn(rows[...], weights[0][0:w, :])
    for n in range(count):
        at = slice(n * blk, (n + 1) * blk)
        g[at, :] = (gate[at, 0:1] * dy_in[n].rows(0, blk).astype(F32)).astype(BF16)
    for r in range(nt):
        u = dot_nn(rows[...], weights[r][0:w, :]) if r else u_first
        second_w = weights[r][w : 2 * w, :]
        cube = 0.7978845608028654 * 0.044715 * u * u
        t = jnp.tanh(u * (0.7978845608028654 + cube))
        h = 0.5 + 0.5 * t
        a = (u * h).astype(BF16)
        slope = h + 2.0 * h * (1.0 - h) * u * (0.7978845608028654 + 3.0 * cube)
        d = (dot_nn(g[...], second_w) * slope).astype(BF16)
        act[r][...] = a
        du[r][...] = d
        o = dot_nt(a, second_w)
        b = dot_nt(d, weights[r][0:w, :])
        o_acc[...] = o if r == 0 else o_acc[...] + o
        d_acc[...] = b if r == 0 else d_acc[...] + b
    row = iota((blk, 1), 0)
    none = jnp.zeros((1, 128), F32)
    for n in range(count):
        at = slice(n * blk, (n + 1) * blk)
        o = o_acc[at, :]
        dgate = jnp.sum(o * dy_in[n].rows(0, blk).astype(F32), axis=1, keepdims=True)
        line = jnp.sum(jnp.where(diag, dgate, 0.0), axis=0, keepdims=True)
        hi, lo = split2(line)
        line = jnp.concatenate([hi, lo, none, none], axis=1)
        back[n].put(jnp.where(row == z.spr, line, d_acc[at, :]).astype(BF16))
        mixed[n].put((gate[at, 0:1] * o).astype(BF16))


def expert_weights_body(z, who, *refs):
    nt, ne, blk, hid = z.nt, z.ne, z.blk, z.hid
    rows_in, refs = [Part(ref, 0) for ref in refs[:ne]], refs[ne:]
    g, refs = refs[:2], refs[2:]
    act, du = (refs[:nt], refs[2 * nt : 3 * nt]), (refs[nt : 2 * nt], refs[3 * nt : 4 * nt])
    one, two, (rows_t, g_t) = refs[4 * nt : 5 * nt], refs[5 * nt : 6 * nt], refs[6 * nt :]
    real = iota((blk, 1), 0) < z.spr
    rows = [jnp.where(real, part.rows(0, blk), jnp.zeros((), BF16)) for part in rows_in]
    half = ne // 2
    for k in range(2):
        rows_t[k] = jnp.concatenate(rows[k * half : (k + 1) * half], axis=0).T
        g_t[k] = g[k][...].T
    for r in range(nt):
        first = dot_nn(rows_t[0], du[0][r][...]) + dot_nn(rows_t[1], du[1][r][...])
        one[r][...] = first.astype(BF16)
        second = dot_nn(g_t[0], act[0][r][...]) + dot_nn(g_t[1], act[1][r][...])
        two[r][...] = second.astype(BF16)


def hot_columns(z, post_ref, c, base):
    lane = iota((z.lp, 128), 1)
    slot = lane % z.blk
    slot = jnp.where(slot < z.spr, slot + base, -2)
    tiles = []
    for p in range(z.ne // z.epl):
        column = post_ref[c, :, p * z.epl : p * z.epl + 1]
        pick = jnp.broadcast_to(column, (z.lp, 128))
        for n in range(1, z.epl):
            e = p * z.epl + n
            pick = jnp.where(lane // z.blk == n, post_ref[c, :, e : e + 1], pick)
        tiles.append(jnp.where(pick == slot, 1.0, 0.0).astype(BF16))
    return jnp.concatenate(tiles, axis=1)


def combine_body(z, with_router, who, post_ref, *refs):
    nt, ne, lp, blk = z.nt, z.ne, z.lp, z.blk
    base = who[0] * z.spr
    if with_router:
        keep_ref, wr_ref = refs[:2]
        rows, refs = refs[2 : 2 + z.chunks], refs[2 + z.chunks :]
    quarter = ne // 4
    at = 0 if with_router else blk
    blocks, refs = [Part(ref, at) for ref in refs[: ne // 2]], refs[ne // 2 :]
    blocks, refs = blocks + blocks_of(z, refs[:quarter], refs[quarter]), refs[quarter + 1 :]
    outs, refs = refs[:nt], refs[nt:]
    if with_router:
        gr_ref, refs = refs[0], refs[1:]
    stack = refs[0]
    for e in range(ne):
        stack[e * blk : (e + 1) * blk, :] = blocks[e].rows(0, blk)
    if with_router:
        row = iota((ne, 128), 0)
        half = iota((ne, 128), 1) // blk
        tiles = []
        for p in range(ne // z.epl):
            hi = jnp.zeros((ne, 128), F32)
            lo = jnp.zeros((ne, 128), F32)
            for n in range(z.epl):
                e = p * z.epl + n
                line, _ = spare_pair(z, blocks[e])
                own = (row == e) & (half == n)
                hi = jnp.where(own, line[:, 0:128], hi)
                lo = jnp.where(own, line[:, 128:256], lo)
            tiles.append(jnp.concatenate([hi, lo], axis=0))
        dgate = jnp.concatenate(tiles, axis=1).astype(BF16)
        unit = jnp.where(iota((lp, lp), 0) == iota((lp, lp), 1), 1.0, 0.0).astype(BF16)
        wr = router_rows(z, who, wr_ref).astype(BF16)
        wr = jnp.concatenate([wr, wr], axis=0)
        total = jnp.zeros((2 * ne, z.width), F32)
    for c in range(z.chunks):
        r, i = c // z.images, c % z.images
        at = slice(i * lp, (i + 1) * lp)
        hot = hot_columns(z, post_ref, c, base)
        part = dot_nn(hot, stack[...])
        if with_router:
            both = dot_nt(dgate, hot)
            dp = (both[0:ne] + both[ne : 2 * ne]) * keep_ref[c]
            pr = probs_of(z, rows[c])
            dl = pr * (dp - jnp.sum(pr * dp, axis=0, keepdims=True))
            dl = jnp.concatenate(split2(dl), axis=0).astype(BF16)
            part = part + dot_nn(dot_nt(unit, dl).astype(BF16), wr)
            total = total + dot_nn(dl, rows[c][...])
        outs[r][at, :] = part.astype(BF16)
    if with_router:
        gr_ref[...] = total[0:ne] + total[ne : 2 * ne]


def spread_rows(z, lines):
    n = lines.shape[0] * z.pieces
    rows = [lines[:, s * z.wide : (s + 1) * z.wide] for s in range(z.pieces)]
    return jnp.concatenate(rows + [jnp.zeros((8 * z.ne - n, z.wide), F32)], axis=0)


def write_parts(z, who, ref, wide, lines):
    for p in range(z.ne):
        c = jnp.bitwise_xor(z.offset[p], who[1])
        ref[p] = jnp.concatenate([wide[c], lines[c]], axis=0).astype(BF16)


def back_one_body(z, parts, who, dy_ref, ln_ref, resid_ref, gr_ref, h1_ref, *refs):
    nt, lp, hw = z.nt, z.lp, z.hw
    dz_parts, refs = refs[:parts], refs[parts:]
    weights, p_ref, ctx_ref, refs = refs[:nt], refs[nt : 2 * nt], refs[2 * nt : 3 * nt], refs[3 * nt :]
    dresid_ref, dctx_ref, dv_ref, pays = refs[0], refs[1:][:nt], refs[1 + nt :][:nt], refs[1 + 2 * nt :][:nt]
    dyp, tail, buf, lines = refs[1 + 3 * nt :]
    dyp[...] = jnp.zeros(dyp.shape, F32)
    for i in range(z.images):
        dyp[i * lp : i * lp + IMAGE_TOKENS, :] = dy_ref[
            i * IMAGE_TOKENS : (i + 1) * IMAGE_TOKENS, :
        ]
    dz = dz_parts[0][...].astype(F32)
    for p in dz_parts[1:]:
        dz = dz + p[...].astype(F32)
    unit, rstd = normalize(resid_ref[...])
    dresid = norm_back(dz * ln_ref[2:3, :], unit, rstd) + dyp[...]
    dresid_ref[...] = dresid
    tail[...] = jnp.zeros(tail.shape, F32)
    tail[0:1, :] = jnp.sum(dz * unit, axis=0, keepdims=True)
    tail[1:2, :] = jnp.sum(dz, axis=0, keepdims=True)
    for e in range(z.ne):
        tail[pl.ds(8 + jnp.bitwise_xor(e, who[1]), 1), :] = gr_ref[e : e + 1, :]
    rows = spread_rows(z, tail[...])
    for p in range(z.ne):
        lines[p] = rows[8 * p : 8 * p + 8]
    da = dresid.astype(BF16)
    h1_t = h1_ref[...].T
    da_t = da.T
    head_of = iota((lp, hw), 1) // HEAD_DIM
    for r in range(nt):
        dctx = dot_nn(da, weights[r][:, 3 * hw : 4 * hw]).astype(BF16)
        dctx_ref[r][...] = dctx
        pieces = []
        for i in range(z.images):
            dc = dctx[i * lp : (i + 1) * lp]
            dv = jnp.zeros((lp, hw), F32)
            for j in range(z.hpb):
                p = p_ref[r][i * z.hpb + j]
                dv = jnp.where(head_of == j, dot_tn(p, dc), dv)
            pieces.append(dv.astype(BF16))
        dv = jnp.concatenate(pieces, axis=0)
        dv_ref[r][...] = dv
        dw = jnp.concatenate([dot_nn(h1_t, dv), dot_nn(da_t, ctx_ref[r][...])], axis=1)
        for p in range(z.ne):
            buf[p] = dw[p * z.crow : (p + 1) * z.crow]
        write_parts(z, who, pays[r], buf, lines)


def back_two_body(z, who, x_ref, ln_ref, h1_ref, *refs):
    nt, lp, hw = z.nt, z.lp, z.hw
    qkv_ref, dctx_ref, p_ref, dv_ref, refs = (*(refs[k * nt : (k + 1) * nt] for k in range(4)), refs[4 * nt :])
    dresid_ref, refs = refs[0], refs[1:]
    weights, in_ref, pays, xp, tail, buf, lines = (
        refs[:nt],
        refs[nt],
        refs[nt + 1 : 2 * nt + 1],
        *refs[2 * nt + 1 :],
    )
    xp[...] = jnp.zeros(xp.shape, F32)
    for i in range(z.images):
        xp[i * lp : i * lp + IMAGE_TOKENS, :] = x_ref[
            i * IMAGE_TOKENS : (i + 1) * IMAGE_TOKENS, :
        ]
    unit, rstd = normalize(xp[...])
    h1_t = h1_ref[...].T
    head_of = iota((lp, hw), 1) // HEAD_DIM
    dh = jnp.zeros((z.rows, z.width), F32)
    scale = HEAD_DIM**-0.5
    grads = []
    for r in range(nt):
        pieces = []
        for i in range(z.images):
            at = slice(i * lp, (i + 1) * lp)
            q, k, v = (qkv_ref[r][at, n * hw : (n + 1) * hw] for n in range(3))
            dc = dctx_ref[r][at, :]
            dq = jnp.zeros((lp, hw), F32)
            dk = jnp.zeros((lp, hw), F32)
            for j in range(z.hpb):
                mine = head_of == j
                pf = p_ref[r][i * z.hpb + j].astype(F32)
                dp = dot_nt(jnp.where(mine, dc, jnp.zeros_like(dc)), v)
                w = pf * dp
                ds = (w - pf * jnp.sum(w, axis=1, keepdims=True)).astype(BF16)
                dq = jnp.where(mine, dot_nn(ds, k) * scale, dq)
                dk = jnp.where(mine, dot_tn(ds, q) * scale, dk)
            pieces.append(jnp.concatenate([dq, dk], axis=1).astype(BF16))
        dqk = jnp.concatenate(pieces, axis=0)
        grads.append(dot_nn(h1_t, dqk))
        dh = dh + dot_nt(dqk, weights[r][:, 0 : 2 * hw]) + dot_nt(
            dv_ref[r][...], weights[r][:, 2 * hw : 3 * hw]
        )
    tail[...] = jnp.zeros(tail.shape, F32)
    tail[0:1, :] = jnp.sum(dh * unit, axis=0, keepdims=True)
    tail[1:2, :] = jnp.sum(dh, axis=0, keepdims=True)
    rows = spread_rows(z, tail[...])
    for p in range(z.ne):
        lines[p] = rows[8 * p : 8 * p + 8]
    for r in range(nt):
        for p in range(z.ne):
            buf[p] = grads[r][p * z.crow : (p + 1) * z.crow]
        write_parts(z, who, pays[r], buf, lines)
    xp[...] = dresid_ref[...] + norm_back(dh * ln_ref[0:1, :], unit, rstd)
    for i in range(z.images):
        in_ref[i * IMAGE_TOKENS : (i + 1) * IMAGE_TOKENS, :] = xp[
            i * lp : i * lp + IMAGE_TOKENS, :
        ]


def last_body(z, who, low, high, q_ref, k_ref, v_ref, o_ref, n1, n2, n3, n4, router_ref, wide, lines):
    hw, half = z.hw, z.ne // 2
    for p in range(z.ne):
        c = jnp.bitwise_xor(z.offset[p], who[1])
        both = (low, high)[p // half][p % half].astype(F32)
        wide[c] = both[0 : z.crow]
        lines[c] = both[z.crow : z.prow]
    both = jnp.concatenate([wide[p] for p in range(z.ne)], axis=0)
    v_ref[...] = both[:, 0:hw]
    o_ref[...] = both[:, hw : 2 * hw].T
    q_ref[...] = both[:, 2 * hw : 3 * hw]
    k_ref[...] = both[:, 3 * hw : 4 * hw]
    both = jnp.concatenate([lines[p] for p in range(z.ne)], axis=0)
    one, two = both[:, 0 : z.wide], both[:, z.wide : 2 * z.wide]
    n = 8 + z.ne
    one = jnp.concatenate([one[s * n : (s + 1) * n] for s in range(z.pieces)], axis=1)
    two = jnp.concatenate([two[s * 8 : (s + 1) * 8] for s in range(z.pieces)], axis=1)
    n1[...], n2[...], n3[...], n4[...] = two[0:1], two[1:2], one[0:1], one[1:2]
    router_ref[...] = one[8:n]


def expert_grads_body(z, parts, who, *refs):
    one, two, (first_ref, second_ref) = refs[:parts], refs[parts : 2 * parts], refs[2 * parts :]
    first_ref[...] = sum(p[...].astype(F32) for p in one)
    second_ref[...] = sum(p[...].astype(F32) for p in two).T


def finish_body(z, parts, who, resid_ref, *refs):
    out_ref, xp = refs[parts], refs[parts + 1]
    total = refs[0][...].astype(F32)
    for p in refs[1:parts]:
        total = total + p[...].astype(F32)
    xp[...] = resid_ref[...] + total
    for i in range(z.images):
        out_ref[i * IMAGE_TOKENS : (i + 1) * IMAGE_TOKENS, :] = xp[
            i * z.lp : i * z.lp + IMAGE_TOKENS, :
        ]


def swap(value, axis, bit):
    n = lax.axis_size(axis)
    return lax.ppermute(value, axis, [(k, k ^ bit) for k in range(n)])


def gather_far(own, axis):
    blocks = [own]
    for bit in halving_bits(lax.axis_size(axis))[1:]:
        blocks += [swap(v, axis, bit) for v in blocks]
    return blocks


def gather_near(blocks, axis):
    return [v for b in blocks for v in (b, swap(b, axis, 1))]


def gather_blocks(own, axis, late=None):
    blocks = gather_far(own, axis)
    if late is not None:
        blocks = blocks[:1] + hold(blocks[1:], late)
    return gather_near(blocks, axis)


def scatter_step(left, axis, bit):
    left = {r: list(parts) for r, parts in left.items()}
    for r in sorted(left, reverse=True):
        if r & bit:
            left[r ^ bit].append(swap(total_low(left.pop(r)), axis, bit))
    return left


def scatter_near(blocks, axis):
    left = {r: [b] for r, b in enumerate(blocks)}
    left = scatter_step(left, axis, 1)
    far = {r: [total_low(parts)] for r, parts in left.items() if r}
    return {**left, **far}


def hold_far(left, after):
    far = [r for r in left if r]
    held = hold([left[r][0] for r in far], after)
    return {0: left[0], **{r: [v] for r, v in zip(far, held)}}


def scatter_far(left, axis):
    for bit in halving_bits(lax.axis_size(axis))[1:]:
        left = scatter_step(left, axis, bit)
    return left[0]


def scatter_sum(blocks, axis):
    return scatter_far(scatter_near(blocks, axis), axis)


def total_low(parts):
    if len(parts) == 1:
        return parts[0]
    return total(parts).astype(BF16)


def total(parts):
    out = parts[0].astype(F32)
    for p in parts[1:]:
        out = out + p.astype(F32)
    return out


def split_last(values):
    return values[:-1], values[-1]


def send_pairs(pairs, first, axis):
    return [v if first + k == 0 else swap(v, axis, 2 * (first + k)) for k, v in enumerate(pairs)]


def pass_on(direct, axis):
    blk = direct[0].shape[0] // 2
    return swap(jnp.concatenate([v[blk:] for v in direct], axis=0), axis, 1)


def scatter_xy(left):
    bits = halving_bits(lax.axis_size("tensor"))
    for bit in bits[2:]:
        left = scatter_step(left, "tensor", bit)
    own, other = total_low(left[0]), total_low(left[2])
    half = own.shape[0] // 2
    nt, ne = lax.axis_size("tensor"), lax.axis_size("expert")
    both = [(e * nt + t, (e ^ 1) * nt + (t ^ 2)) for e in range(ne) for t in range(nt)]
    return [
        own[:half],
        lax.ppermute(other[half:], ("expert", "tensor"), both),
        swap(own[half:], "expert", 1),
        swap(other[:half], "tensor", 2),
    ]


def places(bits):
    n = 1 << len(bits)
    return [sum(b for k, b in enumerate(bits) if p & (n >> (k + 1))) for p in range(n)]


def exchange_sum(value, axis, bits):
    offsets = places(bits)
    step = value.shape[0] // len(offsets)
    parts = [value[p * step : (p + 1) * step] for p in range(len(offsets))]
    return total_low([parts[0]] + [swap(v, axis, o) for v, o in zip(parts[1:], offsets[1:])])


def exchange_all(value, axis, bits):
    return jnp.concatenate([value] + [swap(value, axis, o) for o in places(bits)[1:]], 0)


def sum_rest(value, axis):
    bits = halving_bits(lax.axis_size(axis))
    groups = [bits[k : k + 2] for k in range(1, len(bits), 2)]
    for group in groups:
        value = exchange_sum(value, axis, group)
    for group in groups[::-1]:
        value = exchange_all(value, axis, group)
    return value


def shards(
    block_in,
    out_grad,
    routes,
    kept_pairs,
    ln1_gain,
    ln1_bias,
    w_query,
    w_key,
    w_value,
    w_attn_out,
    ln2_gain,
    ln2_bias,
    w_router,
    w_expert_in,
    w_expert_out,
):
    nt, ne = lax.axis_size("tensor"), lax.axis_size("expert")
    width = block_in.shape[1]
    z = Sizes(
        nt, ne, width, block_in.shape[0], routes.shape[0], w_query.shape[1], w_expert_in.shape[2]
    )
    lp, hw, hid, blk = z.lp, z.hw, z.hid, z.blk
    me_t, me_e = lax.axis_index("tensor"), lax.axis_index("expert")
    who = jnp.stack([me_t, me_e]).astype(I32)
    body = functools.partial

    rows_low = shape((z.rows, width), BF16)
    pair = shape((2 * blk, width), BF16)
    quarter, half = ne // 4, ne // 2

    dy_low, attn_own = call(
        body(first_body, z),
        [rows_low, shape((width, 4 * hw), BF16)],
        [who, *map(Far, (out_grad, w_query, w_key, w_value, w_attn_out))],
        [pltpu.VMEM((z.rows, width), F32)],
    )
    dy_part = gather_far(dy_low, "tensor")
    lines = jnp.pad(
        jnp.stack([routes.T, kept_pairs.T]).reshape(2, 2, z.chunks, IMAGE_TOKENS),
        ((0, 0), (0, 0), (0, 0), (0, lp - IMAGE_TOKENS)),
        constant_values=-1,
    )
    expert_own, pos, keep, post = call(
        body(early_body, z),
        [
            shape((2 * width, hid), BF16),
            shape((z.chunks, ne, lp), I32),
            shape((z.chunks, ne, lp), F32),
            shape((z.chunks, lp, ne), I32),
        ],
        [who, Far(w_expert_in[0]), Far(w_expert_out[0]), lines[0], lines[1].astype(F32)],
        after=[dy_low],
    )
    dy_far = hold(dy_part[1:], [pos])
    dy_rows = gather_near([dy_part[0], *dy_far], "tensor")
    attn_part = gather_far(hold([attn_own], dy_far)[0], "tensor")
    dy_sent = call(
        body(dispatch_dy_body, z),
        [pair] * quarter,
        [who, pos, *dy_rows],
        [pltpu.VMEM((half * blk, width), F32)],
    )
    dy_in = send_pairs(dy_sent, quarter, "expert")
    attn_w = gather_near(attn_part[:1] + hold(attn_part[1:], dy_sent[:1]), "tensor")

    norms = jnp.stack([ln1_gain, ln1_bias, ln2_gain, ln2_bias])
    wr = w_router.T
    second, (resid, h1, *rest) = split_at(z.images, call(
        body(attend_body, z),
        [
            *[shape((lp, width), BF16)] * z.images,
            shape((z.rows, width), F32),
            rows_low,
            *[shape((z.rows, 3 * hw), BF16)] * nt,
            *[shape((z.rows, hw), BF16)] * nt,
            *[shape((z.images * z.hpb, lp, lp), BF16)] * nt,
        ],
        [who, Far(block_in), norms, Far(wr), *attn_w],
        [
            pltpu.VMEM((z.rows, width), F32),
            pltpu.VMEM((lp, width), F32),
            pltpu.VMEM((ne, width), F32),
        ],
    ))
    qkv, ctx, probs = rest[:nt], rest[nt : 2 * nt], rest[2 * nt :]
    rows_part = [gather_far(v, "tensor") for v in second]
    far = nt // 2 - 1
    rest = hold([w for v in rows_part for w in v[1:]] + dy_in, [])
    rows = [
        gather_near([v[0], *rest[i * far : (i + 1) * far]], "tensor")
        for i, v in enumerate(rows_part)
    ]
    rows = [v[r] for r in range(nt) for v in rows]
    dy_in = rest[z.images * far :]
    dy_passed = pass_on(dy_in, "expert")
    sent = call(
        body(dispatch_body, z),
        [pair] * half + [shape((blk, width), BF16)] * half,
        [who, pos, keep, *rows, *dy_rows],
        [
            pltpu.VMEM((z.slots, width), F32),
            pltpu.VMEM((half * blk, width), F32),
            pltpu.VMEM((2 * ne, z.slots), F32),
        ],
    )
    expert_own = hold([expert_own], rest[:1])[0]
    *sent, dy_passed, own_core = hold([*sent, dy_passed, swap(expert_own, "tensor", 1)], [])
    far_in = [swap(v, "expert", half + k) for k, v in enumerate(sent[half:])]
    near_in = hold(sent[1:half], far_in)
    near_in = [sent[0]] + [swap(v, "expert", 1 + k) for k, v in enumerate(near_in)]
    w_part = gather_far(expert_own, "tensor")
    rest = hold(w_part[1:], far_in)
    expert_w = [w_part[0], own_core, *gather_near(rest, "tensor")]

    size = half * blk
    passed = [
        *[shape((size, hid), BF16)] * (2 * nt),
        shape((size, width), BF16),
        shape((1, 128), F32),
    ]
    held = [
        pltpu.VMEM((size, width), BF16),
        pltpu.VMEM((size, 128), F32),
        pltpu.VMEM((size, width), F32),
        pltpu.VMEM((size, width), F32),
    ]
    far = call(
        body(expert_body, z, False, half),
        [pair] * half + passed,
        [who, *far_in, *dy_in, dy_passed, *expert_w],
        held,
    )
    far_out, far_mixed, (*far_hidden, far_g, far_top) = far[:quarter], far[quarter:half], far[half:]
    near = call(
        body(expert_body, z, True, half),
        [pair] * half + passed,
        [who, *near_in, *expert_w, far_top],
        held,
    )
    near_out, (*near_hidden, near_g, tops) = near[:half], near[half:]
    far_out = send_pairs(far_out, quarter, "expert")
    near_out = [v if k == 0 else swap(v, "expert", k) for k, v in enumerate(near_out)]
    expert_grads = call(
        body(expert_weights_body, z),
        [shape((width, hid), BF16)] * (2 * nt),
        [who, *near_in, *far_in, near_g, far_g, *near_hidden, *far_hidden],
        [pltpu.VMEM((2, width, size), BF16), pltpu.VMEM((2, width, size), BF16)],
    )
    far_out = hold(far_out, expert_grads[:1])
    far_out.append(pass_on(far_out, "expert"))
    first_near = scatter_near(expert_grads[:nt], "tensor")
    second_near = scatter_near(expert_grads[nt:], "tensor")

    partial = call(
        body(combine_body, z, True),
        [rows_low] * nt + [shape((ne, width), F32)],
        [who, post, keep, Far(wr), *rows, *near_out, *far_out],
        [pltpu.VMEM((z.slots, width), BF16)],
    )
    router_part = partial[nt]
    dz_near = scatter_near(partial[:nt], "tensor")
    dz_parts = scatter_far(dz_near, "tensor")
    mixed = send_pairs(far_mixed, quarter, "expert")
    second_parts = scatter_far(hold_far(second_near, dz_parts[-1:]), "tensor")

    pay = shape((ne, z.prow, z.wide), BF16)
    buffers = [pltpu.VMEM((ne, z.crow, z.wide), F32), pltpu.VMEM((ne, 8, z.wide), F32)]
    per_head = shape((z.rows, hw), BF16)
    outs = call(
        body(back_one_body, z, len(dz_parts)),
        [shape((z.rows, width), F32)] + [per_head] * (2 * nt) + [pay] * nt,
        [who, Far(out_grad), norms, resid, router_part, h1, *dz_parts, *attn_w, *probs, *ctx],
        [pltpu.VMEM((z.rows, width), F32), pltpu.VMEM((8 + ne, width), F32), *buffers],
    )
    dresid, dctx, dv = outs[0], outs[1:][:nt], outs[1 + nt :][:nt]
    one_near = scatter_near(outs[1 + 2 * nt :], "tensor")
    outs = call(
        body(back_two_body, z),
        [Far(shape((z.tok_dev, width), F32))] + [pay] * nt,
        [who, Far(block_in), norms, h1, *qkv, *dctx, *probs, *dv, dresid, *attn_w],
        [pltpu.VMEM((z.rows, width), F32), pltpu.VMEM((8, width), F32), *buffers],
        after=[one_near[nt // 2][0]],
    )
    input_grad = outs[0]
    one_parts = scatter_far(one_near, "tensor")
    far = [r for r in first_near if r]
    two = hold(
        [
            *outs[1:],
            one_parts[-1],
            second_parts[-1],
            second_parts[1],
            first_near[0][1],
            *[first_near[r][0] for r in far],
        ],
        [],
    )
    two, (one_parts[-1], second_parts[-1], second_parts[1], first_near[0][1], *rest) = split_at(nt, two)
    first_near.update((r, [v]) for r, v in zip(far, rest))
    two[0], *mixed = hold([two[0], *mixed], [])
    passed = pass_on(mixed, "expert")
    one = total_low(one_parts)
    one = total_low([one[:half], swap(one[half:], "expert", 1)])
    two_near = scatter_near(two, "tensor")
    two_parts = scatter_xy(two_near)

    mixed_part = call(
        body(combine_body, z, False),
        [rows_low] * nt,
        [who, post, *near_out, *mixed, passed],
        [pltpu.VMEM((z.slots, width), BF16)],
    )
    mixed_part = hold(mixed_part, [two_parts[-1]])
    mixed_parts = scatter_sum(mixed_part, "tensor")
    first_parts = scatter_far(hold_far(first_near, two_parts[-1:]), "tensor")
    merged = jnp.concatenate([one, total_low(two_parts)], axis=2)
    value = sum_rest(hold([merged], mixed_part[:1])[0], "expert")
    value, mixed_parts[-1] = hold([value, mixed_parts[-1]], [])
    sums = [value, swap(value, "expert", 1)]
    block_out = call(
        body(finish_body, z, len(mixed_parts)),
        Far(shape((z.tok_dev, width), F32)),
        [who, resid, *mixed_parts],
        [pltpu.VMEM((z.rows, width), F32)],
    )

    head = Far(shape((width, hw), F32))
    grad_q, grad_k, grad_v, grad_o, n1, n2, n3, n4, router_grad = call(
        body(last_body, z),
        [head] * 3
        + [Far(shape(v, F32)) for v in ((hw, width), *[(1, width)] * 4, (ne, width))],
        [who, *sums],
        [pltpu.VMEM((ne, z.crow, 2 * z.wide), F32), pltpu.VMEM((ne, 8, 2 * z.wide), F32)],
        after=[place(v, pltpu.HBM) for v in (block_out,)],
    )
    first_parts[-1:] = hold(first_parts[-1:], [place(n1, pltpu.HBM)])
    grad_first, grad_second = call(
        body(expert_grads_body, z, len(first_parts)),
        [Far(shape((width, hid), F32)), Far(shape((hid, width), F32))],
        [who, *first_parts, *second_parts],
    )
    head_maxima = lax.dynamic_slice_in_dim(tops[0], me_t * z.hpb, z.hpb, 0)
    factor = jnp.repeat(jnp.sqrt(jnp.minimum(1.0, clip_limit / head_maxima)), HEAD_DIM)
    return (
        block_out,
        input_grad,
        n1[0],
        n2[0],
        grad_q,
        grad_k,
        grad_v,
        grad_o,
        n3[0],
        n4[0],
        router_grad.T,
        grad_first[None],
        grad_second[None],
        head_maxima,
        w_query * factor[None, :],
        w_key * factor[None, :],
    )


def solution(mesh):
    placed = (
        P(("expert", "tensor"), None),
        P(("expert", "tensor"), None),
        P("expert", None),
        P("expert", None),
        P(),
        P(),
        P(None, "tensor"),
        P(None, "tensor"),
        P(None, "tensor"),
        P("tensor", None),
        P(),
        P(),
        P(),
        P("expert", None, "tensor"),
        P("expert", "tensor", None),
    )
    return jax.shard_map(
        shards,
        mesh=mesh,
        in_specs=placed,
        out_specs=(
            P(("expert", "tensor"), None),
            P(("expert", "tensor"), None),
            P(),
            P(),
            P(None, "tensor"),
            P(None, "tensor"),
            P(None, "tensor"),
            P("tensor", None),
            P(),
            P(),
            P(),
            P("expert", None, "tensor"),
            P("expert", "tensor", None),
            P("tensor"),
            P(None, "tensor"),
            P(None, "tensor"),
        ),
        check_vma=False,
    )
```

```python
import functools

import jax
import jax.numpy as jnp
from jax import lax
from jax.experimental import pallas as pl
from jax.experimental.pallas import tpu as pltpu
from jax.sharding import PartitionSpec as P

HEAD_DIM = 64
IMAGE_TOKENS = 197
SPARE = 200
TOP_ROW = 197

F32 = jnp.float32
BF16 = jnp.bfloat16
I32 = jnp.int32

clip_limit = 4.0
norm_eps = 1e-06
low_value = -1e30


def round_up(value, unit):
    return -(-value // unit) * unit


def dot_nn(a, b):
    return lax.dot_general(a, b, (((1,), (0,)), ((), ())), preferred_element_type=F32)


def dot_nt(a, b):
    return lax.dot_general(a, b, (((1,), (1,)), ((), ())), preferred_element_type=F32)


def dot_tn(a, b):
    return lax.dot_general(a, b, (((0,), (0,)), ((), ())), preferred_element_type=F32)


def iota(shape, dim):
    return lax.broadcasted_iota(I32, shape, dim)


def split2(v):
    high = v.astype(BF16).astype(F32)
    return high, (v - high).astype(BF16).astype(F32)


def normalize(rows):
    center = jnp.mean(rows, axis=-1, keepdims=True)
    offset = rows - center
    rstd = lax.rsqrt(jnp.mean(offset * offset, axis=-1, keepdims=True) + norm_eps)
    return offset * rstd, rstd


def norm_back(grad, unit, rstd):
    return rstd * (
        grad
        - jnp.mean(grad, axis=-1, keepdims=True)
        - unit * jnp.mean(grad * unit, axis=-1, keepdims=True)
    )


def halving_bits(n):
    return [1 << k for k in range(n.bit_length() - 1)]


class Sizes:
    def __init__(self, nt, ne, width, tok_dev, tok_group, head_cols, hidden):
        self.nt, self.ne, self.width = nt, ne, width
        self.tok_dev = tok_dev
        self.images = tok_dev // IMAGE_TOKENS
        self.lp = round_up(SPARE + ne, 16)
        self.rows = self.images * self.lp
        self.chunks = nt * self.images
        self.cap = 5 * tok_group // (2 * ne) + 1
        self.spr = -(-self.cap // nt)
        need = self.spr + 2
        self.blk = next((b for b in (16, 32, 64, 128) if b >= need), round_up(need, 128))
        self.epl = 128 // self.blk
        self.hw = head_cols
        self.hpb = head_cols // HEAD_DIM
        self.hid = hidden
        self.slots = ne * self.blk
        self.wide = 2 * self.hw
        self.pieces = width // self.wide
        self.crow = width // ne
        self.prow = self.crow + 8
        bits = halving_bits(ne)
        self.offset = places(bits)


SM = pl.BlockSpec(memory_space=pltpu.SMEM)
VM = pl.BlockSpec(memory_space=pltpu.VMEM)
ANY = pl.BlockSpec(memory_space=pl.ANY)


class Far:
    def __init__(self, value):
        self.value = value


class Given:
    def __init__(self, ref, copy):
        self.ref, self.copy = ref, copy
        copy.start()

    def wait(self):
        if self.copy is not None:
            self.copy.wait()
            self.copy = None

    def __getitem__(self, at):
        self.wait()
        return self.ref[at]


def place(value, space):
    return pltpu.with_memory_space_constraint(value, space)


def call(body, outs, args, scratch=(), after=()):
    skip = len(after)
    keep = lax.axis_size("tensor") <= 4
    vmem = 12 if keep else 60
    single = not isinstance(outs, list)
    flat = [outs] if single else outs
    far = [k for k, a in enumerate(args) if isinstance(a, Far)]

    def run(*refs):
        ins, refs = [refs[0], *refs[1 + skip : skip + len(args)]], refs[skip + len(args) :]
        results, refs = refs[: len(flat)], refs[len(flat) :]
        own, refs = refs[: len(scratch)], refs[len(scratch) :]
        for n, k in enumerate(far):
            ins[k] = Given(refs[n], pltpu.make_async_copy(ins[k], refs[n], refs[-1].at[n]))
        body(*ins, *results, *own)
        for k in far:
            ins[k].wait()

    extra = [pltpu.VMEM(args[k].value.shape, args[k].value.dtype) for k in far]
    if far:
        extra.append(pltpu.SemaphoreType.DMA((len(far),)))
    got = pl.pallas_call(
        run,
        out_shape=[
            o.value if isinstance(o, Far) else pltpu.VMEM(o.shape, o.dtype) if keep else o
            for o in flat
        ],
        in_specs=[SM] + [ANY] * skip + [ANY if k in far else VM for k in range(1, len(args))],
        out_specs=[VM] * len(flat),
        scratch_shapes=[*scratch, *extra],
        compiler_params=pltpu.CompilerParams(vmem_limit_bytes=vmem * 1024 * 1024),
    )(
        args[0],
        *after,
        *[
            place(a.value, pltpu.HBM) if isinstance(a, Far) else place(a, pltpu.VMEM) if keep else a
            for a in args[1:]
        ],
    )
    return got[0] if single else list(got)


def hold(values, after):
    n, m = len(values), len(after)

    def run(*refs):
        pass

    out = pl.pallas_call(
        run,
        out_shape=[shape(v.shape, v.dtype) for v in values],
        in_specs=[ANY] * (n + m),
        out_specs=[ANY] * n,
        input_output_aliases={k: k for k in range(n)},
        compiler_params=pltpu.CompilerParams(vmem_limit_bytes=1024 * 1024),
    )(*values, *after)
    return list(out)


def shape(dims, kind):
    return jax.ShapeDtypeStruct(dims, kind)


def first_body(z, who, dy_ref, q_ref, k_ref, v_ref, o_ref, low_ref, out_ref, pad):
    hw = z.hw
    pad[...] = jnp.zeros(pad.shape, F32)
    for i in range(z.images):
        pad[i * z.lp : i * z.lp + IMAGE_TOKENS, :] = dy_ref[
            i * IMAGE_TOKENS : (i + 1) * IMAGE_TOKENS, :
        ]
    low_ref[...] = pad[...].astype(BF16)
    for n, ref in enumerate((q_ref, k_ref, v_ref)):
        out_ref[:, n * hw : (n + 1) * hw] = ref[...].astype(BF16)
    out_ref[:, 3 * hw : 4 * hw] = o_ref[...].T.astype(BF16)


def early_body(z, who, in_ref, out_ref, route_ref, kept_ref, *refs):
    w_ref, pos_ref, keep_ref, post_ref = refs
    w_ref[0 : z.width, :] = in_ref[...].astype(BF16)
    w_ref[z.width : 2 * z.width, :] = out_ref[...].T.astype(BF16)
    me_t, me_e = who[0], who[1]
    named = jnp.bitwise_xor(iota((z.ne, z.lp), 0), me_e)
    before = jnp.where(iota((z.lp, z.lp), 0) < iota((z.lp, z.lp), 1), 1.0, 0.0).astype(BF16)
    count = jnp.zeros((z.ne, 1), F32)
    for c in range(z.chunks):
        block, img = c // z.images, c % z.images
        first = route_ref[0, c : c + 1, :] == named
        other = route_ref[1, c : c + 1, :] == named
        hit = jnp.where(first | other, 1.0, 0.0)
        place = dot_nn(hit.astype(BF16), before) + count
        count = count + jnp.sum(hit, axis=1, keepdims=True)
        at = jnp.bitwise_xor(block, me_t) * z.images + img
        place = jnp.where(hit > 0, place, -1.0)
        pos_ref[at] = place.astype(I32)
        post_ref[at] = place.T.astype(I32)
        keep_ref[at] = jnp.where(first, kept_ref[0, c : c + 1, :], 0.0) + jnp.where(
            other, kept_ref[1, c : c + 1, :], 0.0
        )


def attend_body(z, who, x_ref, ln_ref, wr_ref, *refs):
    nt, lp, hw = z.nt, z.lp, z.hw
    weights = refs[:nt]
    z_refs, refs = refs[nt : nt + z.images], refs[nt + z.images :]
    resid_ref, h1_ref, refs = refs[0], refs[1], refs[2:]
    qkv_ref, ctx_ref, p_ref = refs[:nt], refs[nt : 2 * nt], refs[2 * nt : 3 * nt]
    xp, zb, pt = refs[3 * nt :]
    me_t = who[0]
    xp[...] = jnp.zeros(xp.shape, F32)
    for i in range(z.images):
        xp[i * lp : i * lp + IMAGE_TOKENS, :] = x_ref[
            i * IMAGE_TOKENS : (i + 1) * IMAGE_TOKENS, :
        ]
    unit, _ = normalize(xp[...])
    h1 = (unit * ln_ref[0:1, :] + ln_ref[1:2, :]).astype(BF16)
    h1_ref[...] = h1
    head_of = iota((lp, hw), 1) // HEAD_DIM
    real = iota((lp, lp), 1) < IMAGE_TOKENS
    real_row = iota((lp, 1), 0) < IMAGE_TOKENS
    lane = iota((1, 128), 1)
    tops = jnp.full((1, 128), low_value, F32)
    attn = jnp.zeros((z.rows, z.width), F32)
    for r in range(nt):
        qkv = dot_nn(h1, weights[r][:, 0 : 3 * hw]).astype(BF16)
        qkv_ref[r][...] = qkv
        ctxs = []
        for i in range(z.images):
            at = slice(i * lp, (i + 1) * lp)
            q, k, v = (qkv[at, n * hw : (n + 1) * hw] for n in range(3))
            ctx = jnp.zeros((lp, hw), F32)
            for j in range(z.hpb):
                mine = head_of == j
                s = dot_nt(jnp.where(mine, q, jnp.zeros_like(q)), k) * (HEAD_DIM**-0.5)
                s = jnp.where(real, s, low_value)
                peak = jnp.max(s, axis=1, keepdims=True)
                top = jnp.max(jnp.where(real_row, peak, low_value), axis=0, keepdims=True)
                head = jnp.bitwise_xor(me_t, r) * z.hpb + j
                tops = jnp.where(lane == head, jnp.maximum(tops, top), tops)
                e = jnp.exp(s - peak)
                p = (e * (1.0 / jnp.sum(e, axis=1, keepdims=True))).astype(BF16)
                p_ref[r][i * z.hpb + j] = p
                ctx = jnp.where(mine, dot_nn(p, v), ctx)
            ctxs.append(ctx.astype(BF16))
        ctx = jnp.concatenate(ctxs, axis=0)
        ctx_ref[r][...] = ctx
        attn = attn + dot_nt(ctx, weights[r][:, 3 * hw : 4 * hw])
    resid = xp[...] + attn
    resid_ref[...] = resid
    unit, _ = normalize(resid)
    second = unit * ln_ref[2:3, :] + ln_ref[3:4, :]
    w_hi, w_lo = (v.astype(BF16) for v in split2(router_rows(z, who, wr_ref)))
    row = iota((lp, 1), 0)
    t_hi = tops.astype(BF16).astype(F32)
    t_mid = (tops - t_hi).astype(BF16).astype(F32)
    t_lo = tops - t_hi - t_mid
    for i in range(z.images):
        part = second[i * lp : (i + 1) * lp]
        s_hi, s_lo = (v.astype(BF16) for v in split2(part))
        logits = dot_nt(w_hi, s_hi) + (dot_nt(w_hi, s_lo) + dot_nt(w_lo, s_hi))
        e = jnp.exp(logits - jnp.max(logits, axis=0, keepdims=True))
        p_hi, p_lo = split2(e / jnp.sum(e, axis=0, keepdims=True))
        pt[...] = jnp.zeros(pt.shape, F32)
        pt[:, 0:lp] = p_hi
        pt[:, 256 : 256 + lp] = p_lo
        zb[...] = jnp.where(row < IMAGE_TOKENS, part, 0.0)
        for n, t in enumerate((t_hi, t_mid, t_lo)):
            zb[TOP_ROW + n : TOP_ROW + n + 1, 0:128] = t
        zb[SPARE : SPARE + z.ne, :] = pt[...]
        z_refs[i][...] = zb[...].astype(BF16)


def router_rows(z, who, ref):
    return jnp.concatenate(
        [ref[pl.ds(jnp.bitwise_xor(e, who[1]), 1), :] for e in range(z.ne)], axis=0
    )


def split_at(n, values):
    return values[:n], values[n:]


def tail_rows(z, ref):
    start = (TOP_ROW // 16) * 16
    return ref[start : z.lp, :].astype(F32), start


def probs_of(z, ref):
    tail, start = tail_rows(z, ref)
    both = tail[SPARE - start : SPARE - start + z.ne]
    return both[:, 0 : z.lp] + both[:, 256 : 256 + z.lp]


def hot_rows(z, who, pos_ref, c, first, last):
    slot = iota((z.blk, z.lp), 0)
    slot = jnp.where(slot < z.spr, slot + who[0] * z.spr, -2)
    return jnp.concatenate(
        [
            jnp.where(pos_ref[c, e : e + 1, :] == slot, 1.0, 0.0).astype(BF16)
            for e in range(first, last)
        ],
        axis=0,
    )


def dispatch_dy_body(z, who, pos_ref, *refs):
    nt, ne, lp, blk = z.nt, z.ne, z.lp, z.blk
    rows, outs, acc = refs[:nt], refs[nt : nt + ne // 4], refs[nt + ne // 4]
    for c in range(z.chunks):
        r, i = c // z.images, c % z.images
        hot = hot_rows(z, who, pos_ref, c, ne // 2, ne)
        part = dot_nn(hot, rows[r][i * lp : (i + 1) * lp, :])
        acc[...] = part if c == 0 else acc[...] + part
    for k in range(ne // 4):
        outs[k][...] = acc[2 * k * blk : 2 * (k + 1) * blk, :].astype(BF16)


def dispatch_body(z, who, pos_ref, keep_ref, *refs):
    nt, ne, lp, blk = z.nt, z.ne, z.lp, z.blk
    rows, dy_rows, refs = refs[: z.chunks], refs[z.chunks :][:nt], refs[z.chunks + nt :]
    outs, (acc, dy_acc, gacc) = refs[:ne], refs[ne:]
    half = ne // 2
    tops = None
    for c in range(z.chunks):
        r, i = c // z.images, c % z.images
        hot = hot_rows(z, who, pos_ref, c, 0, ne)
        part = dot_nn(hot[: half * blk], dy_rows[r][i * lp : (i + 1) * lp, :])
        dy_acc[...] = part if c == 0 else dy_acc[...] + part
        part = dot_nn(hot, rows[c][...])
        acc[...] = part if c == 0 else acc[...] + part
        g_hi, g_lo = split2(probs_of(z, rows[c]) * keep_ref[c])
        both = jnp.concatenate([g_hi, g_lo], axis=0).astype(BF16)
        part = dot_nt(both, hot)
        gacc[...] = part if c == 0 else gacc[...] + part
        if i == 0:
            tail, start = tail_rows(z, rows[c])
            three = tail[TOP_ROW - start : TOP_ROW - start + 3, 0:128]
            top = three[0:1] + three[1:2] + three[2:3]
            tops = top if tops is None else jnp.maximum(tops, top)
    t_hi = tops.astype(BF16).astype(F32)
    t_mid = (tops - t_hi).astype(BF16).astype(F32)
    t_lo = tops - t_hi - t_mid
    none = jnp.zeros((1, 128), F32)
    top_row = jnp.concatenate([t_hi, t_mid, t_lo, none], axis=1)
    row = iota((blk, 1), 0)
    part_of = iota((1, 128), 1) // blk
    for e in range(ne):
        tile = slice((e // z.epl) * 128, (e // z.epl) * 128 + 128)
        g_hi = jnp.where(part_of == e % z.epl, gacc[e : e + 1, tile], 0.0)
        g_lo = jnp.where(part_of == e % z.epl, gacc[ne + e : ne + e + 1, tile], 0.0)
        gates = jnp.concatenate([g_hi, g_lo, none, none], axis=1)
        block = acc[e * blk : (e + 1) * blk, :]
        block = jnp.where(row == z.spr, gates, block)
        block = jnp.where(row == z.spr + 1, top_row, block)
        outs[e][0:blk, :] = block.astype(BF16)
        if e < half:
            outs[e][blk : 2 * blk, :] = dy_acc[e * blk : (e + 1) * blk, :].astype(BF16)


class Part:
    def __init__(self, ref, first):
        self.ref, self.first = ref, first

    def rows(self, start, stop):
        return self.ref[self.first + start : self.first + stop, :]

    def put(self, value):
        self.ref[self.first : self.first + value.shape[0], :] = value


def blocks_of(z, direct, passed, size=1, at=0):
    out = []
    for k, ref in enumerate(direct):
        out += [Part(ref, at * z.blk), Part(passed, (k * size + at) * z.blk)]
    return out


def spare_pair(z, part):
    start = (z.spr // 16) * 16
    tail = part.rows(start, z.blk).astype(F32)
    return tail[z.spr - start : z.spr - start + 1], tail[z.spr - start + 1 : z.spr - start + 2]


def expert_body(z, near, count, who, *refs):
    nt, ne, blk, hid, width = z.nt, z.ne, z.blk, z.hid, z.width
    half = count // 2
    rows_in = [Part(ref, 0) for ref in refs[:count]]
    if near:
        dy_in, refs = [Part(ref, blk) for ref in refs[:count]], refs[count:]
    else:
        refs = refs[count:]
        dy_in, refs = blocks_of(z, refs[:half], refs[half]), refs[half + 1 :]
    weights, refs = refs[:nt], refs[nt:]
    w = z.width
    if near:
        far_top, refs = refs[0], refs[1:]
        back, mixed = ([Part(ref, at * blk) for ref in refs[:count]] for at in range(2))
        refs = refs[count:]
    else:
        back, mixed = (
            [Part(ref, at * blk) for ref in some for at in range(2)]
            for some in (refs[:half], refs[half:count])
        )
        refs = refs[count:]
    act, du, refs = refs[:nt], refs[nt : 2 * nt], refs[2 * nt :]
    g, top_ref, rows, gate, o_acc, d_acc = refs
    real = iota((blk, 1), 0) < z.spr
    diag = iota((blk, 128), 0) == iota((blk, 128), 1) % blk
    tops = far_top[...] if near else None
    for n in range(count):
        at = slice(n * blk, (n + 1) * blk)
        rows[at, :] = jnp.where(real, rows_in[n].rows(0, blk), jnp.zeros((), BF16))
        gates, top = spare_pair(z, rows_in[n])
        top = top[:, 0:128] + top[:, 128:256] + top[:, 256:384]
        tops = top if tops is None else jnp.maximum(tops, top)
        line = gates[:, 0:128] + gates[:, 128:256]
        column = jnp.sum(jnp.where(diag, line, 0.0), axis=1, keepdims=True)
        gate[at, :] = jnp.broadcast_to(column, (blk, 128))
    top_ref[...] = tops
    u_first = dot_nn(rows[...], weights[0][0:w, :])
    for n in range(count):
        at = slice(n * blk, (n + 1) * blk)
        g[at, :] = (gate[at, 0:1] * dy_in[n].rows(0, blk).astype(F32)).astype(BF16)
    for r in range(nt):
        u = dot_nn(rows[...], weights[r][0:w, :]) if r else u_first
        second_w = weights[r][w : 2 * w, :]
        cube = 0.7978845608028654 * 0.044715 * u * u
        t = jnp.tanh(u * (0.7978845608028654 + cube))
        h = 0.5 + 0.5 * t
        a = (u * h).astype(BF16)
        slope = h + 2.0 * h * (1.0 - h) * u * (0.7978845608028654 + 3.0 * cube)
        d = (dot_nn(g[...], second_w) * slope).astype(BF16)
        act[r][...] = a
        du[r][...] = d
        o = dot_nt(a, second_w)
        b = dot_nt(d, weights[r][0:w, :])
        o_acc[...] = o if r == 0 else o_acc[...] + o
        d_acc[...] = b if r == 0 else d_acc[...] + b
    row = iota((blk, 1), 0)
    none = jnp.zeros((1, 128), F32)
    for n in range(count):
        at = slice(n * blk, (n + 1) * blk)
        o = o_acc[at, :]
        dgate = jnp.sum(o * dy_in[n].rows(0, blk).astype(F32), axis=1, keepdims=True)
        line = jnp.sum(jnp.where(diag, dgate, 0.0), axis=0, keepdims=True)
        hi, lo = split2(line)
        line = jnp.concatenate([hi, lo, none, none], axis=1)
        back[n].put(jnp.where(row == z.spr, line, d_acc[at, :]).astype(BF16))
        mixed[n].put((gate[at, 0:1] * o).astype(BF16))


def expert_weights_body(z, who, *refs):
    nt, ne, blk, hid = z.nt, z.ne, z.blk, z.hid
    rows_in, refs = [Part(ref, 0) for ref in refs[:ne]], refs[ne:]
    g, refs = refs[:2], refs[2:]
    act, du = (refs[:nt], refs[2 * nt : 3 * nt]), (refs[nt : 2 * nt], refs[3 * nt : 4 * nt])
    one, two, (rows_t, g_t) = refs[4 * nt : 5 * nt], refs[5 * nt : 6 * nt], refs[6 * nt :]
    real = iota((blk, 1), 0) < z.spr
    rows = [jnp.where(real, part.rows(0, blk), jnp.zeros((), BF16)) for part in rows_in]
    half = ne // 2
    for k in range(2):
        rows_t[k] = jnp.concatenate(rows[k * half : (k + 1) * half], axis=0).T
        g_t[k] = g[k][...].T
    for r in range(nt):
        first = dot_nn(rows_t[0], du[0][r][...]) + dot_nn(rows_t[1], du[1][r][...])
        one[r][...] = first.astype(BF16)
        second = dot_nn(g_t[0], act[0][r][...]) + dot_nn(g_t[1], act[1][r][...])
        two[r][...] = second.astype(BF16)


def hot_columns(z, post_ref, c, base):
    lane = iota((z.lp, 128), 1)
    slot = lane % z.blk
    slot = jnp.where(slot < z.spr, slot + base, -2)
    tiles = []
    for p in range(z.ne // z.epl):
        column = post_ref[c, :, p * z.epl : p * z.epl + 1]
        pick = jnp.broadcast_to(column, (z.lp, 128))
        for n in range(1, z.epl):
            e = p * z.epl + n
            pick = jnp.where(lane // z.blk == n, post_ref[c, :, e : e + 1], pick)
        tiles.append(jnp.where(pick == slot, 1.0, 0.0).astype(BF16))
    return jnp.concatenate(tiles, axis=1)


def combine_body(z, with_router, who, post_ref, *refs):
    nt, ne, lp, blk = z.nt, z.ne, z.lp, z.blk
    base = who[0] * z.spr
    if with_router:
        keep_ref, wr_ref = refs[:2]
        rows, refs = refs[2 : 2 + z.chunks], refs[2 + z.chunks :]
    quarter = ne // 4
    at = 0 if with_router else blk
    blocks, refs = [Part(ref, at) for ref in refs[: ne // 2]], refs[ne // 2 :]
    blocks, refs = blocks + blocks_of(z, refs[:quarter], refs[quarter]), refs[quarter + 1 :]
    outs, refs = refs[:nt], refs[nt:]
    if with_router:
        gr_ref, refs = refs[0], refs[1:]
    stack = refs[0]
    for e in range(ne):
        stack[e * blk : (e + 1) * blk, :] = blocks[e].rows(0, blk)
    if with_router:
        row = iota((ne, 128), 0)
        half = iota((ne, 128), 1) // blk
        tiles = []
        for p in range(ne // z.epl):
            hi = jnp.zeros((ne, 128), F32)
            lo = jnp.zeros((ne, 128), F32)
            for n in range(z.epl):
                e = p * z.epl + n
                line, _ = spare_pair(z, blocks[e])
                own = (row == e) & (half == n)
                hi = jnp.where(own, line[:, 0:128], hi)
                lo = jnp.where(own, line[:, 128:256], lo)
            tiles.append(jnp.concatenate([hi, lo], axis=0))
        dgate = jnp.concatenate(tiles, axis=1).astype(BF16)
        unit = jnp.where(iota((lp, lp), 0) == iota((lp, lp), 1), 1.0, 0.0).astype(BF16)
        wr = router_rows(z, who, wr_ref).astype(BF16)
        wr = jnp.concatenate([wr, wr], axis=0)
        total = jnp.zeros((2 * ne, z.width), F32)
    for c in range(z.chunks):
        r, i = c // z.images, c % z.images
        at = slice(i * lp, (i + 1) * lp)
        hot = hot_columns(z, post_ref, c, base)
        part = dot_nn(hot, stack[...])
        if with_router:
            both = dot_nt(dgate, hot)
            dp = (both[0:ne] + both[ne : 2 * ne]) * keep_ref[c]
            pr = probs_of(z, rows[c])
            dl = pr * (dp - jnp.sum(pr * dp, axis=0, keepdims=True))
            dl = jnp.concatenate(split2(dl), axis=0).astype(BF16)
            part = part + dot_nn(dot_nt(unit, dl).astype(BF16), wr)
            total = total + dot_nn(dl, rows[c][...])
        outs[r][at, :] = part.astype(BF16)
    if with_router:
        gr_ref[...] = total[0:ne] + total[ne : 2 * ne]


def spread_rows(z, lines):
    n = lines.shape[0] * z.pieces
    rows = [lines[:, s * z.wide : (s + 1) * z.wide] for s in range(z.pieces)]
    return jnp.concatenate(rows + [jnp.zeros((8 * z.ne - n, z.wide), F32)], axis=0)


def write_parts(z, who, ref, wide, lines):
    for p in range(z.ne):
        c = jnp.bitwise_xor(z.offset[p], who[1])
        ref[p] = jnp.concatenate([wide[c], lines[c]], axis=0).astype(BF16)


def back_one_body(z, parts, who, dy_ref, ln_ref, resid_ref, gr_ref, h1_ref, *refs):
    nt, lp, hw = z.nt, z.lp, z.hw
    dz_parts, refs = refs[:parts], refs[parts:]
    weights, p_ref, ctx_ref, refs = refs[:nt], refs[nt : 2 * nt], refs[2 * nt : 3 * nt], refs[3 * nt :]
    dresid_ref, dctx_ref, dv_ref, pays = refs[0], refs[1:][:nt], refs[1 + nt :][:nt], refs[1 + 2 * nt :][:nt]
    dyp, tail, buf, lines = refs[1 + 3 * nt :]
    dyp[...] = jnp.zeros(dyp.shape, F32)
    for i in range(z.images):
        dyp[i * lp : i * lp + IMAGE_TOKENS, :] = dy_ref[
            i * IMAGE_TOKENS : (i + 1) * IMAGE_TOKENS, :
        ]
    dz = dz_parts[0][...].astype(F32)
    for p in dz_parts[1:]:
        dz = dz + p[...].astype(F32)
    unit, rstd = normalize(resid_ref[...])
    dresid = norm_back(dz * ln_ref[2:3, :], unit, rstd) + dyp[...]
    dresid_ref[...] = dresid
    tail[...] = jnp.zeros(tail.shape, F32)
    tail[0:1, :] = jnp.sum(dz * unit, axis=0, keepdims=True)
    tail[1:2, :] = jnp.sum(dz, axis=0, keepdims=True)
    for e in range(z.ne):
        tail[pl.ds(8 + jnp.bitwise_xor(e, who[1]), 1), :] = gr_ref[e : e + 1, :]
    rows = spread_rows(z, tail[...])
    for p in range(z.ne):
        lines[p] = rows[8 * p : 8 * p + 8]
    da = dresid.astype(BF16)
    h1_t = h1_ref[...].T
    da_t = da.T
    head_of = iota((lp, hw), 1) // HEAD_DIM
    for r in range(nt):
        dctx = dot_nn(da, weights[r][:, 3 * hw : 4 * hw]).astype(BF16)
        dctx_ref[r][...] = dctx
        pieces = []
        for i in range(z.images):
            dc = dctx[i * lp : (i + 1) * lp]
            dv = jnp.zeros((lp, hw), F32)
            for j in range(z.hpb):
                p = p_ref[r][i * z.hpb + j]
                dv = jnp.where(head_of == j, dot_tn(p, dc), dv)
            pieces.append(dv.astype(BF16))
        dv = jnp.concatenate(pieces, axis=0)
        dv_ref[r][...] = dv
        dw = jnp.concatenate([dot_nn(h1_t, dv), dot_nn(da_t, ctx_ref[r][...])], axis=1)
        for p in range(z.ne):
            buf[p] = dw[p * z.crow : (p + 1) * z.crow]
        write_parts(z, who, pays[r], buf, lines)


def back_two_body(z, who, x_ref, ln_ref, h1_ref, *refs):
    nt, lp, hw = z.nt, z.lp, z.hw
    qkv_ref, dctx_ref, p_ref, dv_ref, refs = (*(refs[k * nt : (k + 1) * nt] for k in range(4)), refs[4 * nt :])
    dresid_ref, refs = refs[0], refs[1:]
    weights, in_ref, pays, xp, tail, buf, lines = (
        refs[:nt],
        refs[nt],
        refs[nt + 1 : 2 * nt + 1],
        *refs[2 * nt + 1 :],
    )
    xp[...] = jnp.zeros(xp.shape, F32)
    for i in range(z.images):
        xp[i * lp : i * lp + IMAGE_TOKENS, :] = x_ref[
            i * IMAGE_TOKENS : (i + 1) * IMAGE_TOKENS, :
        ]
    unit, rstd = normalize(xp[...])
    h1_t = h1_ref[...].T
    head_of = iota((lp, hw), 1) // HEAD_DIM
    dh = jnp.zeros((z.rows, z.width), F32)
    scale = HEAD_DIM**-0.5
    grads = []
    for r in range(nt):
        pieces = []
        for i in range(z.images):
            at = slice(i * lp, (i + 1) * lp)
            q, k, v = (qkv_ref[r][at, n * hw : (n + 1) * hw] for n in range(3))
            dc = dctx_ref[r][at, :]
            dq = jnp.zeros((lp, hw), F32)
            dk = jnp.zeros((lp, hw), F32)
            for j in range(z.hpb):
                mine = head_of == j
                pf = p_ref[r][i * z.hpb + j].astype(F32)
                dp = dot_nt(jnp.where(mine, dc, jnp.zeros_like(dc)), v)
                w = pf * dp
                ds = (w - pf * jnp.sum(w, axis=1, keepdims=True)).astype(BF16)
                dq = jnp.where(mine, dot_nn(ds, k) * scale, dq)
                dk = jnp.where(mine, dot_tn(ds, q) * scale, dk)
            pieces.append(jnp.concatenate([dq, dk], axis=1).astype(BF16))
        dqk = jnp.concatenate(pieces, axis=0)
        grads.append(dot_nn(h1_t, dqk))
        dh = dh + dot_nt(dqk, weights[r][:, 0 : 2 * hw]) + dot_nt(
            dv_ref[r][...], weights[r][:, 2 * hw : 3 * hw]
        )
    tail[...] = jnp.zeros(tail.shape, F32)
    tail[0:1, :] = jnp.sum(dh * unit, axis=0, keepdims=True)
    tail[1:2, :] = jnp.sum(dh, axis=0, keepdims=True)
    rows = spread_rows(z, tail[...])
    for p in range(z.ne):
        lines[p] = rows[8 * p : 8 * p + 8]
    for r in range(nt):
        for p in range(z.ne):
            buf[p] = grads[r][p * z.crow : (p + 1) * z.crow]
        write_parts(z, who, pays[r], buf, lines)
    xp[...] = dresid_ref[...] + norm_back(dh * ln_ref[0:1, :], unit, rstd)
    for i in range(z.images):
        in_ref[i * IMAGE_TOKENS : (i + 1) * IMAGE_TOKENS, :] = xp[
            i * lp : i * lp + IMAGE_TOKENS, :
        ]


def last_body(z, who, low, high, q_ref, k_ref, v_ref, o_ref, n1, n2, n3, n4, router_ref, wide, lines):
    hw, half = z.hw, z.ne // 2
    for p in range(z.ne):
        c = jnp.bitwise_xor(z.offset[p], who[1])
        both = (low, high)[p // half][p % half].astype(F32)
        wide[c] = both[0 : z.crow]
        lines[c] = both[z.crow : z.prow]
    both = jnp.concatenate([wide[p] for p in range(z.ne)], axis=0)
    v_ref[...] = both[:, 0:hw]
    o_ref[...] = both[:, hw : 2 * hw].T
    q_ref[...] = both[:, 2 * hw : 3 * hw]
    k_ref[...] = both[:, 3 * hw : 4 * hw]
    both = jnp.concatenate([lines[p] for p in range(z.ne)], axis=0)
    one, two = both[:, 0 : z.wide], both[:, z.wide : 2 * z.wide]
    n = 8 + z.ne
    one = jnp.concatenate([one[s * n : (s + 1) * n] for s in range(z.pieces)], axis=1)
    two = jnp.concatenate([two[s * 8 : (s + 1) * 8] for s in range(z.pieces)], axis=1)
    n1[...], n2[...], n3[...], n4[...] = two[0:1], two[1:2], one[0:1], one[1:2]
    router_ref[...] = one[8:n]


def expert_grads_body(z, parts, who, *refs):
    one, two, (first_ref, second_ref) = refs[:parts], refs[parts : 2 * parts], refs[2 * parts :]
    first_ref[...] = sum(p[...].astype(F32) for p in one)
    second_ref[...] = sum(p[...].astype(F32) for p in two).T


def finish_body(z, parts, who, resid_ref, *refs):
    out_ref, xp = refs[parts], refs[parts + 1]
    total = refs[0][...].astype(F32)
    for p in refs[1:parts]:
        total = total + p[...].astype(F32)
    xp[...] = resid_ref[...] + total
    for i in range(z.images):
        out_ref[i * IMAGE_TOKENS : (i + 1) * IMAGE_TOKENS, :] = xp[
            i * z.lp : i * z.lp + IMAGE_TOKENS, :
        ]


def swap(value, axis, bit):
    n = lax.axis_size(axis)
    return lax.ppermute(value, axis, [(k, k ^ bit) for k in range(n)])


def gather_far(own, axis):
    blocks = [own]
    for bit in halving_bits(lax.axis_size(axis))[1:]:
        blocks += [swap(v, axis, bit) for v in blocks]
    return blocks


def gather_near(blocks, axis):
    return [v for b in blocks for v in (b, swap(b, axis, 1))]


def gather_blocks(own, axis, late=None):
    blocks = gather_far(own, axis)
    if late is not None:
        blocks = blocks[:1] + hold(blocks[1:], late)
    return gather_near(blocks, axis)


def scatter_step(left, axis, bit):
    left = {r: list(parts) for r, parts in left.items()}
    for r in sorted(left, reverse=True):
        if r & bit:
            left[r ^ bit].append(swap(total_low(left.pop(r)), axis, bit))
    return left


def scatter_near(blocks, axis):
    left = {r: [b] for r, b in enumerate(blocks)}
    left = scatter_step(left, axis, 1)
    far = {r: [total_low(parts)] for r, parts in left.items() if r}
    return {**left, **far}


def hold_far(left, after):
    far = [r for r in left if r]
    held = hold([left[r][0] for r in far], after)
    return {0: left[0], **{r: [v] for r, v in zip(far, held)}}


def scatter_far(left, axis):
    for bit in halving_bits(lax.axis_size(axis))[1:]:
        left = scatter_step(left, axis, bit)
    return left[0]


def scatter_sum(blocks, axis):
    return scatter_far(scatter_near(blocks, axis), axis)


def total_low(parts):
    if len(parts) == 1:
        return parts[0]
    return total(parts).astype(BF16)


def total(parts):
    out = parts[0].astype(F32)
    for p in parts[1:]:
        out = out + p.astype(F32)
    return out


def split_last(values):
    return values[:-1], values[-1]


def send_pairs(pairs, first, axis):
    return [v if first + k == 0 else swap(v, axis, 2 * (first + k)) for k, v in enumerate(pairs)]


def pass_on(direct, axis):
    blk = direct[0].shape[0] // 2
    return swap(jnp.concatenate([v[blk:] for v in direct], axis=0), axis, 1)


def scatter_xy(left):
    bits = halving_bits(lax.axis_size("tensor"))
    for bit in bits[2:]:
        left = scatter_step(left, "tensor", bit)
    own, other = total_low(left[0]), total_low(left[2])
    half = own.shape[0] // 2
    nt, ne = lax.axis_size("tensor"), lax.axis_size("expert")
    both = [(e * nt + t, (e ^ 1) * nt + (t ^ 2)) for e in range(ne) for t in range(nt)]
    return [
        own[:half],
        lax.ppermute(other[half:], ("expert", "tensor"), both),
        swap(own[half:], "expert", 1),
        swap(other[:half], "tensor", 2),
    ]


def places(bits):
    n = 1 << len(bits)
    return [sum(b for k, b in enumerate(bits) if p & (n >> (k + 1))) for p in range(n)]


def exchange_sum(value, axis, bits):
    offsets = places(bits)
    step = value.shape[0] // len(offsets)
    parts = [value[p * step : (p + 1) * step] for p in range(len(offsets))]
    return total_low([parts[0]] + [swap(v, axis, o) for v, o in zip(parts[1:], offsets[1:])])


def exchange_all(value, axis, bits):
    return jnp.concatenate([value] + [swap(value, axis, o) for o in places(bits)[1:]], 0)


def sum_rest(value, axis):
    for group in groups_of(axis):
        value = exchange_sum(value, axis, group)
    return value


def groups_of(axis):
    bits = halving_bits(lax.axis_size(axis))
    return [bits[k : k + 2] for k in range(1, len(bits), 2)]


def share_rest(value, axis):
    for group in groups_of(axis)[::-1]:
        value = exchange_all(value, axis, group)
    return value


def shards(
    block_in,
    out_grad,
    routes,
    kept_pairs,
    ln1_gain,
    ln1_bias,
    w_query,
    w_key,
    w_value,
    w_attn_out,
    ln2_gain,
    ln2_bias,
    w_router,
    w_expert_in,
    w_expert_out,
):
    nt, ne = lax.axis_size("tensor"), lax.axis_size("expert")
    width = block_in.shape[1]
    z = Sizes(
        nt, ne, width, block_in.shape[0], routes.shape[0], w_query.shape[1], w_expert_in.shape[2]
    )
    lp, hw, hid, blk = z.lp, z.hw, z.hid, z.blk
    me_t, me_e = lax.axis_index("tensor"), lax.axis_index("expert")
    who = jnp.stack([me_t, me_e]).astype(I32)
    body = functools.partial

    rows_low = shape((z.rows, width), BF16)
    pair = shape((2 * blk, width), BF16)
    quarter, half = ne // 4, ne // 2

    dy_low, attn_own = call(
        body(first_body, z),
        [rows_low, shape((width, 4 * hw), BF16)],
        [who, *map(Far, (out_grad, w_query, w_key, w_value, w_attn_out))],
        [pltpu.VMEM((z.rows, width), F32)],
    )
    dy_part = gather_far(dy_low, "tensor")
    lines = jnp.pad(
        jnp.stack([routes.T, kept_pairs.T]).reshape(2, 2, z.chunks, IMAGE_TOKENS),
        ((0, 0), (0, 0), (0, 0), (0, lp - IMAGE_TOKENS)),
        constant_values=-1,
    )
    expert_own, pos, keep, post = call(
        body(early_body, z),
        [
            shape((2 * width, hid), BF16),
            shape((z.chunks, ne, lp), I32),
            shape((z.chunks, ne, lp), F32),
            shape((z.chunks, lp, ne), I32),
        ],
        [who, Far(w_expert_in[0]), Far(w_expert_out[0]), lines[0], lines[1].astype(F32)],
        after=[dy_low],
    )
    dy_far = hold(dy_part[1:], [pos])
    dy_rows = gather_near([dy_part[0], *dy_far], "tensor")
    attn_part = gather_far(hold([attn_own], dy_far)[0], "tensor")
    dy_sent = call(
        body(dispatch_dy_body, z),
        [pair] * quarter,
        [who, pos, *dy_rows],
        [pltpu.VMEM((half * blk, width), F32)],
    )
    dy_in = send_pairs(dy_sent, quarter, "expert")
    attn_w = gather_near(attn_part[:1] + hold(attn_part[1:], dy_sent[:1]), "tensor")

    norms = jnp.stack([ln1_gain, ln1_bias, ln2_gain, ln2_bias])
    wr = w_router.T
    second, (resid, h1, *rest) = split_at(z.images, call(
        body(attend_body, z),
        [
            *[shape((lp, width), BF16)] * z.images,
            shape((z.rows, width), F32),
            rows_low,
            *[shape((z.rows, 3 * hw), BF16)] * nt,
            *[shape((z.rows, hw), BF16)] * nt,
            *[shape((z.images * z.hpb, lp, lp), BF16)] * nt,
        ],
        [who, Far(block_in), norms, Far(wr), *attn_w],
        [
            pltpu.VMEM((z.rows, width), F32),
            pltpu.VMEM((lp, width), F32),
            pltpu.VMEM((ne, width), F32),
        ],
    ))
    qkv, ctx, probs = rest[:nt], rest[nt : 2 * nt], rest[2 * nt :]
    rows_part = [gather_far(v, "tensor") for v in second]
    far = nt // 2 - 1
    rest = hold([w for v in rows_part for w in v[1:]] + dy_in, [])
    rows = [
        gather_near([v[0], *rest[i * far : (i + 1) * far]], "tensor")
        for i, v in enumerate(rows_part)
    ]
    rows = [v[r] for r in range(nt) for v in rows]
    dy_in = rest[z.images * far :]
    dy_passed = pass_on(dy_in, "expert")
    sent = call(
        body(dispatch_body, z),
        [pair] * half + [shape((blk, width), BF16)] * half,
        [who, pos, keep, *rows, *dy_rows],
        [
            pltpu.VMEM((z.slots, width), F32),
            pltpu.VMEM((half * blk, width), F32),
            pltpu.VMEM((2 * ne, z.slots), F32),
        ],
    )
    expert_own = hold([expert_own], rest[:1])[0]
    *sent, dy_passed, own_core = hold([*sent, dy_passed, swap(expert_own, "tensor", 1)], [])
    far_in = [swap(v, "expert", half + k) for k, v in enumerate(sent[half:])]
    near_in = hold(sent[1:half], far_in)
    near_in = [sent[0]] + [swap(v, "expert", 1 + k) for k, v in enumerate(near_in)]
    w_part = gather_far(expert_own, "tensor")
    rest = hold(w_part[1:], far_in)
    expert_w = [w_part[0], own_core, *gather_near(rest, "tensor")]

    size = half * blk
    passed = [
        *[shape((size, hid), BF16)] * (2 * nt),
        shape((size, width), BF16),
        shape((1, 128), F32),
    ]
    held = [
        pltpu.VMEM((size, width), BF16),
        pltpu.VMEM((size, 128), F32),
        pltpu.VMEM((size, width), F32),
        pltpu.VMEM((size, width), F32),
    ]
    far = call(
        body(expert_body, z, False, half),
        [pair] * half + passed,
        [who, *far_in, *dy_in, dy_passed, *expert_w],
        held,
    )
    far_out, far_mixed, (*far_hidden, far_g, far_top) = far[:quarter], far[quarter:half], far[half:]
    near = call(
        body(expert_body, z, True, half),
        [pair] * half + passed,
        [who, *near_in, *expert_w, far_top],
        held,
    )
    near_out, (*near_hidden, near_g, tops) = near[:half], near[half:]
    far_out = send_pairs(far_out, quarter, "expert")
    near_out = [v if k == 0 else swap(v, "expert", k) for k, v in enumerate(near_out)]
    expert_grads = call(
        body(expert_weights_body, z),
        [shape((width, hid), BF16)] * (2 * nt),
        [who, *near_in, *far_in, near_g, far_g, *near_hidden, *far_hidden],
        [pltpu.VMEM((2, width, size), BF16), pltpu.VMEM((2, width, size), BF16)],
    )
    far_out = hold(far_out, expert_grads[:1])
    far_out.append(pass_on(far_out, "expert"))
    first_near = scatter_near(expert_grads[:nt], "tensor")
    second_near = scatter_near(expert_grads[nt:], "tensor")

    partial = call(
        body(combine_body, z, True),
        [rows_low] * nt + [shape((ne, width), F32)],
        [who, post, keep, Far(wr), *rows, *near_out, *far_out],
        [pltpu.VMEM((z.slots, width), BF16)],
    )
    router_part = partial[nt]
    dz_near = scatter_near(partial[:nt], "tensor")
    dz_parts = scatter_far(dz_near, "tensor")
    mixed = send_pairs(far_mixed, quarter, "expert")
    second_parts = scatter_far(hold_far(second_near, dz_parts[-1:]), "tensor")

    pay = shape((ne, z.prow, z.wide), BF16)
    buffers = [pltpu.VMEM((ne, z.crow, z.wide), F32), pltpu.VMEM((ne, 8, z.wide), F32)]
    per_head = shape((z.rows, hw), BF16)
    outs = call(
        body(back_one_body, z, len(dz_parts)),
        [shape((z.rows, width), F32)] + [per_head] * (2 * nt) + [pay] * nt,
        [who, Far(out_grad), norms, resid, router_part, h1, *dz_parts, *attn_w, *probs, *ctx],
        [pltpu.VMEM((z.rows, width), F32), pltpu.VMEM((8 + ne, width), F32), *buffers],
    )
    dresid, dctx, dv = outs[0], outs[1:][:nt], outs[1 + nt :][:nt]
    one_near = scatter_near(outs[1 + 2 * nt :], "tensor")
    outs = call(
        body(back_two_body, z),
        [Far(shape((z.tok_dev, width), F32))] + [pay] * nt,
        [who, Far(block_in), norms, h1, *qkv, *dctx, *probs, *dv, dresid, *attn_w],
        [pltpu.VMEM((z.rows, width), F32), pltpu.VMEM((8, width), F32), *buffers],
        after=[one_near[nt // 2][0]],
    )
    input_grad = outs[0]
    one_parts = scatter_far(one_near, "tensor")
    far = [r for r in first_near if r]
    two = hold(
        [
            *outs[1:],
            one_parts[-1],
            second_parts[1],
            first_near[0][1],
            *[first_near[r][0] for r in far],
        ],
        [],
    )
    two, (one_parts[-1], second_parts[1], first_near[0][1], *rest) = split_at(nt, two)
    first_near.update((r, [v]) for r, v in zip(far, rest))
    one = total_low(one_parts)
    one = total_low([one[:half], swap(one[half:], "expert", 1)])
    two_near = scatter_near(two, "tensor")
    two_parts = scatter_xy(two_near)

    merged = jnp.concatenate([one, total_low(two_parts)], axis=2)
    merged, second_parts[-1], *mixed = hold([merged, second_parts[-1], *mixed], [])
    passed = pass_on(mixed, "expert")
    mixed_part = call(
        body(combine_body, z, False),
        [rows_low] * nt,
        [who, post, *near_out, *mixed, passed],
        [pltpu.VMEM((z.slots, width), BF16)],
    )
    value = sum_rest(merged, "expert")
    first_parts = scatter_far(hold_far(first_near, two_parts[-1:]), "tensor")
    value, first_parts[-1] = hold([value, first_parts[-1]], [])
    value = share_rest(value, "expert")
    mixed_near = scatter_near(mixed_part, "tensor")
    far = [r for r in mixed_near if r]
    value, *rest = hold([value, *[mixed_near[r][0] for r in far]], [])
    mixed_near.update((r, [v]) for r, v in zip(far, rest))
    mixed_parts = scatter_far(mixed_near, "tensor")
    sums = [value, swap(value, "expert", 1)]
    grad_first, grad_second = call(
        body(expert_grads_body, z, len(first_parts)),
        [Far(shape((width, hid), F32)), Far(shape((hid, width), F32))],
        [who, *first_parts, *second_parts],
    )
    block_out = call(
        body(finish_body, z, len(mixed_parts)),
        Far(shape((z.tok_dev, width), F32)),
        [who, resid, *mixed_parts],
        [pltpu.VMEM((z.rows, width), F32)],
    )

    head = Far(shape((width, hw), F32))
    grad_q, grad_k, grad_v, grad_o, n1, n2, n3, n4, router_grad = call(
        body(last_body, z),
        [head] * 3
        + [Far(shape(v, F32)) for v in ((hw, width), *[(1, width)] * 4, (ne, width))],
        [who, *sums],
        [pltpu.VMEM((ne, z.crow, 2 * z.wide), F32), pltpu.VMEM((ne, 8, 2 * z.wide), F32)],
        after=[place(v, pltpu.HBM) for v in (grad_first,)],
    )
    head_maxima = lax.dynamic_slice_in_dim(tops[0], me_t * z.hpb, z.hpb, 0)
    factor = jnp.repeat(jnp.sqrt(jnp.minimum(1.0, clip_limit / head_maxima)), HEAD_DIM)
    return (
        block_out,
        input_grad,
        n1[0],
        n2[0],
        grad_q,
        grad_k,
        grad_v,
        grad_o,
        n3[0],
        n4[0],
        router_grad.T,
        grad_first[None],
        grad_second[None],
        head_maxima,
        w_query * factor[None, :],
        w_key * factor[None, :],
    )


def solution(mesh):
    placed = (
        P(("expert", "tensor"), None),
        P(("expert", "tensor"), None),
        P("expert", None),
        P("expert", None),
        P(),
        P(),
        P(None, "tensor"),
        P(None, "tensor"),
        P(None, "tensor"),
        P("tensor", None),
        P(),
        P(),
        P(),
        P("expert", None, "tensor"),
        P("expert", "tensor", None),
    )
    return jax.shard_map(
        shards,
        mesh=mesh,
        in_specs=placed,
        out_specs=(
            P(("expert", "tensor"), None),
            P(("expert", "tensor"), None),
            P(),
            P(),
            P(None, "tensor"),
            P(None, "tensor"),
            P(None, "tensor"),
            P("tensor", None),
            P(),
            P(),
            P(),
            P("expert", None, "tensor"),
            P("expert", "tensor", None),
            P("tensor"),
            P(None, "tensor"),
            P(None, "tensor"),
        ),
        check_vma=False,
    )
```

```python
import functools

import jax
import jax.numpy as jnp
from jax import lax
from jax.experimental import pallas as pl
from jax.experimental.pallas import tpu as pltpu
from jax.sharding import PartitionSpec as P

HEAD_DIM = 64
IMAGE_TOKENS = 197
SPARE = 200
TOP_ROW = 197

F32 = jnp.float32
BF16 = jnp.bfloat16
I32 = jnp.int32

clip_limit = 4.0
norm_eps = 1e-06
low_value = -1e30


def round_up(value, unit):
    return -(-value // unit) * unit


def dot_nn(a, b):
    return lax.dot_general(a, b, (((1,), (0,)), ((), ())), preferred_element_type=F32)


def dot_nt(a, b):
    return lax.dot_general(a, b, (((1,), (1,)), ((), ())), preferred_element_type=F32)


def dot_tn(a, b):
    return lax.dot_general(a, b, (((0,), (0,)), ((), ())), preferred_element_type=F32)


def iota(shape, dim):
    return lax.broadcasted_iota(I32, shape, dim)


def split2(v):
    high = v.astype(BF16).astype(F32)
    return high, (v - high).astype(BF16).astype(F32)


def normalize(rows):
    center = jnp.mean(rows, axis=-1, keepdims=True)
    offset = rows - center
    rstd = lax.rsqrt(jnp.mean(offset * offset, axis=-1, keepdims=True) + norm_eps)
    return offset * rstd, rstd


def norm_back(grad, unit, rstd):
    return rstd * (
        grad
        - jnp.mean(grad, axis=-1, keepdims=True)
        - unit * jnp.mean(grad * unit, axis=-1, keepdims=True)
    )


def halving_bits(n):
    return [1 << k for k in range(n.bit_length() - 1)]


class Sizes:
    def __init__(self, nt, ne, width, tok_dev, tok_group, head_cols, hidden):
        self.nt, self.ne, self.width = nt, ne, width
        self.tok_dev = tok_dev
        self.images = tok_dev // IMAGE_TOKENS
        self.lp = round_up(SPARE + ne, 16)
        self.rows = self.images * self.lp
        self.chunks = nt * self.images
        self.cap = 5 * tok_group // (2 * ne) + 1
        self.spr = -(-self.cap // nt)
        need = self.spr + 2
        self.blk = next((b for b in (16, 32, 64, 128) if b >= need), round_up(need, 128))
        self.epl = 128 // self.blk
        self.hw = head_cols
        self.hpb = head_cols // HEAD_DIM
        self.hid = hidden
        self.slots = ne * self.blk
        self.wide = 2 * self.hw
        self.pieces = width // self.wide
        self.crow = width // ne
        self.prow = self.crow + 8
        bits = halving_bits(ne)
        self.offset = places(bits)


SM = pl.BlockSpec(memory_space=pltpu.SMEM)
VM = pl.BlockSpec(memory_space=pltpu.VMEM)
ANY = pl.BlockSpec(memory_space=pl.ANY)


class Far:
    def __init__(self, value):
        self.value = value


class Given:
    def __init__(self, ref, copy):
        self.ref, self.copy = ref, copy
        copy.start()

    def wait(self):
        if self.copy is not None:
            self.copy.wait()
            self.copy = None

    def __getitem__(self, at):
        self.wait()
        return self.ref[at]


def place(value, space):
    return pltpu.with_memory_space_constraint(value, space)


def call(body, outs, args, scratch=(), after=()):
    skip = len(after)
    keep = lax.axis_size("tensor") <= 4
    vmem = 12 if keep else 60
    single = not isinstance(outs, list)
    flat = [outs] if single else outs
    far = [k for k, a in enumerate(args) if isinstance(a, Far)]

    def run(*refs):
        ins, refs = [refs[0], *refs[1 + skip : skip + len(args)]], refs[skip + len(args) :]
        results, refs = refs[: len(flat)], refs[len(flat) :]
        own, refs = refs[: len(scratch)], refs[len(scratch) :]
        for n, k in enumerate(far):
            ins[k] = Given(refs[n], pltpu.make_async_copy(ins[k], refs[n], refs[-1].at[n]))
        body(*ins, *results, *own)
        for k in far:
            ins[k].wait()

    extra = [pltpu.VMEM(args[k].value.shape, args[k].value.dtype) for k in far]
    if far:
        extra.append(pltpu.SemaphoreType.DMA((len(far),)))
    got = pl.pallas_call(
        run,
        out_shape=[
            o.value if isinstance(o, Far) else pltpu.VMEM(o.shape, o.dtype) if keep else o
            for o in flat
        ],
        in_specs=[SM] + [ANY] * skip + [ANY if k in far else VM for k in range(1, len(args))],
        out_specs=[VM] * len(flat),
        scratch_shapes=[*scratch, *extra],
        compiler_params=pltpu.CompilerParams(vmem_limit_bytes=vmem * 1024 * 1024),
    )(
        args[0],
        *after,
        *[
            place(a.value, pltpu.HBM) if isinstance(a, Far) else place(a, pltpu.VMEM) if keep else a
            for a in args[1:]
        ],
    )
    return got[0] if single else list(got)


def hold(values, after):
    n, m = len(values), len(after)

    def run(*refs):
        pass

    out = pl.pallas_call(
        run,
        out_shape=[shape(v.shape, v.dtype) for v in values],
        in_specs=[ANY] * (n + m),
        out_specs=[ANY] * n,
        input_output_aliases={k: k for k in range(n)},
        compiler_params=pltpu.CompilerParams(vmem_limit_bytes=1024 * 1024),
    )(*values, *after)
    return list(out)


def shape(dims, kind):
    return jax.ShapeDtypeStruct(dims, kind)


def first_body(z, who, dy_ref, q_ref, k_ref, v_ref, o_ref, low_ref, out_ref, pad):
    hw = z.hw
    pad[...] = jnp.zeros(pad.shape, F32)
    for i in range(z.images):
        pad[i * z.lp : i * z.lp + IMAGE_TOKENS, :] = dy_ref[
            i * IMAGE_TOKENS : (i + 1) * IMAGE_TOKENS, :
        ]
    low_ref[...] = pad[...].astype(BF16)
    for n, ref in enumerate((q_ref, k_ref, v_ref)):
        out_ref[:, n * hw : (n + 1) * hw] = ref[...].astype(BF16)
    out_ref[:, 3 * hw : 4 * hw] = o_ref[...].T.astype(BF16)


def early_body(z, who, in_ref, out_ref, route_ref, kept_ref, *refs):
    w_ref, pos_ref, keep_ref, post_ref = refs
    w_ref[0 : z.width, :] = in_ref[...].astype(BF16)
    w_ref[z.width : 2 * z.width, :] = out_ref[...].T.astype(BF16)
    me_t, me_e = who[0], who[1]
    named = jnp.bitwise_xor(iota((z.ne, z.lp), 0), me_e)
    before = jnp.where(iota((z.lp, z.lp), 0) < iota((z.lp, z.lp), 1), 1.0, 0.0).astype(BF16)
    count = jnp.zeros((z.ne, 1), F32)
    for c in range(z.chunks):
        block, img = c // z.images, c % z.images
        first = route_ref[0, c : c + 1, :] == named
        other = route_ref[1, c : c + 1, :] == named
        hit = jnp.where(first | other, 1.0, 0.0)
        place = dot_nn(hit.astype(BF16), before) + count
        count = count + jnp.sum(hit, axis=1, keepdims=True)
        at = jnp.bitwise_xor(block, me_t) * z.images + img
        place = jnp.where(hit > 0, place, -1.0)
        pos_ref[at] = place.astype(I32)
        post_ref[at] = place.T.astype(I32)
        keep_ref[at] = jnp.where(first, kept_ref[0, c : c + 1, :], 0.0) + jnp.where(
            other, kept_ref[1, c : c + 1, :], 0.0
        )


def attend_body(z, who, x_ref, ln_ref, wr_ref, *refs):
    nt, lp, hw = z.nt, z.lp, z.hw
    weights = refs[:nt]
    z_refs, refs = refs[nt : nt + z.images], refs[nt + z.images :]
    resid_ref, h1_ref, refs = refs[0], refs[1], refs[2:]
    qkv_ref, ctx_ref, p_ref = refs[:nt], refs[nt : 2 * nt], refs[2 * nt : 3 * nt]
    xp, zb, pt = refs[3 * nt :]
    me_t = who[0]
    xp[...] = jnp.zeros(xp.shape, F32)
    for i in range(z.images):
        xp[i * lp : i * lp + IMAGE_TOKENS, :] = x_ref[
            i * IMAGE_TOKENS : (i + 1) * IMAGE_TOKENS, :
        ]
    unit, _ = normalize(xp[...])
    h1 = (unit * ln_ref[0:1, :] + ln_ref[1:2, :]).astype(BF16)
    h1_ref[...] = h1
    head_of = iota((lp, hw), 1) // HEAD_DIM
    real = iota((lp, lp), 1) < IMAGE_TOKENS
    real_row = iota((lp, 1), 0) < IMAGE_TOKENS
    lane = iota((1, 128), 1)
    tops = jnp.full((1, 128), low_value, F32)
    attn = jnp.zeros((z.rows, z.width), F32)
    for r in range(nt):
        qkv = dot_nn(h1, weights[r][:, 0 : 3 * hw]).astype(BF16)
        qkv_ref[r][...] = qkv
        ctxs = []
        for i in range(z.images):
            at = slice(i * lp, (i + 1) * lp)
            q, k, v = (qkv[at, n * hw : (n + 1) * hw] for n in range(3))
            ctx = jnp.zeros((lp, hw), F32)
            for j in range(z.hpb):
                mine = head_of == j
                s = dot_nt(jnp.where(mine, q, jnp.zeros_like(q)), k) * (HEAD_DIM**-0.5)
                s = jnp.where(real, s, low_value)
                peak = jnp.max(s, axis=1, keepdims=True)
                top = jnp.max(jnp.where(real_row, peak, low_value), axis=0, keepdims=True)
                head = jnp.bitwise_xor(me_t, r) * z.hpb + j
                tops = jnp.where(lane == head, jnp.maximum(tops, top), tops)
                e = jnp.exp(s - peak)
                p = (e * (1.0 / jnp.sum(e, axis=1, keepdims=True))).astype(BF16)
                p_ref[r][i * z.hpb + j] = p
                ctx = jnp.where(mine, dot_nn(p, v), ctx)
            ctxs.append(ctx.astype(BF16))
        ctx = jnp.concatenate(ctxs, axis=0)
        ctx_ref[r][...] = ctx
        attn = attn + dot_nt(ctx, weights[r][:, 3 * hw : 4 * hw])
    resid = xp[...] + attn
    resid_ref[...] = resid
    unit, _ = normalize(resid)
    second = unit * ln_ref[2:3, :] + ln_ref[3:4, :]
    w_hi, w_lo = (v.astype(BF16) for v in split2(router_rows(z, who, wr_ref)))
    row = iota((lp, 1), 0)
    t_hi = tops.astype(BF16).astype(F32)
    t_mid = (tops - t_hi).astype(BF16).astype(F32)
    t_lo = tops - t_hi - t_mid
    for i in range(z.images):
        part = second[i * lp : (i + 1) * lp]
        s_hi, s_lo = (v.astype(BF16) for v in split2(part))
        logits = dot_nt(w_hi, s_hi) + (dot_nt(w_hi, s_lo) + dot_nt(w_lo, s_hi))
        e = jnp.exp(logits - jnp.max(logits, axis=0, keepdims=True))
        p_hi, p_lo = split2(e / jnp.sum(e, axis=0, keepdims=True))
        pt[...] = jnp.zeros(pt.shape, F32)
        pt[:, 0:lp] = p_hi
        pt[:, 256 : 256 + lp] = p_lo
        zb[...] = jnp.where(row < IMAGE_TOKENS, part, 0.0)
        for n, t in enumerate((t_hi, t_mid, t_lo)):
            zb[TOP_ROW + n : TOP_ROW + n + 1, 0:128] = t
        zb[SPARE : SPARE + z.ne, :] = pt[...]
        z_refs[i][...] = zb[...].astype(BF16)


def router_rows(z, who, ref):
    return jnp.concatenate(
        [ref[pl.ds(jnp.bitwise_xor(e, who[1]), 1), :] for e in range(z.ne)], axis=0
    )


def split_at(n, values):
    return values[:n], values[n:]


def tail_rows(z, ref):
    start = (TOP_ROW // 16) * 16
    return ref[start : z.lp, :].astype(F32), start


def probs_of(z, ref):
    tail, start = tail_rows(z, ref)
    both = tail[SPARE - start : SPARE - start + z.ne]
    return both[:, 0 : z.lp] + both[:, 256 : 256 + z.lp]


def hot_rows(z, who, pos_ref, c, first, last):
    slot = iota((z.blk, z.lp), 0)
    slot = jnp.where(slot < z.spr, slot + who[0] * z.spr, -2)
    return jnp.concatenate(
        [
            jnp.where(pos_ref[c, e : e + 1, :] == slot, 1.0, 0.0).astype(BF16)
            for e in range(first, last)
        ],
        axis=0,
    )


def dispatch_dy_body(z, who, pos_ref, *refs):
    nt, ne, lp, blk = z.nt, z.ne, z.lp, z.blk
    rows, outs, acc = refs[:nt], refs[nt : nt + ne // 4], refs[nt + ne // 4]
    for c in range(z.chunks):
        r, i = c // z.images, c % z.images
        hot = hot_rows(z, who, pos_ref, c, ne // 2, ne)
        part = dot_nn(hot, rows[r][i * lp : (i + 1) * lp, :])
        acc[...] = part if c == 0 else acc[...] + part
    for k in range(ne // 4):
        outs[k][...] = acc[2 * k * blk : 2 * (k + 1) * blk, :].astype(BF16)


def dispatch_body(z, who, pos_ref, keep_ref, *refs):
    nt, ne, lp, blk = z.nt, z.ne, z.lp, z.blk
    rows, dy_rows, refs = refs[: z.chunks], refs[z.chunks :][:nt], refs[z.chunks + nt :]
    outs, (acc, dy_acc, gacc) = refs[:ne], refs[ne:]
    half = ne // 2
    tops = None
    for c in range(z.chunks):
        r, i = c // z.images, c % z.images
        hot = hot_rows(z, who, pos_ref, c, 0, ne)
        part = dot_nn(hot[: half * blk], dy_rows[r][i * lp : (i + 1) * lp, :])
        dy_acc[...] = part if c == 0 else dy_acc[...] + part
        part = dot_nn(hot, rows[c][...])
        acc[...] = part if c == 0 else acc[...] + part
        g_hi, g_lo = split2(probs_of(z, rows[c]) * keep_ref[c])
        both = jnp.concatenate([g_hi, g_lo], axis=0).astype(BF16)
        part = dot_nt(both, hot)
        gacc[...] = part if c == 0 else gacc[...] + part
        if i == 0:
            tail, start = tail_rows(z, rows[c])
            three = tail[TOP_ROW - start : TOP_ROW - start + 3, 0:128]
            top = three[0:1] + three[1:2] + three[2:3]
            tops = top if tops is None else jnp.maximum(tops, top)
    t_hi = tops.astype(BF16).astype(F32)
    t_mid = (tops - t_hi).astype(BF16).astype(F32)
    t_lo = tops - t_hi - t_mid
    none = jnp.zeros((1, 128), F32)
    top_row = jnp.concatenate([t_hi, t_mid, t_lo, none], axis=1)
    row = iota((blk, 1), 0)
    part_of = iota((1, 128), 1) // blk
    for e in range(ne):
        tile = slice((e // z.epl) * 128, (e // z.epl) * 128 + 128)
        g_hi = jnp.where(part_of == e % z.epl, gacc[e : e + 1, tile], 0.0)
        g_lo = jnp.where(part_of == e % z.epl, gacc[ne + e : ne + e + 1, tile], 0.0)
        gates = jnp.concatenate([g_hi, g_lo, none, none], axis=1)
        block = acc[e * blk : (e + 1) * blk, :]
        block = jnp.where(row == z.spr, gates, block)
        block = jnp.where(row == z.spr + 1, top_row, block)
        outs[e][0:blk, :] = block.astype(BF16)
        if e < half:
            outs[e][blk : 2 * blk, :] = dy_acc[e * blk : (e + 1) * blk, :].astype(BF16)


class Part:
    def __init__(self, ref, first):
        self.ref, self.first = ref, first

    def rows(self, start, stop):
        return self.ref[self.first + start : self.first + stop, :]

    def put(self, value):
        self.ref[self.first : self.first + value.shape[0], :] = value


def blocks_of(z, direct, passed, size=1, at=0):
    out = []
    for k, ref in enumerate(direct):
        out += [Part(ref, at * z.blk), Part(passed, (k * size + at) * z.blk)]
    return out


def spare_pair(z, part):
    start = (z.spr // 16) * 16
    tail = part.rows(start, z.blk).astype(F32)
    return tail[z.spr - start : z.spr - start + 1], tail[z.spr - start + 1 : z.spr - start + 2]


def expert_body(z, near, count, who, *refs):
    nt, ne, blk, hid, width = z.nt, z.ne, z.blk, z.hid, z.width
    half = count // 2
    rows_in = [Part(ref, 0) for ref in refs[:count]]
    if near:
        dy_in, refs = [Part(ref, blk) for ref in refs[:count]], refs[count:]
    else:
        refs = refs[count:]
        dy_in, refs = blocks_of(z, refs[:half], refs[half]), refs[half + 1 :]
    weights, refs = refs[:nt], refs[nt:]
    w = z.width
    if near:
        far_top, refs = refs[0], refs[1:]
        back, mixed = ([Part(ref, at * blk) for ref in refs[:count]] for at in range(2))
        refs = refs[count:]
    else:
        back, mixed = (
            [Part(ref, at * blk) for ref in some for at in range(2)]
            for some in (refs[:half], refs[half:count])
        )
        refs = refs[count:]
    act, du, refs = refs[:nt], refs[nt : 2 * nt], refs[2 * nt :]
    g, top_ref, rows, gate, o_acc, d_acc = refs
    real = iota((blk, 1), 0) < z.spr
    diag = iota((blk, 128), 0) == iota((blk, 128), 1) % blk
    tops = far_top[...] if near else None
    for n in range(count):
        at = slice(n * blk, (n + 1) * blk)
        rows[at, :] = jnp.where(real, rows_in[n].rows(0, blk), jnp.zeros((), BF16))
        gates, top = spare_pair(z, rows_in[n])
        top = top[:, 0:128] + top[:, 128:256] + top[:, 256:384]
        tops = top if tops is None else jnp.maximum(tops, top)
        line = gates[:, 0:128] + gates[:, 128:256]
        column = jnp.sum(jnp.where(diag, line, 0.0), axis=1, keepdims=True)
        gate[at, :] = jnp.broadcast_to(column, (blk, 128))
    top_ref[...] = tops
    u_first = dot_nn(rows[...], weights[0][0:w, :])
    for n in range(count):
        at = slice(n * blk, (n + 1) * blk)
        g[at, :] = (gate[at, 0:1] * dy_in[n].rows(0, blk).astype(F32)).astype(BF16)
    for r in range(nt):
        u = dot_nn(rows[...], weights[r][0:w, :]) if r else u_first
        second_w = weights[r][w : 2 * w, :]
        cube = 0.7978845608028654 * 0.044715 * u * u
        t = jnp.tanh(u * (0.7978845608028654 + cube))
        h = 0.5 + 0.5 * t
        a = (u * h).astype(BF16)
        slope = h + 2.0 * h * (1.0 - h) * u * (0.7978845608028654 + 3.0 * cube)
        d = (dot_nn(g[...], second_w) * slope).astype(BF16)
        act[r][...] = a
        du[r][...] = d
        o = dot_nt(a, second_w)
        b = dot_nt(d, weights[r][0:w, :])
        o_acc[...] = o if r == 0 else o_acc[...] + o
        d_acc[...] = b if r == 0 else d_acc[...] + b
    row = iota((blk, 1), 0)
    none = jnp.zeros((1, 128), F32)
    for n in range(count):
        at = slice(n * blk, (n + 1) * blk)
        o = o_acc[at, :]
        dgate = jnp.sum(o * dy_in[n].rows(0, blk).astype(F32), axis=1, keepdims=True)
        line = jnp.sum(jnp.where(diag, dgate, 0.0), axis=0, keepdims=True)
        hi, lo = split2(line)
        line = jnp.concatenate([hi, lo, none, none], axis=1)
        back[n].put(jnp.where(row == z.spr, line, d_acc[at, :]).astype(BF16))
        mixed[n].put((gate[at, 0:1] * o).astype(BF16))


def expert_weights_body(z, who, *refs):
    nt, ne, blk, hid = z.nt, z.ne, z.blk, z.hid
    rows_in, refs = [Part(ref, 0) for ref in refs[:ne]], refs[ne:]
    g, refs = refs[:2], refs[2:]
    act, du = (refs[:nt], refs[2 * nt : 3 * nt]), (refs[nt : 2 * nt], refs[3 * nt : 4 * nt])
    one, two, (rows_t, g_t) = refs[4 * nt : 5 * nt], refs[5 * nt : 6 * nt], refs[6 * nt :]
    real = iota((blk, 1), 0) < z.spr
    rows = [jnp.where(real, part.rows(0, blk), jnp.zeros((), BF16)) for part in rows_in]
    half = ne // 2
    for k in range(2):
        rows_t[k] = jnp.concatenate(rows[k * half : (k + 1) * half], axis=0).T
        g_t[k] = g[k][...].T
    for r in range(nt):
        first = dot_nn(rows_t[0], du[0][r][...]) + dot_nn(rows_t[1], du[1][r][...])
        one[r][...] = first.astype(BF16)
        second = dot_nn(g_t[0], act[0][r][...]) + dot_nn(g_t[1], act[1][r][...])
        two[r][...] = second.astype(BF16)


def hot_columns(z, post_ref, c, base):
    lane = iota((z.lp, 128), 1)
    slot = lane % z.blk
    slot = jnp.where(slot < z.spr, slot + base, -2)
    tiles = []
    for p in range(z.ne // z.epl):
        column = post_ref[c, :, p * z.epl : p * z.epl + 1]
        pick = jnp.broadcast_to(column, (z.lp, 128))
        for n in range(1, z.epl):
            e = p * z.epl + n
            pick = jnp.where(lane // z.blk == n, post_ref[c, :, e : e + 1], pick)
        tiles.append(jnp.where(pick == slot, 1.0, 0.0).astype(BF16))
    return jnp.concatenate(tiles, axis=1)


def combine_body(z, with_router, which, who, post_ref, *refs):
    nt, ne, lp, blk = len(which), z.ne, z.lp, z.blk
    more = with_router and 0 in which
    base = who[0] * z.spr
    if with_router:
        keep_ref, wr_ref, refs = refs[0], refs[1], refs[2:]
        rows, refs = refs[: nt * z.images], refs[nt * z.images :]
        if more:
            so_far, refs = refs[0], refs[1:]
    quarter = ne // 4
    at = 0 if with_router else blk
    blocks, refs = [Part(ref, at) for ref in refs[: ne // 2]], refs[ne // 2 :]
    blocks, refs = blocks + blocks_of(z, refs[:quarter], refs[quarter]), refs[quarter + 1 :]
    outs, refs = refs[:nt], refs[nt:]
    if with_router:
        gr_ref, refs = refs[0], refs[1:]
    stack = refs[0]
    for e in range(ne):
        stack[e * blk : (e + 1) * blk, :] = blocks[e].rows(0, blk)
    if with_router:
        row = iota((ne, 128), 0)
        half = iota((ne, 128), 1) // blk
        tiles = []
        for p in range(ne // z.epl):
            hi = jnp.zeros((ne, 128), F32)
            lo = jnp.zeros((ne, 128), F32)
            for n in range(z.epl):
                e = p * z.epl + n
                line, _ = spare_pair(z, blocks[e])
                own = (row == e) & (half == n)
                hi = jnp.where(own, line[:, 0:128], hi)
                lo = jnp.where(own, line[:, 128:256], lo)
            tiles.append(jnp.concatenate([hi, lo], axis=0))
        dgate = jnp.concatenate(tiles, axis=1).astype(BF16)
        unit = jnp.where(iota((lp, lp), 0) == iota((lp, lp), 1), 1.0, 0.0).astype(BF16)
        wr = router_rows(z, who, wr_ref).astype(BF16)
        wr = jnp.concatenate([wr, wr], axis=0)
        total = jnp.zeros((2 * ne, z.width), F32)
    for n in range(nt * z.images):
        r, i = n // z.images, n % z.images
        c = which[r] * z.images + i
        at = slice(i * lp, (i + 1) * lp)
        hot = hot_columns(z, post_ref, c, base)
        part = dot_nn(hot, stack[...])
        if with_router:
            both = dot_nt(dgate, hot)
            dp = (both[0:ne] + both[ne : 2 * ne]) * keep_ref[c]
            pr = probs_of(z, rows[n])
            dl = pr * (dp - jnp.sum(pr * dp, axis=0, keepdims=True))
            dl = jnp.concatenate(split2(dl), axis=0).astype(BF16)
            part = part + dot_nn(dot_nt(unit, dl).astype(BF16), wr)
            total = total + dot_nn(dl, rows[n][...])
        outs[r][at, :] = part.astype(BF16)
    if with_router:
        total = total[0:ne] + total[ne : 2 * ne]
        gr_ref[...] = so_far[...] + total if more else total


def spread_rows(z, lines):
    n = lines.shape[0] * z.pieces
    rows = [lines[:, s * z.wide : (s + 1) * z.wide] for s in range(z.pieces)]
    return jnp.concatenate(rows + [jnp.zeros((8 * z.ne - n, z.wide), F32)], axis=0)


def write_parts(z, who, ref, wide, lines):
    for p in range(z.ne):
        c = jnp.bitwise_xor(z.offset[p], who[1])
        ref[p] = jnp.concatenate([wide[c], lines[c]], axis=0).astype(BF16)


def back_one_body(z, parts, who, dy_ref, ln_ref, resid_ref, gr_ref, h1_ref, *refs):
    nt, lp, hw = z.nt, z.lp, z.hw
    dz_parts, refs = refs[:parts], refs[parts:]
    weights, p_ref, ctx_ref, refs = refs[:nt], refs[nt : 2 * nt], refs[2 * nt : 3 * nt], refs[3 * nt :]
    dresid_ref, dctx_ref, dv_ref, pays = refs[0], refs[1:][:nt], refs[1 + nt :][:nt], refs[1 + 2 * nt :][:nt]
    dyp, tail, buf, lines = refs[1 + 3 * nt :]
    dyp[...] = jnp.zeros(dyp.shape, F32)
    for i in range(z.images):
        dyp[i * lp : i * lp + IMAGE_TOKENS, :] = dy_ref[
            i * IMAGE_TOKENS : (i + 1) * IMAGE_TOKENS, :
        ]
    dz = dz_parts[0][...].astype(F32)
    for p in dz_parts[1:]:
        dz = dz + p[...].astype(F32)
    unit, rstd = normalize(resid_ref[...])
    dresid = norm_back(dz * ln_ref[2:3, :], unit, rstd) + dyp[...]
    dresid_ref[...] = dresid
    tail[...] = jnp.zeros(tail.shape, F32)
    tail[0:1, :] = jnp.sum(dz * unit, axis=0, keepdims=True)
    tail[1:2, :] = jnp.sum(dz, axis=0, keepdims=True)
    for e in range(z.ne):
        tail[pl.ds(8 + jnp.bitwise_xor(e, who[1]), 1), :] = gr_ref[e : e + 1, :]
    rows = spread_rows(z, tail[...])
    for p in range(z.ne):
        lines[p] = rows[8 * p : 8 * p + 8]
    da = dresid.astype(BF16)
    h1_t = h1_ref[...].T
    da_t = da.T
    head_of = iota((lp, hw), 1) // HEAD_DIM
    for r in range(nt):
        dctx = dot_nn(da, weights[r][:, 3 * hw : 4 * hw]).astype(BF16)
        dctx_ref[r][...] = dctx
        pieces = []
        for i in range(z.images):
            dc = dctx[i * lp : (i + 1) * lp]
            dv = jnp.zeros((lp, hw), F32)
            for j in range(z.hpb):
                p = p_ref[r][i * z.hpb + j]
                dv = jnp.where(head_of == j, dot_tn(p, dc), dv)
            pieces.append(dv.astype(BF16))
        dv = jnp.concatenate(pieces, axis=0)
        dv_ref[r][...] = dv
        dw = jnp.concatenate([dot_nn(h1_t, dv), dot_nn(da_t, ctx_ref[r][...])], axis=1)
        for p in range(z.ne):
            buf[p] = dw[p * z.crow : (p + 1) * z.crow]
        write_parts(z, who, pays[r], buf, lines)


def back_two_body(z, who, x_ref, ln_ref, h1_ref, *refs):
    nt, lp, hw = z.nt, z.lp, z.hw
    qkv_ref, dctx_ref, p_ref, dv_ref, refs = (*(refs[k * nt : (k + 1) * nt] for k in range(4)), refs[4 * nt :])
    dresid_ref, refs = refs[0], refs[1:]
    weights, in_ref, pays, xp, tail, buf, lines = (
        refs[:nt],
        refs[nt],
        refs[nt + 1 : 2 * nt + 1],
        *refs[2 * nt + 1 :],
    )
    xp[...] = jnp.zeros(xp.shape, F32)
    for i in range(z.images):
        xp[i * lp : i * lp + IMAGE_TOKENS, :] = x_ref[
            i * IMAGE_TOKENS : (i + 1) * IMAGE_TOKENS, :
        ]
    unit, rstd = normalize(xp[...])
    h1_t = h1_ref[...].T
    head_of = iota((lp, hw), 1) // HEAD_DIM
    dh = jnp.zeros((z.rows, z.width), F32)
    scale = HEAD_DIM**-0.5
    grads = []
    for r in range(nt):
        pieces = []
        for i in range(z.images):
            at = slice(i * lp, (i + 1) * lp)
            q, k, v = (qkv_ref[r][at, n * hw : (n + 1) * hw] for n in range(3))
            dc = dctx_ref[r][at, :]
            dq = jnp.zeros((lp, hw), F32)
            dk = jnp.zeros((lp, hw), F32)
            for j in range(z.hpb):
                mine = head_of == j
                pf = p_ref[r][i * z.hpb + j].astype(F32)
                dp = dot_nt(jnp.where(mine, dc, jnp.zeros_like(dc)), v)
                w = pf * dp
                ds = (w - pf * jnp.sum(w, axis=1, keepdims=True)).astype(BF16)
                dq = jnp.where(mine, dot_nn(ds, k) * scale, dq)
                dk = jnp.where(mine, dot_tn(ds, q) * scale, dk)
            pieces.append(jnp.concatenate([dq, dk], axis=1).astype(BF16))
        dqk = jnp.concatenate(pieces, axis=0)
        grads.append(dot_nn(h1_t, dqk))
        dh = dh + dot_nt(dqk, weights[r][:, 0 : 2 * hw]) + dot_nt(
            dv_ref[r][...], weights[r][:, 2 * hw : 3 * hw]
        )
    tail[...] = jnp.zeros(tail.shape, F32)
    tail[0:1, :] = jnp.sum(dh * unit, axis=0, keepdims=True)
    tail[1:2, :] = jnp.sum(dh, axis=0, keepdims=True)
    rows = spread_rows(z, tail[...])
    for p in range(z.ne):
        lines[p] = rows[8 * p : 8 * p + 8]
    for r in range(nt):
        for p in range(z.ne):
            buf[p] = grads[r][p * z.crow : (p + 1) * z.crow]
        write_parts(z, who, pays[r], buf, lines)
    xp[...] = dresid_ref[...] + norm_back(dh * ln_ref[0:1, :], unit, rstd)
    for i in range(z.images):
        in_ref[i * IMAGE_TOKENS : (i + 1) * IMAGE_TOKENS, :] = xp[
            i * lp : i * lp + IMAGE_TOKENS, :
        ]


def last_body(z, who, low, high, q_ref, k_ref, v_ref, o_ref, n1, n2, n3, n4, router_ref, wide, lines):
    hw, half = z.hw, z.ne // 2
    for p in range(z.ne):
        c = jnp.bitwise_xor(z.offset[p], who[1])
        both = (low, high)[p // half][p % half].astype(F32)
        wide[c] = both[0 : z.crow]
        lines[c] = both[z.crow : z.prow]
    both = jnp.concatenate([wide[p] for p in range(z.ne)], axis=0)
    v_ref[...] = both[:, 0:hw]
    o_ref[...] = both[:, hw : 2 * hw].T
    q_ref[...] = both[:, 2 * hw : 3 * hw]
    k_ref[...] = both[:, 3 * hw : 4 * hw]
    both = jnp.concatenate([lines[p] for p in range(z.ne)], axis=0)
    one, two = both[:, 0 : z.wide], both[:, z.wide : 2 * z.wide]
    n = 8 + z.ne
    one = jnp.concatenate([one[s * n : (s + 1) * n] for s in range(z.pieces)], axis=1)
    two = jnp.concatenate([two[s * 8 : (s + 1) * 8] for s in range(z.pieces)], axis=1)
    n1[...], n2[...], n3[...], n4[...] = two[0:1], two[1:2], one[0:1], one[1:2]
    router_ref[...] = one[8:n]


def expert_grads_body(z, parts, who, *refs):
    one, two, (first_ref, second_ref) = refs[:parts], refs[parts : 2 * parts], refs[2 * parts :]
    first_ref[...] = sum(p[...].astype(F32) for p in one)
    second_ref[...] = sum(p[...].astype(F32) for p in two).T


def finish_body(z, parts, who, resid_ref, *refs):
    out_ref, xp = refs[parts], refs[parts + 1]
    total = refs[0][...].astype(F32)
    for p in refs[1:parts]:
        total = total + p[...].astype(F32)
    xp[...] = resid_ref[...] + total
    for i in range(z.images):
        out_ref[i * IMAGE_TOKENS : (i + 1) * IMAGE_TOKENS, :] = xp[
            i * z.lp : i * z.lp + IMAGE_TOKENS, :
        ]


def swap(value, axis, bit):
    n = lax.axis_size(axis)
    return lax.ppermute(value, axis, [(k, k ^ bit) for k in range(n)])


def gather_far(own, axis):
    blocks = [own]
    for bit in halving_bits(lax.axis_size(axis))[1:]:
        blocks += [swap(v, axis, bit) for v in blocks]
    return blocks


def gather_near(blocks, axis):
    return [v for b in blocks for v in (b, swap(b, axis, 1))]


def gather_blocks(own, axis, late=None):
    blocks = gather_far(own, axis)
    if late is not None:
        blocks = blocks[:1] + hold(blocks[1:], late)
    return gather_near(blocks, axis)


def scatter_step(left, axis, bit):
    left = {r: list(parts) for r, parts in left.items()}
    for r in sorted(left, reverse=True):
        if r & bit:
            left[r ^ bit].append(swap(total_low(left.pop(r)), axis, bit))
    return left


def scatter_near(blocks, axis):
    left = {r: [b] for r, b in enumerate(blocks)}
    left = scatter_step(left, axis, 1)
    far = {r: [total_low(parts)] for r, parts in left.items() if r}
    return {**left, **far}


def hold_far(left, after):
    far = [r for r in left if r]
    held = hold([left[r][0] for r in far], after)
    return {0: left[0], **{r: [v] for r, v in zip(far, held)}}


def scatter_far(left, axis):
    for bit in halving_bits(lax.axis_size(axis))[1:]:
        left = scatter_step(left, axis, bit)
    return left[0]


def scatter_sum(blocks, axis):
    return scatter_far(scatter_near(blocks, axis), axis)


def total_low(parts):
    if len(parts) == 1:
        return parts[0]
    return total(parts).astype(BF16)


def total(parts):
    out = parts[0].astype(F32)
    for p in parts[1:]:
        out = out + p.astype(F32)
    return out


def split_last(values):
    return values[:-1], values[-1]


def send_pairs(pairs, first, axis):
    return [v if first + k == 0 else swap(v, axis, 2 * (first + k)) for k, v in enumerate(pairs)]


def pass_on(direct, axis):
    blk = direct[0].shape[0] // 2
    return swap(jnp.concatenate([v[blk:] for v in direct], axis=0), axis, 1)


def scatter_xy(left):
    bits = halving_bits(lax.axis_size("tensor"))
    for bit in bits[2:]:
        left = scatter_step(left, "tensor", bit)
    own, other = total_low(left[0]), total_low(left[2])
    half = own.shape[0] // 2
    nt, ne = lax.axis_size("tensor"), lax.axis_size("expert")
    both = [(e * nt + t, (e ^ 1) * nt + (t ^ 2)) for e in range(ne) for t in range(nt)]
    return [
        own[:half],
        lax.ppermute(other[half:], ("expert", "tensor"), both),
        swap(own[half:], "expert", 1),
        swap(other[:half], "tensor", 2),
    ]


def places(bits):
    n = 1 << len(bits)
    return [sum(b for k, b in enumerate(bits) if p & (n >> (k + 1))) for p in range(n)]


def exchange_sum(value, axis, bits):
    offsets = places(bits)
    step = value.shape[0] // len(offsets)
    parts = [value[p * step : (p + 1) * step] for p in range(len(offsets))]
    return total_low([parts[0]] + [swap(v, axis, o) for v, o in zip(parts[1:], offsets[1:])])


def exchange_all(value, axis, bits):
    return jnp.concatenate([value] + [swap(value, axis, o) for o in places(bits)[1:]], 0)


def sum_rest(value, axis):
    for group in groups_of(axis):
        value = exchange_sum(value, axis, group)
    return value


def groups_of(axis):
    bits = halving_bits(lax.axis_size(axis))
    return [bits[k : k + 2] for k in range(1, len(bits), 2)]


def share_rest(value, axis):
    for group in groups_of(axis)[::-1]:
        value = exchange_all(value, axis, group)
    return value


def shards(
    block_in,
    out_grad,
    routes,
    kept_pairs,
    ln1_gain,
    ln1_bias,
    w_query,
    w_key,
    w_value,
    w_attn_out,
    ln2_gain,
    ln2_bias,
    w_router,
    w_expert_in,
    w_expert_out,
):
    nt, ne = lax.axis_size("tensor"), lax.axis_size("expert")
    width = block_in.shape[1]
    z = Sizes(
        nt, ne, width, block_in.shape[0], routes.shape[0], w_query.shape[1], w_expert_in.shape[2]
    )
    lp, hw, hid, blk = z.lp, z.hw, z.hid, z.blk
    me_t, me_e = lax.axis_index("tensor"), lax.axis_index("expert")
    who = jnp.stack([me_t, me_e]).astype(I32)
    body = functools.partial

    rows_low = shape((z.rows, width), BF16)
    pair = shape((2 * blk, width), BF16)
    quarter, half = ne // 4, ne // 2

    dy_low, attn_own = call(
        body(first_body, z),
        [rows_low, shape((width, 4 * hw), BF16)],
        [who, *map(Far, (out_grad, w_query, w_key, w_value, w_attn_out))],
        [pltpu.VMEM((z.rows, width), F32)],
    )
    dy_part = gather_far(dy_low, "tensor")
    lines = jnp.pad(
        jnp.stack([routes.T, kept_pairs.T]).reshape(2, 2, z.chunks, IMAGE_TOKENS),
        ((0, 0), (0, 0), (0, 0), (0, lp - IMAGE_TOKENS)),
        constant_values=-1,
    )
    expert_own, pos, keep, post = call(
        body(early_body, z),
        [
            shape((2 * width, hid), BF16),
            shape((z.chunks, ne, lp), I32),
            shape((z.chunks, ne, lp), F32),
            shape((z.chunks, lp, ne), I32),
        ],
        [who, Far(w_expert_in[0]), Far(w_expert_out[0]), lines[0], lines[1].astype(F32)],
        after=[dy_low],
    )
    dy_far = hold(dy_part[1:], [pos])
    dy_rows = gather_near([dy_part[0], *dy_far], "tensor")
    attn_part = gather_far(hold([attn_own], dy_far)[0], "tensor")
    dy_sent = call(
        body(dispatch_dy_body, z),
        [pair] * quarter,
        [who, pos, *dy_rows],
        [pltpu.VMEM((half * blk, width), F32)],
    )
    dy_in = send_pairs(dy_sent, quarter, "expert")
    attn_w = gather_near(attn_part[:1] + hold(attn_part[1:], dy_sent[:1]), "tensor")

    norms = jnp.stack([ln1_gain, ln1_bias, ln2_gain, ln2_bias])
    wr = w_router.T
    second, (resid, h1, *rest) = split_at(z.images, call(
        body(attend_body, z),
        [
            *[shape((lp, width), BF16)] * z.images,
            shape((z.rows, width), F32),
            rows_low,
            *[shape((z.rows, 3 * hw), BF16)] * nt,
            *[shape((z.rows, hw), BF16)] * nt,
            *[shape((z.images * z.hpb, lp, lp), BF16)] * nt,
        ],
        [who, Far(block_in), norms, Far(wr), *attn_w],
        [
            pltpu.VMEM((z.rows, width), F32),
            pltpu.VMEM((lp, width), F32),
            pltpu.VMEM((ne, width), F32),
        ],
    ))
    qkv, ctx, probs = rest[:nt], rest[nt : 2 * nt], rest[2 * nt :]
    rows_part = [gather_far(v, "tensor") for v in second]
    far = nt // 2 - 1
    rest = hold([w for v in rows_part for w in v[1:]] + dy_in, [])
    rows = [
        gather_near([v[0], *rest[i * far : (i + 1) * far]], "tensor")
        for i, v in enumerate(rows_part)
    ]
    rows = [v[r] for r in range(nt) for v in rows]
    dy_in = rest[z.images * far :]
    dy_passed = pass_on(dy_in, "expert")
    sent = call(
        body(dispatch_body, z),
        [pair] * half + [shape((blk, width), BF16)] * half,
        [who, pos, keep, *rows, *dy_rows],
        [
            pltpu.VMEM((z.slots, width), F32),
            pltpu.VMEM((half * blk, width), F32),
            pltpu.VMEM((2 * ne, z.slots), F32),
        ],
    )
    expert_own = hold([expert_own], rest[:1])[0]
    *sent, dy_passed, own_core = hold([*sent, dy_passed, swap(expert_own, "tensor", 1)], [])
    far_in = [swap(v, "expert", half + k) for k, v in enumerate(sent[half:])]
    near_in = hold(sent[1:half], far_in)
    near_in = [sent[0]] + [swap(v, "expert", 1 + k) for k, v in enumerate(near_in)]
    w_part = gather_far(expert_own, "tensor")
    rest = hold(w_part[1:], far_in)
    expert_w = [w_part[0], own_core, *gather_near(rest, "tensor")]

    size = half * blk
    passed = [
        *[shape((size, hid), BF16)] * (2 * nt),
        shape((size, width), BF16),
        shape((1, 128), F32),
    ]
    held = [
        pltpu.VMEM((size, width), BF16),
        pltpu.VMEM((size, 128), F32),
        pltpu.VMEM((size, width), F32),
        pltpu.VMEM((size, width), F32),
    ]
    far = call(
        body(expert_body, z, False, half),
        [pair] * half + passed,
        [who, *far_in, *dy_in, dy_passed, *expert_w],
        held,
    )
    far_out, far_mixed, (*far_hidden, far_g, far_top) = far[:quarter], far[quarter:half], far[half:]
    near = call(
        body(expert_body, z, True, half),
        [pair] * half + passed,
        [who, *near_in, *expert_w, far_top],
        held,
    )
    near_out, (*near_hidden, near_g, tops) = near[:half], near[half:]
    far_out = send_pairs(far_out, quarter, "expert")
    near_out = [v if k == 0 else swap(v, "expert", k) for k, v in enumerate(near_out)]
    expert_grads = call(
        body(expert_weights_body, z),
        [shape((width, hid), BF16)] * (2 * nt),
        [who, *near_in, *far_in, near_g, far_g, *near_hidden, *far_hidden],
        [pltpu.VMEM((2, width, size), BF16), pltpu.VMEM((2, width, size), BF16)],
    )
    far_out = hold(far_out, expert_grads[:1])
    far_out.append(pass_on(far_out, "expert"))
    first_near = scatter_near(expert_grads[:nt], "tensor")
    second_near = scatter_near(expert_grads[nt:], "tensor")

    def combine(which, more):
        return call(
            body(combine_body, z, True, which),
            [rows_low] * len(which) + [shape((ne, width), F32)],
            [
                who,
                post,
                keep,
                Far(wr),
                *[rows[r * z.images + i] for r in which for i in range(z.images)],
                *more,
                *near_out,
                *far_out,
            ],
            [pltpu.VMEM((z.slots, width), BF16)],
        )

    *partial, router_part = combine(range(2, nt), [])
    dz_near = scatter_step({r + 2: [b] for r, b in enumerate(partial)}, "tensor", 1)
    dz_near = {r: [total_low(parts)] for r, parts in dz_near.items()}
    router_part = hold([router_part], dz_near[2])[0]
    own, other, router_part = combine(range(2), [router_part])
    other = [swap(other[i * lp : (i + 1) * lp], "tensor", 1) for i in range(z.images)]
    dz_near[0] = [own, jnp.concatenate(other, axis=0)]
    dz_parts = scatter_far(dz_near, "tensor")
    mixed = send_pairs(far_mixed, quarter, "expert")
    second_parts = scatter_far(hold_far(second_near, dz_parts[-1:]), "tensor")

    pay = shape((ne, z.prow, z.wide), BF16)
    buffers = [pltpu.VMEM((ne, z.crow, z.wide), F32), pltpu.VMEM((ne, 8, z.wide), F32)]
    per_head = shape((z.rows, hw), BF16)
    outs = call(
        body(back_one_body, z, len(dz_parts)),
        [shape((z.rows, width), F32)] + [per_head] * (2 * nt) + [pay] * nt,
        [who, Far(out_grad), norms, resid, router_part, h1, *dz_parts, *attn_w, *probs, *ctx],
        [pltpu.VMEM((z.rows, width), F32), pltpu.VMEM((8 + ne, width), F32), *buffers],
    )
    dresid, dctx, dv = outs[0], outs[1:][:nt], outs[1 + nt :][:nt]
    one_near = scatter_near(outs[1 + 2 * nt :], "tensor")
    outs = call(
        body(back_two_body, z),
        [Far(shape((z.tok_dev, width), F32))] + [pay] * nt,
        [who, Far(block_in), norms, h1, *qkv, *dctx, *probs, *dv, dresid, *attn_w],
        [pltpu.VMEM((z.rows, width), F32), pltpu.VMEM((8, width), F32), *buffers],
        after=[one_near[nt // 2][0]],
    )
    input_grad = outs[0]
    one_parts = scatter_far(one_near, "tensor")
    far = [r for r in first_near if r]
    two = hold(
        [
            *outs[1:],
            one_parts[-1],
            second_parts[1],
            first_near[0][1],
            *[first_near[r][0] for r in far],
        ],
        [],
    )
    two, (one_parts[-1], second_parts[1], first_near[0][1], *rest) = split_at(nt, two)
    first_near.update((r, [v]) for r, v in zip(far, rest))
    one = total_low(one_parts)
    one = total_low([one[:half], swap(one[half:], "expert", 1)])
    two_near = scatter_near(two, "tensor")
    two_parts = scatter_xy(two_near)

    merged = jnp.concatenate([one, total_low(two_parts)], axis=2)
    merged, second_parts[-1], *mixed = hold([merged, second_parts[-1], *mixed], [])
    passed = pass_on(mixed, "expert")
    mixed_part = call(
        body(combine_body, z, False, range(nt)),
        [rows_low] * nt,
        [who, post, *near_out, *mixed, passed],
        [pltpu.VMEM((z.slots, width), BF16)],
    )
    value = sum_rest(merged, "expert")
    first_parts = scatter_far(hold_far(first_near, two_parts[-1:]), "tensor")
    value, first_parts[-1] = hold([value, first_parts[-1]], [])
    value = share_rest(value, "expert")
    mixed_near = scatter_near(mixed_part, "tensor")
    far = [r for r in mixed_near if r]
    value, *rest = hold([value, *[mixed_near[r][0] for r in far]], [])
    mixed_near.update((r, [v]) for r, v in zip(far, rest))
    mixed_parts = scatter_far(mixed_near, "tensor")
    sums = [value, swap(value, "expert", 1)]
    grad_first, grad_second = call(
        body(expert_grads_body, z, len(first_parts)),
        [Far(shape((width, hid), F32)), Far(shape((hid, width), F32))],
        [who, *first_parts, *second_parts],
    )
    block_out = call(
        body(finish_body, z, len(mixed_parts)),
        Far(shape((z.tok_dev, width), F32)),
        [who, resid, *mixed_parts],
        [pltpu.VMEM((z.rows, width), F32)],
    )

    head = Far(shape((width, hw), F32))
    grad_q, grad_k, grad_v, grad_o, n1, n2, n3, n4, router_grad = call(
        body(last_body, z),
        [head] * 3
        + [Far(shape(v, F32)) for v in ((hw, width), *[(1, width)] * 4, (ne, width))],
        [who, *sums],
        [pltpu.VMEM((ne, z.crow, 2 * z.wide), F32), pltpu.VMEM((ne, 8, 2 * z.wide), F32)],
        after=[place(v, pltpu.HBM) for v in (grad_first,)],
    )
    head_maxima = lax.dynamic_slice_in_dim(tops[0], me_t * z.hpb, z.hpb, 0)
    factor = jnp.repeat(jnp.sqrt(jnp.minimum(1.0, clip_limit / head_maxima)), HEAD_DIM)
    return (
        block_out,
        input_grad,
        n1[0],
        n2[0],
        grad_q,
        grad_k,
        grad_v,
        grad_o,
        n3[0],
        n4[0],
        router_grad.T,
        grad_first[None],
        grad_second[None],
        head_maxima,
        w_query * factor[None, :],
        w_key * factor[None, :],
    )


def solution(mesh):
    placed = (
        P(("expert", "tensor"), None),
        P(("expert", "tensor"), None),
        P("expert", None),
        P("expert", None),
        P(),
        P(),
        P(None, "tensor"),
        P(None, "tensor"),
        P(None, "tensor"),
        P("tensor", None),
        P(),
        P(),
        P(),
        P("expert", None, "tensor"),
        P("expert", "tensor", None),
    )
    return jax.shard_map(
        shards,
        mesh=mesh,
        in_specs=placed,
        out_specs=(
            P(("expert", "tensor"), None),
            P(("expert", "tensor"), None),
            P(),
            P(),
            P(None, "tensor"),
            P(None, "tensor"),
            P(None, "tensor"),
            P("tensor", None),
            P(),
            P(),
            P(),
            P("expert", None, "tensor"),
            P("expert", "tensor", None),
            P("tensor"),
            P(None, "tensor"),
            P(None, "tensor"),
        ),
        check_vma=False,
    )
```

```python
import functools

import jax
import jax.numpy as jnp
from jax import lax
from jax.experimental import pallas as pl
from jax.experimental.pallas import tpu as pltpu
from jax.sharding import PartitionSpec as P

HEAD_DIM = 64
IMAGE_TOKENS = 197
SPARE = 200
TOP_ROW = 197

F32 = jnp.float32
BF16 = jnp.bfloat16
I32 = jnp.int32

clip_limit = 4.0
norm_eps = 1e-06
low_value = -1e30


def round_up(value, unit):
    return -(-value // unit) * unit


def dot_nn(a, b):
    return lax.dot_general(a, b, (((1,), (0,)), ((), ())), preferred_element_type=F32)


def dot_nt(a, b):
    return lax.dot_general(a, b, (((1,), (1,)), ((), ())), preferred_element_type=F32)


def dot_tn(a, b):
    return lax.dot_general(a, b, (((0,), (0,)), ((), ())), preferred_element_type=F32)


def iota(shape, dim):
    return lax.broadcasted_iota(I32, shape, dim)


def split2(v):
    high = v.astype(BF16).astype(F32)
    return high, (v - high).astype(BF16).astype(F32)


def normalize(rows):
    center = jnp.mean(rows, axis=-1, keepdims=True)
    offset = rows - center
    rstd = lax.rsqrt(jnp.mean(offset * offset, axis=-1, keepdims=True) + norm_eps)
    return offset * rstd, rstd


def norm_back(grad, unit, rstd):
    return rstd * (
        grad
        - jnp.mean(grad, axis=-1, keepdims=True)
        - unit * jnp.mean(grad * unit, axis=-1, keepdims=True)
    )


def halving_bits(n):
    return [1 << k for k in range(n.bit_length() - 1)]


class Sizes:
    def __init__(self, nt, ne, width, tok_dev, tok_group, head_cols, hidden):
        self.nt, self.ne, self.width = nt, ne, width
        self.tok_dev = tok_dev
        self.images = tok_dev // IMAGE_TOKENS
        self.lp = round_up(SPARE + ne, 16)
        self.rows = self.images * self.lp
        self.chunks = nt * self.images
        self.cap = 5 * tok_group // (2 * ne) + 1
        self.spr = -(-self.cap // nt)
        need = self.spr + 2
        self.blk = next((b for b in (16, 32, 64, 128) if b >= need), round_up(need, 128))
        self.epl = 128 // self.blk
        self.hw = head_cols
        self.hpb = head_cols // HEAD_DIM
        self.hid = hidden
        self.slots = ne * self.blk
        self.wide = 2 * self.hw
        self.pieces = width // self.wide
        self.crow = width // ne
        self.prow = self.crow + 8
        bits = halving_bits(ne)
        self.offset = places(bits)


SM = pl.BlockSpec(memory_space=pltpu.SMEM)
VM = pl.BlockSpec(memory_space=pltpu.VMEM)
ANY = pl.BlockSpec(memory_space=pl.ANY)


class Far:
    def __init__(self, value):
        self.value = value


class Given:
    def __init__(self, ref, copy):
        self.ref, self.copy = ref, copy
        copy.start()

    def wait(self):
        if self.copy is not None:
            self.copy.wait()
            self.copy = None

    def __getitem__(self, at):
        self.wait()
        return self.ref[at]


def place(value, space):
    return pltpu.with_memory_space_constraint(value, space)


def call(body, outs, args, scratch=(), after=()):
    skip = len(after)
    keep = lax.axis_size("tensor") <= 4
    vmem = 12 if keep else 60
    single = not isinstance(outs, list)
    flat = [outs] if single else outs
    far = [k for k, a in enumerate(args) if isinstance(a, Far)]

    def run(*refs):
        ins, refs = [refs[0], *refs[1 + skip : skip + len(args)]], refs[skip + len(args) :]
        results, refs = refs[: len(flat)], refs[len(flat) :]
        own, refs = refs[: len(scratch)], refs[len(scratch) :]
        for n, k in enumerate(far):
            ins[k] = Given(refs[n], pltpu.make_async_copy(ins[k], refs[n], refs[-1].at[n]))
        body(*ins, *results, *own)
        for k in far:
            ins[k].wait()

    extra = [pltpu.VMEM(args[k].value.shape, args[k].value.dtype) for k in far]
    if far:
        extra.append(pltpu.SemaphoreType.DMA((len(far),)))
    got = pl.pallas_call(
        run,
        out_shape=[
            o.value if isinstance(o, Far) else pltpu.VMEM(o.shape, o.dtype) if keep else o
            for o in flat
        ],
        in_specs=[SM] + [ANY] * skip + [ANY if k in far else VM for k in range(1, len(args))],
        out_specs=[VM] * len(flat),
        scratch_shapes=[*scratch, *extra],
        compiler_params=pltpu.CompilerParams(vmem_limit_bytes=vmem * 1024 * 1024),
    )(
        args[0],
        *after,
        *[
            place(a.value, pltpu.HBM) if isinstance(a, Far) else place(a, pltpu.VMEM) if keep else a
            for a in args[1:]
        ],
    )
    return got[0] if single else list(got)


def hold(values, after):
    n, m = len(values), len(after)

    def run(*refs):
        pass

    out = pl.pallas_call(
        run,
        out_shape=[shape(v.shape, v.dtype) for v in values],
        in_specs=[ANY] * (n + m),
        out_specs=[ANY] * n,
        input_output_aliases={k: k for k in range(n)},
        compiler_params=pltpu.CompilerParams(vmem_limit_bytes=1024 * 1024),
    )(*values, *after)
    return list(out)


def shape(dims, kind):
    return jax.ShapeDtypeStruct(dims, kind)


def first_body(z, who, dy_ref, q_ref, k_ref, v_ref, o_ref, low_ref, out_ref, pad):
    hw = z.hw
    pad[...] = jnp.zeros(pad.shape, F32)
    for i in range(z.images):
        pad[i * z.lp : i * z.lp + IMAGE_TOKENS, :] = dy_ref[
            i * IMAGE_TOKENS : (i + 1) * IMAGE_TOKENS, :
        ]
    low_ref[...] = pad[...].astype(BF16)
    for n, ref in enumerate((q_ref, k_ref, v_ref)):
        out_ref[:, n * hw : (n + 1) * hw] = ref[...].astype(BF16)
    out_ref[:, 3 * hw : 4 * hw] = o_ref[...].T.astype(BF16)


def early_body(z, who, in_ref, out_ref, route_ref, kept_ref, *refs):
    w_ref, pos_ref, keep_ref, post_ref = refs
    w_ref[0 : z.width, :] = in_ref[...].astype(BF16)
    w_ref[z.width : 2 * z.width, :] = out_ref[...].T.astype(BF16)
    me_t, me_e = who[0], who[1]
    named = jnp.bitwise_xor(iota((z.ne, z.lp), 0), me_e)
    before = jnp.where(iota((z.lp, z.lp), 0) < iota((z.lp, z.lp), 1), 1.0, 0.0).astype(BF16)
    count = jnp.zeros((z.ne, 1), F32)
    for c in range(z.chunks):
        block, img = c // z.images, c % z.images
        first = route_ref[0, c : c + 1, :] == named
        other = route_ref[1, c : c + 1, :] == named
        hit = jnp.where(first | other, 1.0, 0.0)
        place = dot_nn(hit.astype(BF16), before) + count
        count = count + jnp.sum(hit, axis=1, keepdims=True)
        at = jnp.bitwise_xor(block, me_t) * z.images + img
        place = jnp.where(hit > 0, place, -1.0)
        pos_ref[at] = place.astype(I32)
        post_ref[at] = place.T.astype(I32)
        keep_ref[at] = jnp.where(first, kept_ref[0, c : c + 1, :], 0.0) + jnp.where(
            other, kept_ref[1, c : c + 1, :], 0.0
        )


def attend_body(z, who, x_ref, ln_ref, wr_ref, *refs):
    nt, lp, hw = z.nt, z.lp, z.hw
    weights = refs[:nt]
    z_refs, refs = refs[nt : nt + z.images], refs[nt + z.images :]
    resid_ref, h1_ref, refs = refs[0], refs[1], refs[2:]
    qkv_ref, ctx_ref, p_ref = refs[:nt], refs[nt : 2 * nt], refs[2 * nt : 3 * nt]
    xp, zb, pt = refs[3 * nt :]
    me_t = who[0]
    xp[...] = jnp.zeros(xp.shape, F32)
    for i in range(z.images):
        xp[i * lp : i * lp + IMAGE_TOKENS, :] = x_ref[
            i * IMAGE_TOKENS : (i + 1) * IMAGE_TOKENS, :
        ]
    unit, _ = normalize(xp[...])
    h1 = (unit * ln_ref[0:1, :] + ln_ref[1:2, :]).astype(BF16)
    h1_ref[...] = h1
    head_of = iota((lp, hw), 1) // HEAD_DIM
    real = iota((lp, lp), 1) < IMAGE_TOKENS
    real_row = iota((lp, 1), 0) < IMAGE_TOKENS
    lane = iota((1, 128), 1)
    tops = jnp.full((1, 128), low_value, F32)
    attn = jnp.zeros((z.rows, z.width), F32)
    for r in range(nt):
        qkv = dot_nn(h1, weights[r][:, 0 : 3 * hw]).astype(BF16)
        qkv_ref[r][...] = qkv
        ctxs = []
        for i in range(z.images):
            at = slice(i * lp, (i + 1) * lp)
            q, k, v = (qkv[at, n * hw : (n + 1) * hw] for n in range(3))
            ctx = jnp.zeros((lp, hw), F32)
            for j in range(z.hpb):
                mine = head_of == j
                s = dot_nt(jnp.where(mine, q, jnp.zeros_like(q)), k) * (HEAD_DIM**-0.5)
                s = jnp.where(real, s, low_value)
                peak = jnp.max(s, axis=1, keepdims=True)
                top = jnp.max(jnp.where(real_row, peak, low_value), axis=0, keepdims=True)
                head = jnp.bitwise_xor(me_t, r) * z.hpb + j
                tops = jnp.where(lane == head, jnp.maximum(tops, top), tops)
                e = jnp.exp(s - peak)
                p = (e * (1.0 / jnp.sum(e, axis=1, keepdims=True))).astype(BF16)
                p_ref[r][i * z.hpb + j] = p
                ctx = jnp.where(mine, dot_nn(p, v), ctx)
            ctxs.append(ctx.astype(BF16))
        ctx = jnp.concatenate(ctxs, axis=0)
        ctx_ref[r][...] = ctx
        attn = attn + dot_nt(ctx, weights[r][:, 3 * hw : 4 * hw])
    resid = xp[...] + attn
    resid_ref[...] = resid
    unit, _ = normalize(resid)
    second = unit * ln_ref[2:3, :] + ln_ref[3:4, :]
    w_hi, w_lo = (v.astype(BF16) for v in split2(router_rows(z, who, wr_ref)))
    row = iota((lp, 1), 0)
    t_hi = tops.astype(BF16).astype(F32)
    t_mid = (tops - t_hi).astype(BF16).astype(F32)
    t_lo = tops - t_hi - t_mid
    for i in range(z.images):
        part = second[i * lp : (i + 1) * lp]
        s_hi, s_lo = (v.astype(BF16) for v in split2(part))
        logits = dot_nt(w_hi, s_hi) + (dot_nt(w_hi, s_lo) + dot_nt(w_lo, s_hi))
        e = jnp.exp(logits - jnp.max(logits, axis=0, keepdims=True))
        p_hi, p_lo = split2(e / jnp.sum(e, axis=0, keepdims=True))
        pt[...] = jnp.zeros(pt.shape, F32)
        pt[:, 0:lp] = p_hi
        pt[:, 256 : 256 + lp] = p_lo
        zb[...] = jnp.where(row < IMAGE_TOKENS, part, 0.0)
        for n, t in enumerate((t_hi, t_mid, t_lo)):
            zb[TOP_ROW + n : TOP_ROW + n + 1, 0:128] = t
        zb[SPARE : SPARE + z.ne, :] = pt[...]
        z_refs[i][...] = zb[...].astype(BF16)


def router_rows(z, who, ref):
    return jnp.concatenate(
        [ref[pl.ds(jnp.bitwise_xor(e, who[1]), 1), :] for e in range(z.ne)], axis=0
    )


def split_at(n, values):
    return values[:n], values[n:]


def tail_rows(z, ref):
    start = (TOP_ROW // 16) * 16
    return ref[start : z.lp, :].astype(F32), start


def probs_of(z, ref):
    tail, start = tail_rows(z, ref)
    both = tail[SPARE - start : SPARE - start + z.ne]
    return both[:, 0 : z.lp] + both[:, 256 : 256 + z.lp]


def hot_rows(z, who, pos_ref, c, first, last):
    slot = iota((z.blk, z.lp), 0)
    slot = jnp.where(slot < z.spr, slot + who[0] * z.spr, -2)
    return jnp.concatenate(
        [
            jnp.where(pos_ref[c, e : e + 1, :] == slot, 1.0, 0.0).astype(BF16)
            for e in range(first, last)
        ],
        axis=0,
    )


def dispatch_dy_body(z, who, pos_ref, *refs):
    nt, ne, lp, blk = z.nt, z.ne, z.lp, z.blk
    rows, outs, acc = refs[:nt], refs[nt : nt + ne // 4], refs[nt + ne // 4]
    for c in range(z.chunks):
        r, i = c // z.images, c % z.images
        hot = hot_rows(z, who, pos_ref, c, ne // 2, ne)
        part = dot_nn(hot, rows[r][i * lp : (i + 1) * lp, :])
        acc[...] = part if c == 0 else acc[...] + part
    for k in range(ne // 4):
        outs[k][...] = acc[2 * k * blk : 2 * (k + 1) * blk, :].astype(BF16)


def dispatch_body(z, who, pos_ref, keep_ref, *refs):
    nt, ne, lp, blk = z.nt, z.ne, z.lp, z.blk
    rows, dy_rows, refs = refs[: z.chunks], refs[z.chunks :][:nt], refs[z.chunks + nt :]
    outs, (acc, dy_acc, gacc) = refs[:ne], refs[ne:]
    half = ne // 2
    tops = None
    for c in range(z.chunks):
        r, i = c // z.images, c % z.images
        hot = hot_rows(z, who, pos_ref, c, 0, ne)
        part = dot_nn(hot[: half * blk], dy_rows[r][i * lp : (i + 1) * lp, :])
        dy_acc[...] = part if c == 0 else dy_acc[...] + part
        part = dot_nn(hot, rows[c][...])
        acc[...] = part if c == 0 else acc[...] + part
        g_hi, g_lo = split2(probs_of(z, rows[c]) * keep_ref[c])
        both = jnp.concatenate([g_hi, g_lo], axis=0).astype(BF16)
        part = dot_nt(both, hot)
        gacc[...] = part if c == 0 else gacc[...] + part
        if i == 0:
            tail, start = tail_rows(z, rows[c])
            three = tail[TOP_ROW - start : TOP_ROW - start + 3, 0:128]
            top = three[0:1] + three[1:2] + three[2:3]
            tops = top if tops is None else jnp.maximum(tops, top)
    t_hi = tops.astype(BF16).astype(F32)
    t_mid = (tops - t_hi).astype(BF16).astype(F32)
    t_lo = tops - t_hi - t_mid
    none = jnp.zeros((1, 128), F32)
    top_row = jnp.concatenate([t_hi, t_mid, t_lo, none], axis=1)
    row = iota((blk, 1), 0)
    part_of = iota((1, 128), 1) // blk
    for e in range(ne):
        tile = slice((e // z.epl) * 128, (e // z.epl) * 128 + 128)
        g_hi = jnp.where(part_of == e % z.epl, gacc[e : e + 1, tile], 0.0)
        g_lo = jnp.where(part_of == e % z.epl, gacc[ne + e : ne + e + 1, tile], 0.0)
        gates = jnp.concatenate([g_hi, g_lo, none, none], axis=1)
        block = acc[e * blk : (e + 1) * blk, :]
        block = jnp.where(row == z.spr, gates, block)
        block = jnp.where(row == z.spr + 1, top_row, block)
        outs[e][0:blk, :] = block.astype(BF16)
        if e < half:
            outs[e][blk : 2 * blk, :] = dy_acc[e * blk : (e + 1) * blk, :].astype(BF16)


class Part:
    def __init__(self, ref, first):
        self.ref, self.first = ref, first

    def rows(self, start, stop):
        return self.ref[self.first + start : self.first + stop, :]

    def put(self, value):
        self.ref[self.first : self.first + value.shape[0], :] = value


def blocks_of(z, direct, passed, size=1, at=0):
    out = []
    for k, ref in enumerate(direct):
        out += [Part(ref, at * z.blk), Part(passed, (k * size + at) * z.blk)]
    return out


def spare_pair(z, part):
    start = (z.spr // 16) * 16
    tail = part.rows(start, z.blk).astype(F32)
    return tail[z.spr - start : z.spr - start + 1], tail[z.spr - start + 1 : z.spr - start + 2]


def expert_body(z, near, count, who, *refs):
    nt, ne, blk, hid, width = z.nt, z.ne, z.blk, z.hid, z.width
    half = count // 2
    rows_in = [Part(ref, 0) for ref in refs[:count]]
    if near:
        dy_in, refs = [Part(ref, blk) for ref in refs[:count]], refs[count:]
    else:
        refs = refs[count:]
        dy_in, refs = blocks_of(z, refs[:half], refs[half]), refs[half + 1 :]
    weights, refs = refs[:nt], refs[nt:]
    w = z.width
    if near:
        far_top, refs = refs[0], refs[1:]
        back, mixed = ([Part(ref, at * blk) for ref in refs[:count]] for at in range(2))
        refs = refs[count:]
    else:
        back, mixed = (
            [Part(ref, at * blk) for ref in some for at in range(2)]
            for some in (refs[:half], refs[half:count])
        )
        refs = refs[count:]
    act, du, refs = refs[:nt], refs[nt : 2 * nt], refs[2 * nt :]
    g, top_ref, rows, gate, o_acc, d_acc = refs
    real = iota((blk, 1), 0) < z.spr
    diag = iota((blk, 128), 0) == iota((blk, 128), 1) % blk
    tops = far_top[...] if near else None
    for n in range(count):
        at = slice(n * blk, (n + 1) * blk)
        rows[at, :] = jnp.where(real, rows_in[n].rows(0, blk), jnp.zeros((), BF16))
        gates, top = spare_pair(z, rows_in[n])
        top = top[:, 0:128] + top[:, 128:256] + top[:, 256:384]
        tops = top if tops is None else jnp.maximum(tops, top)
        line = gates[:, 0:128] + gates[:, 128:256]
        column = jnp.sum(jnp.where(diag, line, 0.0), axis=1, keepdims=True)
        gate[at, :] = jnp.broadcast_to(column, (blk, 128))
    top_ref[...] = tops
    u_first = dot_nn(rows[...], weights[0][0:w, :])
    for n in range(count):
        at = slice(n * blk, (n + 1) * blk)
        g[at, :] = (gate[at, 0:1] * dy_in[n].rows(0, blk).astype(F32)).astype(BF16)
    for r in range(nt):
        u = dot_nn(rows[...], weights[r][0:w, :]) if r else u_first
        second_w = weights[r][w : 2 * w, :]
        cube = 0.7978845608028654 * 0.044715 * u * u
        t = jnp.tanh(u * (0.7978845608028654 + cube))
        h = 0.5 + 0.5 * t
        a = (u * h).astype(BF16)
        slope = h + 2.0 * h * (1.0 - h) * u * (0.7978845608028654 + 3.0 * cube)
        d = (dot_nn(g[...], second_w) * slope).astype(BF16)
        act[r][...] = a
        du[r][...] = d
        o = dot_nt(a, second_w)
        b = dot_nt(d, weights[r][0:w, :])
        o_acc[...] = o if r == 0 else o_acc[...] + o
        d_acc[...] = b if r == 0 else d_acc[...] + b
    row = iota((blk, 1), 0)
    none = jnp.zeros((1, 128), F32)
    for n in range(count):
        at = slice(n * blk, (n + 1) * blk)
        o = o_acc[at, :]
        dgate = jnp.sum(o * dy_in[n].rows(0, blk).astype(F32), axis=1, keepdims=True)
        line = jnp.sum(jnp.where(diag, dgate, 0.0), axis=0, keepdims=True)
        hi, lo = split2(line)
        line = jnp.concatenate([hi, lo, none, none], axis=1)
        back[n].put(jnp.where(row == z.spr, line, d_acc[at, :]).astype(BF16))
        mixed[n].put((gate[at, 0:1] * o).astype(BF16))


def expert_weights_body(z, who, *refs):
    nt, ne, blk, hid = z.nt, z.ne, z.blk, z.hid
    rows_in, refs = [Part(ref, 0) for ref in refs[:ne]], refs[ne:]
    g, refs = refs[:2], refs[2:]
    act, du = (refs[:nt], refs[2 * nt : 3 * nt]), (refs[nt : 2 * nt], refs[3 * nt : 4 * nt])
    one, two, (rows_t, g_t) = refs[4 * nt : 5 * nt], refs[5 * nt : 6 * nt], refs[6 * nt :]
    real = iota((blk, 1), 0) < z.spr
    rows = [jnp.where(real, part.rows(0, blk), jnp.zeros((), BF16)) for part in rows_in]
    half = ne // 2
    for k in range(2):
        rows_t[k] = jnp.concatenate(rows[k * half : (k + 1) * half], axis=0).T
        g_t[k] = g[k][...].T
    for r in range(nt):
        first = dot_nn(rows_t[0], du[0][r][...]) + dot_nn(rows_t[1], du[1][r][...])
        one[r][...] = first.astype(BF16)
        second = dot_nn(g_t[0], act[0][r][...]) + dot_nn(g_t[1], act[1][r][...])
        two[r][...] = second.astype(BF16)


def hot_columns(z, post_ref, c, base):
    lane = iota((z.lp, 128), 1)
    slot = lane % z.blk
    slot = jnp.where(slot < z.spr, slot + base, -2)
    tiles = []
    for p in range(z.ne // z.epl):
        column = post_ref[c, :, p * z.epl : p * z.epl + 1]
        pick = jnp.broadcast_to(column, (z.lp, 128))
        for n in range(1, z.epl):
            e = p * z.epl + n
            pick = jnp.where(lane // z.blk == n, post_ref[c, :, e : e + 1], pick)
        tiles.append(jnp.where(pick == slot, 1.0, 0.0).astype(BF16))
    return jnp.concatenate(tiles, axis=1)


def combine_body(z, with_router, which, who, post_ref, *refs):
    nt, ne, lp, blk = len(which), z.ne, z.lp, z.blk
    more = with_router and 0 in which
    base = who[0] * z.spr
    if with_router:
        keep_ref, wr_ref, refs = refs[0], refs[1], refs[2:]
        rows, refs = refs[: nt * z.images], refs[nt * z.images :]
        if more:
            so_far, refs = refs[0], refs[1:]
    quarter = ne // 4
    at = 0 if with_router else blk
    blocks, refs = [Part(ref, at) for ref in refs[: ne // 2]], refs[ne // 2 :]
    blocks, refs = blocks + blocks_of(z, refs[:quarter], refs[quarter]), refs[quarter + 1 :]
    outs, refs = refs[:nt], refs[nt:]
    if with_router:
        gr_ref, refs = refs[0], refs[1:]
    stack = refs[0]
    for e in range(ne):
        stack[e * blk : (e + 1) * blk, :] = blocks[e].rows(0, blk)
    if with_router:
        row = iota((ne, 128), 0)
        half = iota((ne, 128), 1) // blk
        tiles = []
        for p in range(ne // z.epl):
            hi = jnp.zeros((ne, 128), F32)
            lo = jnp.zeros((ne, 128), F32)
            for n in range(z.epl):
                e = p * z.epl + n
                line, _ = spare_pair(z, blocks[e])
                own = (row == e) & (half == n)
                hi = jnp.where(own, line[:, 0:128], hi)
                lo = jnp.where(own, line[:, 128:256], lo)
            tiles.append(jnp.concatenate([hi, lo], axis=0))
        dgate = jnp.concatenate(tiles, axis=1).astype(BF16)
        unit = jnp.where(iota((lp, lp), 0) == iota((lp, lp), 1), 1.0, 0.0).astype(BF16)
        wr = router_rows(z, who, wr_ref).astype(BF16)
        wr = jnp.concatenate([wr, wr], axis=0)
        total = jnp.zeros((2 * ne, z.width), F32)
    for n in range(nt * z.images):
        r, i = n // z.images, n % z.images
        c = which[r] * z.images + i
        at = slice(i * lp, (i + 1) * lp)
        hot = hot_columns(z, post_ref, c, base)
        part = dot_nn(hot, stack[...])
        if with_router:
            both = dot_nt(dgate, hot)
            dp = (both[0:ne] + both[ne : 2 * ne]) * keep_ref[c]
            pr = probs_of(z, rows[n])
            dl = pr * (dp - jnp.sum(pr * dp, axis=0, keepdims=True))
            dl = jnp.concatenate(split2(dl), axis=0).astype(BF16)
            part = part + dot_nn(dot_nt(unit, dl).astype(BF16), wr)
            total = total + dot_nn(dl, rows[n][...])
        outs[r][at, :] = part.astype(BF16)
    if with_router:
        total = total[0:ne] + total[ne : 2 * ne]
        gr_ref[...] = so_far[...] + total if more else total


def spread_rows(z, lines):
    n = lines.shape[0] * z.pieces
    rows = [lines[:, s * z.wide : (s + 1) * z.wide] for s in range(z.pieces)]
    return jnp.concatenate(rows + [jnp.zeros((8 * z.ne - n, z.wide), F32)], axis=0)


def write_parts(z, who, ref, wide, lines):
    for p in range(z.ne):
        c = jnp.bitwise_xor(z.offset[p], who[1])
        ref[p] = jnp.concatenate([wide[c], lines[c]], axis=0).astype(BF16)


def back_one_body(z, parts, who, dy_ref, ln_ref, resid_ref, gr_ref, h1_ref, *refs):
    nt, lp, hw = z.nt, z.lp, z.hw
    dz_parts, refs = refs[:parts], refs[parts:]
    weights, p_ref, ctx_ref, refs = refs[:nt], refs[nt : 2 * nt], refs[2 * nt : 3 * nt], refs[3 * nt :]
    dresid_ref, dctx_ref, dv_ref, pays = refs[0], refs[1:][:nt], refs[1 + nt :][:nt], refs[1 + 2 * nt :][:nt]
    dyp, tail, buf, lines = refs[1 + 3 * nt :]
    dyp[...] = jnp.zeros(dyp.shape, F32)
    for i in range(z.images):
        dyp[i * lp : i * lp + IMAGE_TOKENS, :] = dy_ref[
            i * IMAGE_TOKENS : (i + 1) * IMAGE_TOKENS, :
        ]
    dz = dz_parts[0][...].astype(F32)
    for p in dz_parts[1:]:
        dz = dz + p[...].astype(F32)
    unit, rstd = normalize(resid_ref[...])
    dresid = norm_back(dz * ln_ref[2:3, :], unit, rstd) + dyp[...]
    dresid_ref[...] = dresid
    tail[...] = jnp.zeros(tail.shape, F32)
    tail[0:1, :] = jnp.sum(dz * unit, axis=0, keepdims=True)
    tail[1:2, :] = jnp.sum(dz, axis=0, keepdims=True)
    for e in range(z.ne):
        tail[pl.ds(8 + jnp.bitwise_xor(e, who[1]), 1), :] = gr_ref[e : e + 1, :]
    rows = spread_rows(z, tail[...])
    for p in range(z.ne):
        lines[p] = rows[8 * p : 8 * p + 8]
    da = dresid.astype(BF16)
    h1_t = h1_ref[...].T
    da_t = da.T
    head_of = iota((lp, hw), 1) // HEAD_DIM
    for r in range(nt):
        dctx = dot_nn(da, weights[r][:, 3 * hw : 4 * hw]).astype(BF16)
        dctx_ref[r][...] = dctx
        pieces = []
        for i in range(z.images):
            dc = dctx[i * lp : (i + 1) * lp]
            dv = jnp.zeros((lp, hw), F32)
            for j in range(z.hpb):
                p = p_ref[r][i * z.hpb + j]
                dv = jnp.where(head_of == j, dot_tn(p, dc), dv)
            pieces.append(dv.astype(BF16))
        dv = jnp.concatenate(pieces, axis=0)
        dv_ref[r][...] = dv
        dw = jnp.concatenate([dot_nn(h1_t, dv), dot_nn(da_t, ctx_ref[r][...])], axis=1)
        for p in range(z.ne):
            buf[p] = dw[p * z.crow : (p + 1) * z.crow]
        write_parts(z, who, pays[r], buf, lines)


def back_two_body(z, who, x_ref, ln_ref, h1_ref, *refs):
    nt, lp, hw = z.nt, z.lp, z.hw
    qkv_ref, dctx_ref, p_ref, dv_ref, refs = (*(refs[k * nt : (k + 1) * nt] for k in range(4)), refs[4 * nt :])
    dresid_ref, refs = refs[0], refs[1:]
    weights, in_ref, pays, xp, tail, buf, lines = (
        refs[:nt],
        refs[nt],
        refs[nt + 1 : 2 * nt + 1],
        *refs[2 * nt + 1 :],
    )
    xp[...] = jnp.zeros(xp.shape, F32)
    for i in range(z.images):
        xp[i * lp : i * lp + IMAGE_TOKENS, :] = x_ref[
            i * IMAGE_TOKENS : (i + 1) * IMAGE_TOKENS, :
        ]
    unit, rstd = normalize(xp[...])
    h1_t = h1_ref[...].T
    head_of = iota((lp, hw), 1) // HEAD_DIM
    dh = jnp.zeros((z.rows, z.width), F32)
    scale = HEAD_DIM**-0.5
    grads = []
    for r in range(nt):
        pieces = []
        for i in range(z.images):
            at = slice(i * lp, (i + 1) * lp)
            q, k, v = (qkv_ref[r][at, n * hw : (n + 1) * hw] for n in range(3))
            dc = dctx_ref[r][at, :]
            dq = jnp.zeros((lp, hw), F32)
            dk = jnp.zeros((lp, hw), F32)
            for j in range(z.hpb):
                mine = head_of == j
                pf = p_ref[r][i * z.hpb + j].astype(F32)
                dp = dot_nt(jnp.where(mine, dc, jnp.zeros_like(dc)), v)
                w = pf * dp
                ds = (w - pf * jnp.sum(w, axis=1, keepdims=True)).astype(BF16)
                dq = jnp.where(mine, dot_nn(ds, k) * scale, dq)
                dk = jnp.where(mine, dot_tn(ds, q) * scale, dk)
            pieces.append(jnp.concatenate([dq, dk], axis=1).astype(BF16))
        dqk = jnp.concatenate(pieces, axis=0)
        grads.append(dot_nn(h1_t, dqk))
        all_three = jnp.concatenate([dqk, dv_ref[r][...]], axis=1)
        dh = dh + dot_nt(all_three, weights[r][:, 0 : 3 * hw])
    tail[...] = jnp.zeros(tail.shape, F32)
    tail[0:1, :] = jnp.sum(dh * unit, axis=0, keepdims=True)
    tail[1:2, :] = jnp.sum(dh, axis=0, keepdims=True)
    rows = spread_rows(z, tail[...])
    for p in range(z.ne):
        lines[p] = rows[8 * p : 8 * p + 8]
    for r in range(nt):
        for p in range(z.ne):
            buf[p] = grads[r][p * z.crow : (p + 1) * z.crow]
        write_parts(z, who, pays[r], buf, lines)
    xp[...] = dresid_ref[...] + norm_back(dh * ln_ref[0:1, :], unit, rstd)
    for i in range(z.images):
        in_ref[i * IMAGE_TOKENS : (i + 1) * IMAGE_TOKENS, :] = xp[
            i * lp : i * lp + IMAGE_TOKENS, :
        ]


def last_body(z, who, low, high, q_ref, k_ref, v_ref, o_ref, n1, n2, n3, n4, router_ref, wide, lines):
    hw, half = z.hw, z.ne // 2
    for p in range(z.ne):
        c = jnp.bitwise_xor(z.offset[p], who[1])
        both = (low, high)[p // half][p % half].astype(F32)
        wide[c] = both[0 : z.crow]
        lines[c] = both[z.crow : z.prow]
    both = jnp.concatenate([wide[p] for p in range(z.ne)], axis=0)
    v_ref[...] = both[:, 0:hw]
    o_ref[...] = both[:, hw : 2 * hw].T
    q_ref[...] = both[:, 2 * hw : 3 * hw]
    k_ref[...] = both[:, 3 * hw : 4 * hw]
    both = jnp.concatenate([lines[p] for p in range(z.ne)], axis=0)
    one, two = both[:, 0 : z.wide], both[:, z.wide : 2 * z.wide]
    n = 8 + z.ne
    one = jnp.concatenate([one[s * n : (s + 1) * n] for s in range(z.pieces)], axis=1)
    two = jnp.concatenate([two[s * 8 : (s + 1) * 8] for s in range(z.pieces)], axis=1)
    n1[...], n2[...], n3[...], n4[...] = two[0:1], two[1:2], one[0:1], one[1:2]
    router_ref[...] = one[8:n]


def expert_grads_body(z, parts, who, *refs):
    one, two, (first_ref, second_ref) = refs[:parts], refs[parts : 2 * parts], refs[2 * parts :]
    first_ref[...] = sum(p[...].astype(F32) for p in one)
    second_ref[...] = sum(p[...].astype(F32) for p in two).T


def finish_body(z, parts, who, resid_ref, *refs):
    out_ref, xp = refs[parts], refs[parts + 1]
    total = refs[0][...].astype(F32)
    for p in refs[1:parts]:
        total = total + p[...].astype(F32)
    xp[...] = resid_ref[...] + total
    for i in range(z.images):
        out_ref[i * IMAGE_TOKENS : (i + 1) * IMAGE_TOKENS, :] = xp[
            i * z.lp : i * z.lp + IMAGE_TOKENS, :
        ]


def swap(value, axis, bit):
    n = lax.axis_size(axis)
    return lax.ppermute(value, axis, [(k, k ^ bit) for k in range(n)])


def gather_far(own, axis):
    blocks = [own]
    for bit in halving_bits(lax.axis_size(axis))[1:]:
        blocks += [swap(v, axis, bit) for v in blocks]
    return blocks


def gather_near(blocks, axis):
    return [v for b in blocks for v in (b, swap(b, axis, 1))]


def gather_blocks(own, axis, late=None):
    blocks = gather_far(own, axis)
    if late is not None:
        blocks = blocks[:1] + hold(blocks[1:], late)
    return gather_near(blocks, axis)


def scatter_step(left, axis, bit):
    left = {r: list(parts) for r, parts in left.items()}
    for r in sorted(left, reverse=True):
        if r & bit:
            left[r ^ bit].append(swap(total_low(left.pop(r)), axis, bit))
    return left


def scatter_near(blocks, axis):
    left = {r: [b] for r, b in enumerate(blocks)}
    left = scatter_step(left, axis, 1)
    far = {r: [total_low(parts)] for r, parts in left.items() if r}
    return {**left, **far}


def hold_far(left, after):
    far = [r for r in left if r]
    held = hold([left[r][0] for r in far], after)
    return {0: left[0], **{r: [v] for r, v in zip(far, held)}}


def scatter_far(left, axis):
    for bit in halving_bits(lax.axis_size(axis))[1:]:
        left = scatter_step(left, axis, bit)
    return left[0]


def scatter_sum(blocks, axis):
    return scatter_far(scatter_near(blocks, axis), axis)


def total_low(parts):
    if len(parts) == 1:
        return parts[0]
    return total(parts).astype(BF16)


def total(parts):
    out = parts[0].astype(F32)
    for p in parts[1:]:
        out = out + p.astype(F32)
    return out


def split_last(values):
    return values[:-1], values[-1]


def send_pairs(pairs, first, axis):
    return [v if first + k == 0 else swap(v, axis, 2 * (first + k)) for k, v in enumerate(pairs)]


def pass_on(direct, axis):
    blk = direct[0].shape[0] // 2
    return swap(jnp.concatenate([v[blk:] for v in direct], axis=0), axis, 1)


def scatter_xy(left):
    bits = halving_bits(lax.axis_size("tensor"))
    for bit in bits[2:]:
        left = scatter_step(left, "tensor", bit)
    own, other = total_low(left[0]), total_low(left[2])
    half = own.shape[0] // 2
    nt, ne = lax.axis_size("tensor"), lax.axis_size("expert")
    both = [(e * nt + t, (e ^ 1) * nt + (t ^ 2)) for e in range(ne) for t in range(nt)]
    return [
        own[:half],
        lax.ppermute(other[half:], ("expert", "tensor"), both),
        swap(own[half:], "expert", 1),
        swap(other[:half], "tensor", 2),
    ]


def places(bits):
    n = 1 << len(bits)
    return [sum(b for k, b in enumerate(bits) if p & (n >> (k + 1))) for p in range(n)]


def exchange_sum(value, axis, bits):
    offsets = places(bits)
    step = value.shape[0] // len(offsets)
    parts = [value[p * step : (p + 1) * step] for p in range(len(offsets))]
    return total_low([parts[0]] + [swap(v, axis, o) for v, o in zip(parts[1:], offsets[1:])])


def exchange_all(value, axis, bits):
    return jnp.concatenate([value] + [swap(value, axis, o) for o in places(bits)[1:]], 0)


def sum_rest(value, axis):
    for group in groups_of(axis):
        value = exchange_sum(value, axis, group)
    return value


def groups_of(axis):
    bits = halving_bits(lax.axis_size(axis))
    return [bits[k : k + 2] for k in range(1, len(bits), 2)]


def share_rest(value, axis):
    for group in groups_of(axis)[::-1]:
        value = exchange_all(value, axis, group)
    return value


def shards(
    block_in,
    out_grad,
    routes,
    kept_pairs,
    ln1_gain,
    ln1_bias,
    w_query,
    w_key,
    w_value,
    w_attn_out,
    ln2_gain,
    ln2_bias,
    w_router,
    w_expert_in,
    w_expert_out,
):
    nt, ne = lax.axis_size("tensor"), lax.axis_size("expert")
    width = block_in.shape[1]
    z = Sizes(
        nt, ne, width, block_in.shape[0], routes.shape[0], w_query.shape[1], w_expert_in.shape[2]
    )
    lp, hw, hid, blk = z.lp, z.hw, z.hid, z.blk
    me_t, me_e = lax.axis_index("tensor"), lax.axis_index("expert")
    who = jnp.stack([me_t, me_e]).astype(I32)
    body = functools.partial

    rows_low = shape((z.rows, width), BF16)
    pair = shape((2 * blk, width), BF16)
    quarter, half = ne // 4, ne // 2

    dy_low, attn_own = call(
        body(first_body, z),
        [rows_low, shape((width, 4 * hw), BF16)],
        [who, *map(Far, (out_grad, w_query, w_key, w_value, w_attn_out))],
        [pltpu.VMEM((z.rows, width), F32)],
    )
    dy_part = gather_far(dy_low, "tensor")
    lines = jnp.pad(
        jnp.stack([routes.T, kept_pairs.T]).reshape(2, 2, z.chunks, IMAGE_TOKENS),
        ((0, 0), (0, 0), (0, 0), (0, lp - IMAGE_TOKENS)),
        constant_values=-1,
    )
    expert_own, pos, keep, post = call(
        body(early_body, z),
        [
            shape((2 * width, hid), BF16),
            shape((z.chunks, ne, lp), I32),
            shape((z.chunks, ne, lp), F32),
            shape((z.chunks, lp, ne), I32),
        ],
        [who, Far(w_expert_in[0]), Far(w_expert_out[0]), lines[0], lines[1].astype(F32)],
        after=[dy_low],
    )
    dy_far = hold(dy_part[1:], [pos])
    dy_rows = gather_near([dy_part[0], *dy_far], "tensor")
    attn_part = gather_far(hold([attn_own], dy_far)[0], "tensor")
    dy_sent = call(
        body(dispatch_dy_body, z),
        [pair] * quarter,
        [who, pos, *dy_rows],
        [pltpu.VMEM((half * blk, width), F32)],
    )
    dy_in = send_pairs(dy_sent, quarter, "expert")
    attn_w = gather_near(attn_part[:1] + hold(attn_part[1:], dy_sent[:1]), "tensor")

    norms = jnp.stack([ln1_gain, ln1_bias, ln2_gain, ln2_bias])
    wr = w_router.T
    second, (resid, h1, *rest) = split_at(z.images, call(
        body(attend_body, z),
        [
            *[shape((lp, width), BF16)] * z.images,
            shape((z.rows, width), F32),
            rows_low,
            *[shape((z.rows, 3 * hw), BF16)] * nt,
            *[shape((z.rows, hw), BF16)] * nt,
            *[shape((z.images * z.hpb, lp, lp), BF16)] * nt,
        ],
        [who, Far(block_in), norms, Far(wr), *attn_w],
        [
            pltpu.VMEM((z.rows, width), F32),
            pltpu.VMEM((lp, width), F32),
            pltpu.VMEM((ne, width), F32),
        ],
    ))
    qkv, ctx, probs = rest[:nt], rest[nt : 2 * nt], rest[2 * nt :]
    rows_part = [gather_far(v, "tensor") for v in second]
    far = nt // 2 - 1
    rest = hold([w for v in rows_part for w in v[1:]] + dy_in, [])
    rows = [
        gather_near([v[0], *rest[i * far : (i + 1) * far]], "tensor")
        for i, v in enumerate(rows_part)
    ]
    rows = [v[r] for r in range(nt) for v in rows]
    dy_in = rest[z.images * far :]
    dy_passed = pass_on(dy_in, "expert")
    sent = call(
        body(dispatch_body, z),
        [pair] * half + [shape((blk, width), BF16)] * half,
        [who, pos, keep, *rows, *dy_rows],
        [
            pltpu.VMEM((z.slots, width), F32),
            pltpu.VMEM((half * blk, width), F32),
            pltpu.VMEM((2 * ne, z.slots), F32),
        ],
    )
    expert_own = hold([expert_own], rest[:1])[0]
    *sent, dy_passed, own_core = hold([*sent, dy_passed, swap(expert_own, "tensor", 1)], [])
    far_in = [swap(v, "expert", half + k) for k, v in enumerate(sent[half:])]
    near_in = hold(sent[1:half], far_in)
    near_in = [sent[0]] + [swap(v, "expert", 1 + k) for k, v in enumerate(near_in)]
    w_part = gather_far(expert_own, "tensor")
    rest = hold(w_part[1:], far_in)
    expert_w = [w_part[0], own_core, *gather_near(rest, "tensor")]

    size = half * blk
    passed = [
        *[shape((size, hid), BF16)] * (2 * nt),
        shape((size, width), BF16),
        shape((1, 128), F32),
    ]
    held = [
        pltpu.VMEM((size, width), BF16),
        pltpu.VMEM((size, 128), F32),
        pltpu.VMEM((size, width), F32),
        pltpu.VMEM((size, width), F32),
    ]
    far = call(
        body(expert_body, z, False, half),
        [pair] * half + passed,
        [who, *far_in, *dy_in, dy_passed, *expert_w],
        held,
    )
    far_out, far_mixed, (*far_hidden, far_g, far_top) = far[:quarter], far[quarter:half], far[half:]
    near = call(
        body(expert_body, z, True, half),
        [pair] * half + passed,
        [who, *near_in, *expert_w, far_top],
        held,
    )
    near_out, (*near_hidden, near_g, tops) = near[:half], near[half:]
    far_out = send_pairs(far_out, quarter, "expert")
    near_out = [v if k == 0 else swap(v, "expert", k) for k, v in enumerate(near_out)]
    expert_grads = call(
        body(expert_weights_body, z),
        [shape((width, hid), BF16)] * (2 * nt),
        [who, *near_in, *far_in, near_g, far_g, *near_hidden, *far_hidden],
        [pltpu.VMEM((2, width, size), BF16), pltpu.VMEM((2, width, size), BF16)],
    )
    far_out = hold(far_out, expert_grads[:1])
    far_out.append(pass_on(far_out, "expert"))
    first_near = scatter_near(expert_grads[:nt], "tensor")
    second_near = scatter_near(expert_grads[nt:], "tensor")

    def combine(which, more):
        return call(
            body(combine_body, z, True, which),
            [rows_low] * len(which) + [shape((ne, width), F32)],
            [
                who,
                post,
                keep,
                Far(wr),
                *[rows[r * z.images + i] for r in which for i in range(z.images)],
                *more,
                *near_out,
                *far_out,
            ],
            [pltpu.VMEM((z.slots, width), BF16)],
        )

    *partial, router_part = combine(range(2, nt), [])
    dz_near = scatter_step({r + 2: [b] for r, b in enumerate(partial)}, "tensor", 1)
    dz_near = {r: [total_low(parts)] for r, parts in dz_near.items()}
    router_part = hold([router_part], dz_near[2])[0]
    own, other, router_part = combine(range(2), [router_part])
    other = [swap(other[i * lp : (i + 1) * lp], "tensor", 1) for i in range(z.images)]
    dz_near[0] = [own, jnp.concatenate(other, axis=0)]
    dz_parts = scatter_far(dz_near, "tensor")
    mixed = send_pairs(far_mixed, quarter, "expert")
    second_parts = scatter_far(hold_far(second_near, dz_parts[-1:]), "tensor")

    pay = shape((ne, z.prow, z.wide), BF16)
    buffers = [pltpu.VMEM((ne, z.crow, z.wide), F32), pltpu.VMEM((ne, 8, z.wide), F32)]
    per_head = shape((z.rows, hw), BF16)
    outs = call(
        body(back_one_body, z, len(dz_parts)),
        [shape((z.rows, width), F32)] + [per_head] * (2 * nt) + [pay] * nt,
        [who, Far(out_grad), norms, resid, router_part, h1, *dz_parts, *attn_w, *probs, *ctx],
        [pltpu.VMEM((z.rows, width), F32), pltpu.VMEM((8 + ne, width), F32), *buffers],
    )
    dresid, dctx, dv = outs[0], outs[1:][:nt], outs[1 + nt :][:nt]
    one_near = scatter_near(outs[1 + 2 * nt :], "tensor")
    outs = call(
        body(back_two_body, z),
        [Far(shape((z.tok_dev, width), F32))] + [pay] * nt,
        [who, Far(block_in), norms, h1, *qkv, *dctx, *probs, *dv, dresid, *attn_w],
        [pltpu.VMEM((z.rows, width), F32), pltpu.VMEM((8, width), F32), *buffers],
        after=[one_near[nt // 2][0]],
    )
    input_grad = outs[0]
    one_parts = scatter_far(one_near, "tensor")
    far = [r for r in first_near if r]
    two = hold(
        [
            *outs[1:],
            one_parts[-1],
            second_parts[1],
            first_near[0][1],
            *[first_near[r][0] for r in far],
        ],
        [],
    )
    two, (one_parts[-1], second_parts[1], first_near[0][1], *rest) = split_at(nt, two)
    first_near.update((r, [v]) for r, v in zip(far, rest))
    one = total_low(one_parts)
    one = total_low([one[:half], swap(one[half:], "expert", 1)])
    two_near = scatter_near(two, "tensor")
    two_parts = scatter_xy(two_near)

    merged = jnp.concatenate([one, total_low(two_parts)], axis=2)
    merged, second_parts[-1], *mixed = hold([merged, second_parts[-1], *mixed], [])
    passed = pass_on(mixed, "expert")
    mixed_part = call(
        body(combine_body, z, False, range(nt)),
        [rows_low] * nt,
        [who, post, *near_out, *mixed, passed],
        [pltpu.VMEM((z.slots, width), BF16)],
    )
    value = sum_rest(merged, "expert")
    first_parts = scatter_far(hold_far(first_near, two_parts[-1:]), "tensor")
    value, first_parts[-1] = hold([value, first_parts[-1]], [])
    value = share_rest(value, "expert")
    mixed_near = scatter_near(mixed_part, "tensor")
    far = [r for r in mixed_near if r]
    value, *rest = hold([value, *[mixed_near[r][0] for r in far]], [])
    mixed_near.update((r, [v]) for r, v in zip(far, rest))
    mixed_parts = scatter_far(mixed_near, "tensor")
    sums = [value, swap(value, "expert", 1)]
    grad_first, grad_second = call(
        body(expert_grads_body, z, len(first_parts)),
        [Far(shape((width, hid), F32)), Far(shape((hid, width), F32))],
        [who, *first_parts, *second_parts],
    )
    block_out = call(
        body(finish_body, z, len(mixed_parts)),
        Far(shape((z.tok_dev, width), F32)),
        [who, resid, *mixed_parts],
        [pltpu.VMEM((z.rows, width), F32)],
    )

    head = Far(shape((width, hw), F32))
    grad_q, grad_k, grad_v, grad_o, n1, n2, n3, n4, router_grad = call(
        body(last_body, z),
        [head] * 3
        + [Far(shape(v, F32)) for v in ((hw, width), *[(1, width)] * 4, (ne, width))],
        [who, *sums],
        [pltpu.VMEM((ne, z.crow, 2 * z.wide), F32), pltpu.VMEM((ne, 8, 2 * z.wide), F32)],
        after=[place(v, pltpu.HBM) for v in (grad_first,)],
    )
    head_maxima = lax.dynamic_slice_in_dim(tops[0], me_t * z.hpb, z.hpb, 0)
    factor = jnp.repeat(jnp.sqrt(jnp.minimum(1.0, clip_limit / head_maxima)), HEAD_DIM)
    return (
        block_out,
        input_grad,
        n1[0],
        n2[0],
        grad_q,
        grad_k,
        grad_v,
        grad_o,
        n3[0],
        n4[0],
        router_grad.T,
        grad_first[None],
        grad_second[None],
        head_maxima,
        w_query * factor[None, :],
        w_key * factor[None, :],
    )


def solution(mesh):
    placed = (
        P(("expert", "tensor"), None),
        P(("expert", "tensor"), None),
        P("expert", None),
        P("expert", None),
        P(),
        P(),
        P(None, "tensor"),
        P(None, "tensor"),
        P(None, "tensor"),
        P("tensor", None),
        P(),
        P(),
        P(),
        P("expert", None, "tensor"),
        P("expert", "tensor", None),
    )
    return jax.shard_map(
        shards,
        mesh=mesh,
        in_specs=placed,
        out_specs=(
            P(("expert", "tensor"), None),
            P(("expert", "tensor"), None),
            P(),
            P(),
            P(None, "tensor"),
            P(None, "tensor"),
            P(None, "tensor"),
            P("tensor", None),
            P(),
            P(),
            P(),
            P("expert", None, "tensor"),
            P("expert", "tensor", None),
            P("tensor"),
            P(None, "tensor"),
            P(None, "tensor"),
        ),
        check_vma=False,
    )
```
